128 devices in a mesh: samp: 8 (over x_hi, z), cent: 16 (over x_lo, y, core).
Axes of the slice: x: 4 (x_hi: 2, x_lo: 2; x = x_hi * 2 + x_lo), y: 4, z: 4, core: 2. Of those that a mesh axis runs over, the one named last changes fastest.
Arguments:
- embeddings: bfloat16 [8192, 1024], P(('samp', 'cent'))
- destination: int32 [8192], P(('samp', 'cent')), may hold values from 0 to 8191, as said below
- centroids: bfloat16 [65536, 1024], P('cent')
Outputs:
- new_centroids: float32 [65536, 1024], P(('cent', 'samp'))
- row_lse: float32 [8192], P(('samp', 'cent'))
The draws below stay inside these ranges and needn't reach their ends.
Inputs may be any that keep to these rules, and one draw needn't show every extreme that they name: destination is a permutation of the 8192 rows; of the 64 rows that each device holds in file order, exactly 8 fall in each aligned block of 1024 logical rows.
All inputs are finite; a program needn't handle non-finite values.
Results may differ from the reference program's by a relative error of at most 0.00125.
Values may be sent and summed in bfloat16 or wider, within the bound.
No kernel may reach another device: no remote copies, remote signals or barrier semaphores. Data moves between devices by JAX's collectives and lax.ppermute only.
A program may use at most 128 MiB of HBM per device.

```python
import math
import jax
import jax.numpy as jnp
from jax import lax

D = 1024
CENT_DEV = 4096
ROWS_DEV = 64
K = 65536
SEND = 8
ROWS_SAMP = 1024
NROWS = 8192
N_SAMP = 8
N_CENT = 16


def centroid_base(key):
    key_vals, key_scale = jax.random.split(jax.random.fold_in(key, 11), 2)
    values = jnp.clip(jax.random.normal(key_vals, (K, D), jnp.float32), -6.0, 6.0)
    spread = jnp.exp(jax.random.uniform(key_scale, (K, 1), jnp.float32, math.log(0.5), math.log(2.0)))
    return values * spread


def draw_centroids(key, part):
    base = centroid_base(key)
    return base.astype(jnp.bfloat16)


def draw_embeddings(key, part):
    key = jax.random.fold_in(key, 5)
    key_rows, key_scale = jax.random.split(key, 2)
    row_scale = jnp.exp(jax.random.uniform(key_scale, (NROWS, 1), jnp.float32, math.log(0.3), math.log(3.0)))
    values = jnp.clip(jax.random.normal(key_rows, (NROWS, D), jnp.float32), -6.0, 6.0) * row_scale
    return values.astype(jnp.bfloat16)


def draw_destination(key, part):
    key = jax.random.fold_in(key, 7)
    key_group, key_shuffle = jax.random.split(key, 2)
    device_count = N_SAMP * N_CENT
    group_keys = jax.random.split(key_group, N_SAMP)
    perms = jax.vmap(lambda one: jax.random.permutation(one, ROWS_SAMP))(group_keys)
    perms = perms + (jnp.arange(N_SAMP, dtype=jnp.int32) * ROWS_SAMP)[:, None]
    spread_out = perms.reshape(N_SAMP, device_count, SEND).transpose(1, 0, 2).reshape(device_count, ROWS_DEV)
    shuffle_keys = jax.random.split(key_shuffle, device_count)
    shuffled = jax.vmap(lambda one, line: jax.random.permutation(one, line))(shuffle_keys, spread_out)
    return shuffled.reshape(NROWS).astype(jnp.int32)


def setup_inputs(seed: int = 0) -> dict:
    splits = jax.random.split(jax.random.key(seed), 4)
    embeddings = draw_embeddings(jax.random.fold_in(splits[3], 71), 0)
    destination = draw_destination(jax.random.fold_in(splits[3], 71), 0)
    centroids = draw_centroids(jax.random.fold_in(splits[3], 71), 0)
    return {"embeddings": embeddings, "destination": destination, "centroids": centroids}


inv_temp = 2.5
prior_mass = 0.25

def reference(embeddings, destination, centroids):
    placed = jnp.zeros_like(embeddings).at[destination].set(embeddings)
    scale = inv_temp / math.sqrt(D)
    blocks = centroids.reshape(K // CENT_DEV, CENT_DEV, D)

    def block_scores(block):
        return lax.dot_general(placed, block, (((1,), (1,)), ((), ())), preferred_element_type=jnp.float32) * scale

    def merge_step(running, block):
        run_max, run_total = running
        scores = block_scores(block)
        new_max = jnp.maximum(run_max, lax.optimization_barrier(jnp.max(scores, axis=1)))
        run_total = run_total * jnp.exp(run_max - new_max) + lax.optimization_barrier(jnp.sum(jnp.exp(scores - new_max[:, None]), axis=1))
        return ((new_max, run_total), None)
    start = (jnp.full((NROWS,), -1e+30, jnp.float32), jnp.zeros((NROWS,), jnp.float32))
    (row_max, row_total), _ = lax.scan(merge_step, start, blocks)
    row_lse = row_max + jnp.log(row_total)

    def refresh(block):
        weights = jnp.exp(block_scores(block) - row_lse[:, None]).astype(jnp.bfloat16)
        center_sums = lax.dot_general(weights, placed, (((0,), (0,)), ((), ())), preferred_element_type=jnp.float32)
        soft_mass = lax.optimization_barrier(jnp.sum(weights.astype(jnp.float32), axis=0))
        return (center_sums + prior_mass * block.astype(jnp.float32)) / (soft_mass + prior_mass)[:, None]
    new_centroids = lax.map(refresh, blocks).reshape(K, D)
    return (new_centroids, row_lse)
```

```python
import functools
import math

import jax
import jax.numpy as jnp
from jax import lax
from jax.experimental import pallas as pl
from jax.experimental.pallas import tpu as pltpu
from jax.sharding import PartitionSpec as P

inv_temp = 2.5
prior_mass = 0.25
BOTH = ("samp", "cent")
BIG, SMALL = 40, 24
TILE = 256
X, Y, Z = 0, 1, 2
ORDER_0 = (X, Y, Z)
ORDER_1 = (Z, X, Y)
ORDER_S = (Y, Z, X)


def place(x, y, z, core):
    return ((x // 2) * 4 + z) * 16 + (x % 2) * 8 + y * 2 + core


def fetch(value, axes, offset):
    pairs = []
    for x in range(4):
        for y in range(4):
            for z in range(4):
                for core in range(2):
                    at = [x, y, z]
                    at[axes[core]] = (at[axes[core]] + offset) % 4
                    pairs.append((place(*at, core), place(x, y, z, core)))
    return lax.ppermute(value, BOTH, pairs)


def swap_cores(value):
    pairs = [(i, i ^ 1) for i in range(128)]
    return lax.ppermute(value, BOTH, pairs)


def scores_kernel(factor, mine_ref, other_ref, rows_ref, p_ref, stat_ref):
    rows = rows_ref[...]
    tops, sums = [], []
    for half, cents in enumerate((mine_ref, other_ref)):
        for part in range(512 // TILE):
            s = lax.dot_general(
                cents[part * TILE : (part + 1) * TILE, :],
                rows,
                (((1,), (1,)), ((), ())),
                preferred_element_type=jnp.float32,
            )
            s = s * factor
            top = jnp.max(s, axis=0, keepdims=True)
            e = jnp.exp2(s - top)
            first = half * 512 + part * TILE
            p_ref[first : first + TILE, :] = e
            tops.append(top)
            sums.append(jnp.sum(e, axis=0, keepdims=True))
    stat_ref[...] = jnp.concatenate(tops + sums, axis=0)


def scores_call(mine, other, rows):
    n, width = rows.shape
    factor = inv_temp / math.sqrt(width) * math.log2(math.e)
    return pl.pallas_call(
        functools.partial(scores_kernel, factor),
        out_shape=(
            jax.ShapeDtypeStruct((1024, n), jnp.float32),
            jax.ShapeDtypeStruct((8, n), jnp.float32),
        ),
        compiler_params=pltpu.CompilerParams(vmem_limit_bytes=24 << 20),
        cost_estimate=pl.CostEstimate(
            flops=2 * 1024 * n * width, bytes_accessed=n * 6144 + (2 << 20), transcendentals=1024 * n
        ),
        name="scores",
    )(mine, other, rows)


def first_kernel(*refs):
    out_ref = refs[-1]
    at = 0
    for ref in refs[:-1]:
        n = ref.shape[1]
        top = jnp.max(ref[0:4, :], axis=0, keepdims=True)
        total = jnp.sum(ref[4:8, :] * jnp.exp2(ref[0:4, :] - top), axis=0, keepdims=True)
        out_ref[0:1, at : at + n] = top
        out_ref[1:2, at : at + n] = total
        at += n


def roll_within(value, dim, step, unit):
    inner = unit * 4**dim
    group = inner * 4
    size = value.shape[1]
    lane = lax.broadcasted_iota(jnp.int32, value.shape, 1) % group
    ahead = pltpu.roll(value, step * inner, 1)
    back = pltpu.roll(value, size - (group - step * inner), 1)
    return jnp.where(lane >= step * inner, ahead, back)


def merge_kernel(stage, core_ref, own_ref, one_ref, two_ref, three_ref, out_ref):
    first_core = core_ref[0] == 0
    cut = 64 * BIG
    small_0 = ORDER_S.index(ORDER_0[stage])
    small_1 = ORDER_S.index(ORDER_1[stage])
    big = [(own_ref[0:1, :cut], own_ref[1:2, :cut])]
    small = [(own_ref[0:1, cut:], own_ref[1:2, cut:])]
    for step, ref in ((1, one_ref), (2, two_ref), (3, three_ref)):
        big.append(tuple(roll_within(ref[k : k + 1, :cut], stage, step, BIG) for k in range(2)))
        pair = []
        for k in range(2):
            v = ref[k : k + 1, cut:]
            pair.append(
                jnp.where(first_core, roll_within(v, small_0, step, SMALL), roll_within(v, small_1, step, SMALL))
            )
        small.append(tuple(pair))
    for group, lanes in ((big, slice(0, cut)), (small, slice(cut, 4096))):
        top = functools.reduce(jnp.maximum, [t for t, _ in group])
        total = sum(l * jnp.exp2(t - top) for t, l in group)
        out_ref[0:1, lanes] = top
        out_ref[1:2, lanes] = total


def merge(stage, core, own):
    axes = (ORDER_0[stage], ORDER_1[stage])
    others = [fetch(own, axes, step) for step in (1, 2, 3)]
    vmem = pl.BlockSpec(memory_space=pltpu.VMEM)
    return pl.pallas_call(
        functools.partial(merge_kernel, stage),
        out_shape=jax.ShapeDtypeStruct(own.shape, own.dtype),
        in_specs=[pl.BlockSpec(memory_space=pltpu.SMEM), vmem, vmem, vmem, vmem],
        name="merge",
    )(core, own, *others)


def sums_kernel(half, count, pairs_ref, *refs):
    stats = refs[:count]
    ps = refs[count : 2 * count]
    rows = refs[2 * count : 3 * count]
    out_ref = refs[3 * count]
    p_bufs = refs[3 * count + 1 : 4 * count + 1]
    row_bufs = refs[4 * count + 1 : 5 * count + 1]
    sems = refs[5 * count + 1]
    copies = []
    for k in range(count):
        pair = (
            pltpu.make_async_copy(ps[k].at[pl.ds(half * 512, 512)], p_bufs[k], sems.at[0, k]),
            pltpu.make_async_copy(rows[k], row_bufs[k], sems.at[1, k]),
        )
        for copy in pair:
            copy.start()
        copies.append(pair)
    width = rows[0].shape[1]
    lse = pairs_ref[0:1, :] + jnp.log2(pairs_ref[1:2, :])
    at = 0
    for k in range(count):
        n = rows[k].shape[0]
        for copy in copies[k]:
            copy.wait()
        for part in range(512 // TILE):
            tile = half * (512 // TILE) + part
            lines = slice(part * TILE, (part + 1) * TILE)
            f = jnp.exp2(stats[k][tile : tile + 1, :] - lse[:, at : at + n])
            w = (p_bufs[k][lines, :] * f).astype(jnp.bfloat16)
            add = jnp.dot(w, row_bufs[k][...], preferred_element_type=jnp.float32)
            wide = w.astype(jnp.float32)
            mass = sum(wide[:, c : c + 128] for c in range(0, n, 128))
            if k == 0:
                out_ref[lines, :width] = add
                out_ref[lines, width:] = mass
            else:
                out_ref[lines, :width] += add
                out_ref[lines, width:] += mass
        at += n


def sums_call(half, pairs, stats, ps, rows):
    count = len(rows)
    width = rows[0].shape[1]
    vmem = pl.BlockSpec(memory_space=pltpu.VMEM)
    hbm = pl.BlockSpec(memory_space=pl.ANY)
    return pl.pallas_call(
        functools.partial(sums_kernel, half, count),
        out_shape=jax.ShapeDtypeStruct((512, width + 128), jnp.float32),
        in_specs=[vmem] * (1 + count) + [hbm] * (2 * count),
        scratch_shapes=[pltpu.VMEM((512, r.shape[0]), jnp.float32) for r in rows]
        + [pltpu.VMEM(r.shape, r.dtype) for r in rows]
        + [pltpu.SemaphoreType.DMA((2, count))],
        compiler_params=pltpu.CompilerParams(vmem_limit_bytes=40 << 20),
        cost_estimate=pl.CostEstimate(
            flops=2 * 512 * 4096 * width, bytes_accessed=18 << 20, transcendentals=8192
        ),
        name="sums",
    )(pairs, *stats, *ps, *rows)


def shards(embeddings, destination, centroids):
    core = lax.rem(lax.axis_index("cent"), 2)
    share = centroids.shape[0] // 8
    mine = lax.dynamic_slice_in_dim(centroids, lax.axis_index("samp") * share, share, 0)
    other = swap_cores(mine)
    big, small = embeddings[:BIG], embeddings[BIG:]
    for stage in range(3):
        big_axes = (ORDER_0[stage], ORDER_1[stage])
        small_axes = (ORDER_S[stage], ORDER_S[stage])
        bigs = [big] + [fetch(big, big_axes, step) for step in (1, 2, 3)]
        smalls = [small] + [fetch(small, small_axes, step) for step in (1, 2, 3)]
        if stage < 2:
            big, small = jnp.concatenate(bigs), jnp.concatenate(smalls)
    chunks = bigs + smalls
    ps, stats = zip(*[scores_call(mine, other, rows) for rows in chunks])
    pairs = pl.pallas_call(
        first_kernel, out_shape=jax.ShapeDtypeStruct((2, 4096), jnp.float32), name="first"
    )(*stats)
    core_word = core.astype(jnp.int32).reshape(1)
    for stage in range(3):
        pairs = merge(stage, core_word, pairs)
    theirs = sums_call(1, pairs, stats, ps, chunks)
    received = swap_cores(theirs)
    ours = sums_call(0, pairs, stats, ps, chunks)
    lse = (pairs[0] + jnp.log2(pairs[1])) * math.log(2.0)
    own = jnp.concatenate([lse[:BIG], lse[64 * BIG : 64 * BIG + SMALL]])
    spots = lax.broadcasted_iota(jnp.int32, (64, 8192), 1)
    spread = jnp.sum(jnp.where(spots == destination[:, None], own[:, None], 0.0), axis=0)
    arrived = lax.all_to_all(spread.reshape(128, 64), BOTH, split_axis=0, concat_axis=0, tiled=True)
    row_lse = jnp.sum(arrived, axis=0)
    width = embeddings.shape[1]
    both = ours + received
    mass = jnp.sum(both[:, width:], axis=1)
    new_centers = (both[:, :width] + prior_mass * mine.astype(jnp.float32)) / (mass + prior_mass)[:, None]
    return new_centers, row_lse


def solution(mesh):
    in_specs = (P(BOTH, None), P(BOTH), P("cent", None))
    out_specs = (P(("cent", "samp"), None), P(BOTH))
    return jax.shard_map(shards, mesh=mesh, in_specs=in_specs, out_specs=out_specs, check_vma=False)
```

```python
import functools
import math

import jax
import jax.numpy as jnp
from jax import lax
from jax.experimental import pallas as pl
from jax.experimental.pallas import tpu as pltpu
from jax.sharding import PartitionSpec as P

inv_temp = 2.5
prior_mass = 0.25
BOTH = ("samp", "cent")
UNIT = 64
TILE = 512
X, Y, Z = 0, 1, 2
ORDERS = ((X, Y, Z), (Z, X, Y))


def place(x, y, z, core):
    return ((x // 2) * 4 + z) * 16 + (x % 2) * 8 + y * 2 + core


def fetch(value, stage, offset):
    pairs = []
    for x in range(4):
        for y in range(4):
            for z in range(4):
                for core in range(2):
                    at = [x, y, z]
                    axis = ORDERS[core][stage]
                    at[axis] = (at[axis] + offset) % 4
                    pairs.append((place(*at, core), place(x, y, z, core)))
    return lax.ppermute(value, BOTH, pairs)


def swap_cores(value):
    pairs = [(i, i ^ 1) for i in range(128)]
    return lax.ppermute(value, BOTH, pairs)


def scores_kernel(factor, mine_ref, other_ref, rows_ref, p_ref, stat_ref, buf, sems):
    rows = rows_ref[...]
    tops, sums, copies = [], [], []
    for half, cents in enumerate((mine_ref, other_ref)):
        s = lax.dot_general(
            cents[...], rows, (((1,), (1,)), ((), ())), preferred_element_type=jnp.float32
        )
        s = s * factor
        top = jnp.max(s, axis=0, keepdims=True)
        e = jnp.exp2(s - top)
        buf[half] = e
        copy = pltpu.make_async_copy(buf.at[half], p_ref.at[half], sems.at[half])
        copy.start()
        copies.append(copy)
        tops.append(top)
        sums.append(jnp.sum(e, axis=0, keepdims=True))
    stat_ref[...] = jnp.concatenate(tops + sums, axis=0)
    for copy in copies:
        copy.wait()


def scores_call(mine, other, rows):
    n, width = rows.shape
    factor = inv_temp / math.sqrt(width) * math.log2(math.e)
    vmem = pl.BlockSpec(memory_space=pltpu.VMEM)
    return pl.pallas_call(
        functools.partial(scores_kernel, factor),
        out_shape=(
            jax.ShapeDtypeStruct((2, 512, n), jnp.float32),
            jax.ShapeDtypeStruct((4, n), jnp.float32),
        ),
        in_specs=[vmem] * 3,
        out_specs=(pl.BlockSpec(memory_space=pl.ANY), vmem),
        scratch_shapes=[pltpu.VMEM((2, 512, n), jnp.float32), pltpu.SemaphoreType.DMA((2,))],
        compiler_params=pltpu.CompilerParams(vmem_limit_bytes=32 << 20),
        cost_estimate=pl.CostEstimate(
            flops=2 * 1024 * n * width, bytes_accessed=n * 6144 + (2 << 20), transcendentals=1024 * n
        ),
        name="scores",
    )(mine, other, rows)


def roll_within(value, dim, step):
    inner = UNIT * 4**dim
    group = inner * 4
    size = value.shape[1]
    lane = lax.broadcasted_iota(jnp.int32, value.shape, 1) % group
    ahead = pltpu.roll(value, step * inner, 1)
    back = pltpu.roll(value, size - group + step * inner, 1)
    return jnp.where(lane >= step * inner, ahead, back)


def first_kernel(spot_ref, *refs):
    out_ref = refs[-1]
    parts = []
    for ref in refs[:-1]:
        top = jnp.max(ref[0:2, :], axis=0, keepdims=True)
        total = jnp.sum(ref[2:4, :] * jnp.exp2(ref[0:2, :] - top), axis=0, keepdims=True)
        parts.append(top + jnp.log2(total))
    value = jnp.concatenate(parts, axis=1)
    for dim in range(3):
        value = roll_within(value, dim, spot_ref[dim])
    for line in range(8):
        piece = value[:, line * 512 : (line + 1) * 512]
        out_ref[:, line, :] = jnp.broadcast_to(piece, (64, 512))


def merge_kernel(spot_ref, all_ref, whole_ref, own_ref):
    top = jnp.max(all_ref[...], axis=0)
    total = jnp.sum(jnp.exp2(all_ref[...] - top[None]), axis=0)
    lse = top + jnp.log2(total)
    whole_ref[...] = lse
    value = jnp.concatenate([lse[line : line + 1, :] for line in range(8)], axis=1)
    for dim in range(3):
        value = roll_within(value, dim, (4 - spot_ref[dim]) % 4)
    own_ref[...] = value


def sums_kernel(half, count, lse_ref, *refs):
    stats = refs[:count]
    ps = refs[count : 2 * count]
    rows = refs[2 * count : 3 * count]
    out_ref = refs[3 * count]
    p_bufs = refs[3 * count + 1 : 4 * count + 1]
    row_bufs = refs[4 * count + 1 : 5 * count + 1]
    sems = refs[5 * count + 1]
    copies = []
    for k in range(count):
        pair = (
            pltpu.make_async_copy(ps[k].at[half], p_bufs[k], sems.at[0, k]),
            pltpu.make_async_copy(rows[k], row_bufs[k], sems.at[1, k]),
        )
        for copy in pair:
            copy.start()
        copies.append(pair)
    width = rows[0].shape[1]
    at = 0
    for k in range(count):
        n = rows[k].shape[0]
        for copy in copies[k]:
            copy.wait()
        f = jnp.exp2(stats[k][half : half + 1, :] - lse_ref[:, at : at + n])
        w = (p_bufs[k][...] * f).astype(jnp.bfloat16)
        add = jnp.dot(w, row_bufs[k][...], preferred_element_type=jnp.float32)
        wide = w.astype(jnp.float32)
        mass = sum(wide[:, c : c + 128] for c in range(0, n, 128))
        if k == 0:
            out_ref[:, :width] = add
            out_ref[:, width:] = mass
        else:
            out_ref[:, :width] += add
            out_ref[:, width:] += mass
        at += n


def sums_call(half, lse, stats, ps, rows):
    count = len(rows)
    width = rows[0].shape[1]
    vmem = pl.BlockSpec(memory_space=pltpu.VMEM)
    hbm = pl.BlockSpec(memory_space=pl.ANY)
    return pl.pallas_call(
        functools.partial(sums_kernel, half, count),
        out_shape=jax.ShapeDtypeStruct((512, width + 128), jnp.float32),
        in_specs=[vmem] * (1 + count) + [hbm] * (2 * count),
        scratch_shapes=[pltpu.VMEM((512, r.shape[0]), jnp.float32) for r in rows]
        + [pltpu.VMEM(r.shape, r.dtype) for r in rows]
        + [pltpu.SemaphoreType.DMA((2, count))],
        compiler_params=pltpu.CompilerParams(vmem_limit_bytes=58 << 20),
        cost_estimate=pl.CostEstimate(
            flops=2 * 512 * 4096 * width, bytes_accessed=18 << 20, transcendentals=8192
        ),
        name="sums",
    )(lse, *stats, *ps, *rows)


def shards(embeddings, destination, centroids):
    samp, cent = lax.axis_index("samp"), lax.axis_index("cent")
    core = cent % 2
    x, y, z = (samp // 4) * 2 + cent // 8, (cent // 2) % 4, samp % 4
    spot = jnp.where(core == 0, jnp.stack([x, y, z]), jnp.stack([z, x, y])).astype(jnp.int32)
    share = centroids.shape[0] // 8
    width = embeddings.shape[1]
    mine = lax.dynamic_slice_in_dim(centroids, samp * share, share, 0)
    other = swap_cores(mine)
    line = jnp.concatenate([embeddings] + [fetch(embeddings, 0, step) for step in (1, 2, 3)])
    plane = jnp.concatenate([line] + [fetch(line, 1, step) for step in (1, 2, 3)])
    after, before = fetch(plane, 2, 1), fetch(plane, 2, 3)
    far = [fetch(after[:512], 2, 1), fetch(before[512:], 2, 3)]
    chunks = [plane, after] + far + [before]

    late, _ = lax.optimization_barrier((destination, plane))
    start = core * 4096 + ((spot[2] * 4 + spot[1]) * 4 + spot[0]) * UNIT
    spots = lax.broadcasted_iota(jnp.int32, (UNIT, 8192), 1)
    keys = (start + jnp.arange(UNIT, dtype=jnp.int32))[:, None]
    spread = jnp.sum(jnp.where(spots == late[:, None], keys, 0), axis=0)
    arrived = lax.all_to_all(spread.reshape(128, UNIT), BOTH, split_axis=0, concat_axis=0, tiled=True)
    keys = jnp.sum(arrived, axis=0)

    results = {k: scores_call(mine, other, chunks[k]) for k in (0, 1, 4, 2, 3)}
    ps = [results[k][0] for k in range(5)]
    stats = [results[k][1] for k in range(5)]
    smem = pl.BlockSpec(memory_space=pltpu.SMEM)
    vmem = pl.BlockSpec(memory_space=pltpu.VMEM)
    local = pl.pallas_call(
        first_kernel,
        out_shape=jax.ShapeDtypeStruct((64, 8, 512), jnp.float32),
        in_specs=[smem] + [vmem] * 5,
        name="first",
    )(spot, *stats)
    chips = [
        [place(i // 16, i // 4 % 4, i % 4, side) for i in range(64)] for side in range(2)
    ]
    shared = lax.all_to_all(local, BOTH, split_axis=0, concat_axis=0, tiled=True, axis_index_groups=chips)
    whole, lse = pl.pallas_call(
        merge_kernel,
        out_shape=(
            jax.ShapeDtypeStruct((8, 512), jnp.float32),
            jax.ShapeDtypeStruct((1, 4096), jnp.float32),
        ),
        in_specs=[smem, vmem],
        name="merge",
    )(spot, shared)
    theirs = sums_call(1, lse, stats, ps, chunks)
    received = swap_cores(theirs)
    ours = sums_call(0, lse, stats, ps, chunks)
    whole = whole.reshape(4096)
    partner = swap_cores(whole)
    every = jnp.where(core == 0, jnp.concatenate([whole, partner]), jnp.concatenate([partner, whole]))
    row_lse = jnp.sum(jnp.where(spots == keys[:, None], every[None, :], 0.0), axis=1) * math.log(2.0)
    both = ours + received
    mass = jnp.sum(both[:, width:], axis=1)
    new_centers = (both[:, :width] + prior_mass * mine.astype(jnp.float32)) / (mass + prior_mass)[:, None]
    return new_centers, row_lse


def solution(mesh):
    in_specs = (P(BOTH, None), P(BOTH), P("cent", None))
    out_specs = (P(("cent", "samp"), None), P(BOTH))
    return jax.shard_map(shards, mesh=mesh, in_specs=in_specs, out_specs=out_specs, check_vma=False)
```

```python
import functools
import math

import jax
import jax.numpy as jnp
from jax import lax
from jax.experimental import pallas as pl
from jax.experimental.pallas import tpu as pltpu
from jax.sharding import PartitionSpec as P

inv_temp = 2.5
prior_mass = 0.25
BOTH = ("samp", "cent")
UNIT = 64
X, Y, Z = 0, 1, 2
ORDERS = ((X, Y, Z), (Z, X, Y))


def place(x, y, z, core):
    return ((x // 2) * 4 + z) * 16 + (x % 2) * 8 + y * 2 + core


def fetch(value, stage, offset):
    pairs = []
    for x in range(4):
        for y in range(4):
            for z in range(4):
                for core in range(2):
                    at = [x, y, z]
                    axis = ORDERS[core][stage]
                    at[axis] = (at[axis] + offset) % 4
                    pairs.append((place(*at, core), place(x, y, z, core)))
    return lax.ppermute(value, BOTH, pairs)


def swap_cores(value):
    pairs = [(i, i ^ 1) for i in range(128)]
    return lax.ppermute(value, BOTH, pairs)


def scores_kernel(factor, count, mine_ref, other_ref, *refs):
    rows = refs[:count]
    ps = refs[count : 2 * count]
    stat_ref = refs[2 * count]
    tiles = [(k, part, half) for k in range(count) for part in range(2) for half in range(2)]

    def product(tile):
        k, part, half = tile
        return lax.dot_general(
            (mine_ref, other_ref)[half][...],
            rows[k][part * 256 : (part + 1) * 256, :],
            (((1,), (1,)), ((), ())),
            preferred_element_type=jnp.float32,
        )

    following = product(tiles[0])
    for i, (k, part, half) in enumerate(tiles):
        s = following * factor
        if i + 1 < len(tiles):
            following = product(tiles[i + 1])
        top = jnp.max(s, axis=0, keepdims=True)
        e = jnp.exp2(s - top)
        ps[k][half, :, part * 256 : (part + 1) * 256] = e
        lanes = slice(k * 512 + part * 256, k * 512 + (part + 1) * 256)
        stat_ref[half : half + 1, lanes] = top
        stat_ref[2 + half : 3 + half, lanes] = jnp.sum(e, axis=0, keepdims=True)


def scores_call(mine, other, rows):
    count = len(rows)
    n, width = rows[0].shape
    factor = inv_temp / math.sqrt(width) * math.log2(math.e)
    vmem = pl.BlockSpec(memory_space=pltpu.VMEM)
    *ps, stat = pl.pallas_call(
        functools.partial(scores_kernel, factor, count),
        out_shape=tuple([jax.ShapeDtypeStruct((2, 512, n), jnp.float32)] * count)
        + (jax.ShapeDtypeStruct((4, count * n), jnp.float32),),
        in_specs=[vmem] * (2 + count),
        out_specs=tuple([vmem] * (count + 1)),
        compiler_params=pltpu.CompilerParams(vmem_limit_bytes=16 << 20),
        cost_estimate=pl.CostEstimate(
            flops=4 * 1024 * n * width * count,
            bytes_accessed=count * n * 6144 + (2 << 20),
            transcendentals=1024 * n * count,
        ),
        name="scores",
    )(mine, other, *rows)
    return ps, stat


def roll_within(value, dim, step):
    inner = UNIT * 4**dim
    group = inner * 4
    size = value.shape[1]
    lane = lax.broadcasted_iota(jnp.int32, value.shape, 1) % group
    ahead = pltpu.roll(value, step * inner, 1)
    back = pltpu.roll(value, size - group + step * inner, 1)
    return jnp.where(lane >= step * inner, ahead, back)


def first_kernel(order, spot_ref, *refs):
    *stats, out_ref, top_ref = refs
    parts = []
    for k, (ref, piece) in enumerate(order):
        lanes = slice(piece * 512, (piece + 1) * 512)
        tops = stats[ref][0:2, lanes]
        top = jnp.max(tops, axis=0, keepdims=True)
        total = jnp.sum(stats[ref][2:4, lanes] * jnp.exp2(tops - top), axis=0, keepdims=True)
        parts.append(top + jnp.log2(total))
        top_ref[:, k * 512 : (k + 1) * 512] = tops
    value = jnp.concatenate(parts, axis=1)
    for dim in range(3):
        value = roll_within(value, dim, spot_ref[dim])
    for line in range(8):
        piece = value[:, line * 512 : (line + 1) * 512]
        out_ref[:, line, :] = jnp.broadcast_to(piece, (64, 512))


def merge_kernel(spot_ref, all_ref, whole_ref, own_ref):
    top = jnp.max(all_ref[...], axis=0)
    total = jnp.sum(jnp.exp2(all_ref[...] - top[None]), axis=0)
    lse = top + jnp.log2(total)
    whole_ref[...] = lse
    value = jnp.concatenate([lse[line : line + 1, :] for line in range(8)], axis=1)
    for dim in range(3):
        value = roll_within(value, dim, (4 - spot_ref[dim]) % 4)
    own_ref[...] = value


def sums_kernel(half, count, lse_ref, top_ref, *refs):
    ps = refs[:count]
    rows = refs[count : 2 * count]
    out_ref, row_buf, sems = refs[2 * count :]
    n, width = rows[0].shape
    loads = [pltpu.make_async_copy(rows[k], row_buf.at[k], sems.at[k]) for k in range(count)]
    for load in loads:
        load.start()

    def weights(k):
        lanes = slice(k * n, (k + 1) * n)
        f = jnp.exp2(top_ref[half : half + 1, lanes] - lse_ref[:, lanes])
        w = (ps[k][half] * f).astype(jnp.bfloat16)
        wide = w.astype(jnp.float32)
        return w, sum(wide[:, c : c + 128] for c in range(0, n, 128))

    w, mass = weights(0)
    for k in range(count):
        now = w
        if k + 1 < count:
            w, more = weights(k + 1)
            mass = mass + more
        loads[k].wait()
        add = jnp.dot(now, row_buf[k], preferred_element_type=jnp.float32)
        if k == 0:
            out_ref[:, :width] = add
        else:
            out_ref[:, :width] += add
    out_ref[:, width:] = mass


def sums_call(half, lse, tops, ps, rows):
    count = len(rows)
    n, width = rows[0].shape
    vmem = pl.BlockSpec(memory_space=pltpu.VMEM)
    hbm = pl.BlockSpec(memory_space=pltpu.HBM)
    return pl.pallas_call(
        functools.partial(sums_kernel, half, count),
        out_shape=jax.ShapeDtypeStruct((512, width + 128), jnp.float32),
        in_specs=[vmem] * (2 + count) + [hbm] * count,
        scratch_shapes=[pltpu.VMEM((count, n, width), jnp.bfloat16), pltpu.SemaphoreType.DMA((count,))],
        compiler_params=pltpu.CompilerParams(vmem_limit_bytes=20 << 20),
        cost_estimate=pl.CostEstimate(
            flops=2 * 512 * 4096 * width, bytes_accessed=18 << 20, transcendentals=8192
        ),
        name="sums",
    )(lse, tops, *ps, *rows)


def final_kernel(ours_ref, theirs_ref, mine_ref, out_ref):
    width = out_ref.shape[1]
    mass = jnp.sum(ours_ref[:, width:] + theirs_ref[:, width:], axis=1, keepdims=True) + prior_mass
    total = ours_ref[:, :width] + theirs_ref[:, :width] + prior_mass * mine_ref[...].astype(jnp.float32)
    out_ref[...] = total * (1.0 / mass)


def share_kernel(at_ref, cents_ref, out_ref, sem):
    size = out_ref.shape[0]
    first = pl.multiple_of(at_ref[0] * size, size)
    copy = pltpu.make_async_copy(cents_ref.at[pl.ds(first, size)], out_ref, sem)
    copy.start()
    copy.wait()


def shards(embeddings, destination, centroids):
    samp, cent = lax.axis_index("samp"), lax.axis_index("cent")
    core = cent % 2
    x, y, z = (samp // 4) * 2 + cent // 8, (cent // 2) % 4, samp % 4
    spot = jnp.where(core == 0, jnp.stack([x, y, z]), jnp.stack([z, x, y])).astype(jnp.int32)
    share = centroids.shape[0] // 8
    width = embeddings.shape[1]
    smem = pl.BlockSpec(memory_space=pltpu.SMEM)
    vmem = pl.BlockSpec(memory_space=pltpu.VMEM)
    mine = pl.pallas_call(
        share_kernel,
        out_shape=jax.ShapeDtypeStruct((share, width), centroids.dtype),
        in_specs=[smem, pl.BlockSpec(memory_space=pltpu.HBM)],
        out_specs=vmem,
        scratch_shapes=[pltpu.SemaphoreType.DMA(())],
        name="share",
    )(samp.astype(jnp.int32).reshape(1), centroids)
    other = swap_cores(mine)
    line = jnp.concatenate([embeddings] + [fetch(embeddings, 0, step) for step in (1, 2, 3)])
    near, across, back = [fetch(line, 1, step) for step in (1, 2, 3)]
    upper, lower = jnp.concatenate([line, near]), jnp.concatenate([across, back])
    upper, lower, other = lax.optimization_barrier((upper, lower, other))
    after_upper, before_lower = fetch(upper, 2, 1), fetch(lower, 2, 3)

    late, _, _ = lax.optimization_barrier((destination, upper, lower))
    start = core * 4096 + ((spot[2] * 4 + spot[1]) * 4 + spot[0]) * UNIT
    spots = lax.broadcasted_iota(jnp.int32, (UNIT, 8192), 1)
    keys = (start + jnp.arange(UNIT, dtype=jnp.int32))[:, None]
    spread = jnp.sum(jnp.where(spots == late[:, None], keys, 0), axis=0)
    arrived = lax.all_to_all(spread.reshape(128, UNIT), BOTH, split_axis=0, concat_axis=0, tiled=True)
    keys = jnp.sum(arrived, axis=0)

    p_upper, stat_upper = scores_call(mine, other, [upper])
    upper_again, lower_again, _ = lax.optimization_barrier((upper, lower, stat_upper))
    after_lower, before_upper = fetch(lower_again, 2, 1), fetch(upper_again, 2, 3)
    p_lower, stat_lower = scores_call(mine, other, [lower])
    passed_up, passed_down, keys, _ = lax.optimization_barrier((after_upper, before_lower, keys, stat_lower))
    far_upper, far_lower = fetch(passed_up, 2, 1), fetch(passed_down, 2, 3)
    p_first, stat_first = scores_call(mine, other, [after_upper, before_lower])
    p_second, stat_second = scores_call(mine, other, [after_lower, before_upper])
    p_far, stat_far = scores_call(mine, other, [far_upper, far_lower])
    chunks = [upper, lower, after_upper, after_lower, far_upper, far_lower, before_upper, before_lower]
    ps = p_upper + p_lower + [p_first[0], p_second[0]] + p_far + [p_second[1], p_first[1]]
    order = ((0, 0), (1, 0), (2, 0), (3, 0), (4, 0), (4, 1), (3, 1), (2, 1))

    local, tops = pl.pallas_call(
        functools.partial(first_kernel, order),
        out_shape=(
            jax.ShapeDtypeStruct((64, 8, 512), jnp.float32),
            jax.ShapeDtypeStruct((2, 4096), jnp.float32),
        ),
        in_specs=[smem] + [vmem] * 5,
        name="first",
    )(spot, stat_upper, stat_lower, stat_first, stat_second, stat_far)
    chips = [
        [place(i // 16, i // 4 % 4, i % 4, side) for i in range(64)] for side in range(2)
    ]
    shared = lax.all_to_all(local, BOTH, split_axis=0, concat_axis=0, tiled=True, axis_index_groups=chips)
    whole, lse = pl.pallas_call(
        merge_kernel,
        out_shape=(
            jax.ShapeDtypeStruct((8, 512), jnp.float32),
            jax.ShapeDtypeStruct((1, 4096), jnp.float32),
        ),
        in_specs=[smem, vmem],
        name="merge",
    )(spot, shared)
    theirs = sums_call(1, lse, tops, ps, chunks)
    received = swap_cores(theirs)
    ours = sums_call(0, lse, tops, ps, chunks)
    whole = whole.reshape(4096)
    partner = swap_cores(whole)
    every = jnp.where(core == 0, jnp.concatenate([whole, partner]), jnp.concatenate([partner, whole]))
    row_lse = jnp.sum(jnp.where(spots == keys[:, None], every[None, :], 0.0), axis=1) * math.log(2.0)
    new_centers = pl.pallas_call(
        final_kernel, out_shape=jax.ShapeDtypeStruct((share, width), jnp.float32), name="final",
        compiler_params=pltpu.CompilerParams(vmem_limit_bytes=16 << 20),
    )(ours, received, mine)
    return new_centers, row_lse


def solution(mesh):
    in_specs = (P(BOTH, None), P(BOTH), P("cent", None))
    out_specs = (P(("cent", "samp"), None), P(BOTH))
    return jax.shard_map(shards, mesh=mesh, in_specs=in_specs, out_specs=out_specs, check_vma=False)
```

```python
import functools
import math

import jax
import jax.numpy as jnp
from jax import lax
from jax.experimental import pallas as pl
from jax.experimental.pallas import tpu as pltpu
from jax.sharding import PartitionSpec as P

inv_temp = 2.5
prior_mass = 0.25
BOTH = ("samp", "cent")
UNIT = 64
X, Y, Z = 0, 1, 2
ORDERS = ((X, Y, Z), (Z, X, Y))


def place(x, y, z, core):
    return ((x // 2) * 4 + z) * 16 + (x % 2) * 8 + y * 2 + core


def fetch(value, stage, offset):
    pairs = []
    for x in range(4):
        for y in range(4):
            for z in range(4):
                for core in range(2):
                    at = [x, y, z]
                    axis = ORDERS[core][stage]
                    at[axis] = (at[axis] + offset) % 4
                    pairs.append((place(*at, core), place(x, y, z, core)))
    return lax.ppermute(value, BOTH, pairs)


def swap_cores(value):
    pairs = [(i, i ^ 1) for i in range(128)]
    return lax.ppermute(value, BOTH, pairs)


def scores_kernel(factor, count, mine_ref, other_ref, *refs):
    rows = refs[:count]
    ps = refs[count : 2 * count]
    stat_ref = refs[2 * count]
    tiles = [(k, part, half) for k in range(count) for part in range(2) for half in range(2)]

    def product(tile):
        k, part, half = tile
        return lax.dot_general(
            (mine_ref, other_ref)[half][...],
            rows[k][part * 256 : (part + 1) * 256, :],
            (((1,), (1,)), ((), ())),
            preferred_element_type=jnp.float32,
        )

    following = product(tiles[0])
    for i, (k, part, half) in enumerate(tiles):
        s = following * factor
        if i + 1 < len(tiles):
            following = product(tiles[i + 1])
        top = jnp.max(s, axis=0, keepdims=True)
        e = jnp.exp2(s - top)
        ps[k][half, :, part * 256 : (part + 1) * 256] = e
        lanes = slice(k * 512 + part * 256, k * 512 + (part + 1) * 256)
        stat_ref[half : half + 1, lanes] = top
        stat_ref[2 + half : 3 + half, lanes] = jnp.sum(e, axis=0, keepdims=True)


def scores_call(mine, other, rows):
    count = len(rows)
    n, width = rows[0].shape
    factor = inv_temp / math.sqrt(width) * math.log2(math.e)
    vmem = pl.BlockSpec(memory_space=pltpu.VMEM)
    *ps, stat = pl.pallas_call(
        functools.partial(scores_kernel, factor, count),
        out_shape=tuple([jax.ShapeDtypeStruct((2, 512, n), jnp.float32)] * count)
        + (jax.ShapeDtypeStruct((4, count * n), jnp.float32),),
        in_specs=[vmem] * (2 + count),
        out_specs=tuple([vmem] * (count + 1)),
        compiler_params=pltpu.CompilerParams(vmem_limit_bytes=12 << 20),
        cost_estimate=pl.CostEstimate(
            flops=4 * 1024 * n * width * count,
            bytes_accessed=count * n * 6144 + (2 << 20),
            transcendentals=1024 * n * count,
        ),
        name="scores",
    )(mine, other, *rows)
    return ps, stat


def roll_within(value, dim, step):
    inner = UNIT * 4**dim
    group = inner * 4
    size = value.shape[1]
    lane = lax.broadcasted_iota(jnp.int32, value.shape, 1) % group
    ahead = pltpu.roll(value, step * inner, 1)
    back = pltpu.roll(value, size - group + step * inner, 1)
    return jnp.where(lane >= step * inner, ahead, back)


def first_kernel(order, spot_ref, *refs):
    *stats, out_ref, top_ref = refs
    parts = []
    for k, (ref, piece) in enumerate(order):
        lanes = slice(piece * 512, (piece + 1) * 512)
        tops = stats[ref][0:2, lanes]
        top = jnp.max(tops, axis=0, keepdims=True)
        total = jnp.sum(stats[ref][2:4, lanes] * jnp.exp2(tops - top), axis=0, keepdims=True)
        parts.append(top + jnp.log2(total))
        top_ref[:, k * 512 : (k + 1) * 512] = tops
    value = jnp.concatenate(parts, axis=1)
    for dim in range(3):
        value = roll_within(value, dim, spot_ref[dim])
    for line in range(8):
        piece = value[:, line * 512 : (line + 1) * 512]
        out_ref[:, line, :] = jnp.broadcast_to(piece, (64, 512))


def merge_kernel(spot_ref, all_ref, whole_ref, own_ref):
    top = jnp.max(all_ref[...], axis=0)
    total = jnp.sum(jnp.exp2(all_ref[...] - top[None]), axis=0)
    lse = top + jnp.log2(total)
    whole_ref[...] = lse
    value = jnp.concatenate([lse[line : line + 1, :] for line in range(8)], axis=1)
    for dim in range(3):
        value = roll_within(value, dim, (4 - spot_ref[dim]) % 4)
    own_ref[...] = value


def sums_kernel(half, count, lse_ref, top_ref, *refs):
    ps = refs[:count]
    rows = refs[count : 2 * count]
    out_ref = refs[2 * count]
    n, width = rows[0].shape

    def weights(k):
        lanes = slice(k * n, (k + 1) * n)
        f = jnp.exp2(top_ref[half : half + 1, lanes] - lse_ref[:, lanes])
        w = (ps[k][half] * f).astype(jnp.bfloat16)
        wide = w.astype(jnp.float32)
        return w, sum(wide[:, c : c + 128] for c in range(0, n, 128))

    w, mass = weights(0)
    for k in range(count):
        now = w
        if k + 1 < count:
            w, more = weights(k + 1)
            mass = mass + more
        add = jnp.dot(now, rows[k][...], preferred_element_type=jnp.float32)
        if k == 0:
            out_ref[:, :width] = add
        else:
            out_ref[:, :width] += add
    out_ref[:, width:] = mass


def sums_call(half, lse, tops, ps, rows):
    count = len(rows)
    width = rows[0].shape[1]
    vmem = pl.BlockSpec(memory_space=pltpu.VMEM)
    return pl.pallas_call(
        functools.partial(sums_kernel, half, count),
        out_shape=jax.ShapeDtypeStruct((512, width + 128), jnp.float32),
        in_specs=[vmem] * (2 + 2 * count),
        compiler_params=pltpu.CompilerParams(vmem_limit_bytes=10 << 20),
        cost_estimate=pl.CostEstimate(
            flops=2 * 512 * 4096 * width, bytes_accessed=18 << 20, transcendentals=8192
        ),
        name="sums",
    )(lse, tops, *ps, *rows)


def final_kernel(ours_ref, theirs_ref, mine_ref, out_ref):
    width = out_ref.shape[1]
    mass = jnp.sum(ours_ref[:, width:] + theirs_ref[:, width:], axis=1, keepdims=True) + prior_mass
    total = ours_ref[:, :width] + theirs_ref[:, :width] + prior_mass * mine_ref[...].astype(jnp.float32)
    out_ref[...] = total * (1.0 / mass)


def share_kernel(at_ref, cents_ref, out_ref, sem):
    size = out_ref.shape[0]
    first = pl.multiple_of(at_ref[0] * size, size)
    copy = pltpu.make_async_copy(cents_ref.at[pl.ds(first, size)], out_ref, sem)
    copy.start()
    copy.wait()


def shards(embeddings, destination, centroids):
    samp, cent = lax.axis_index("samp"), lax.axis_index("cent")
    core = lax.bitwise_and(cent, 1)
    x = lax.shift_right_logical(samp, 2) * 2 + lax.shift_right_logical(cent, 3)
    y, z = lax.bitwise_and(lax.shift_right_logical(cent, 1), 3), lax.bitwise_and(samp, 3)
    spot = jnp.where(core == 0, jnp.stack([x, y, z]), jnp.stack([z, x, y])).astype(jnp.int32)
    share = centroids.shape[0] // 8
    width = embeddings.shape[1]
    smem = pl.BlockSpec(memory_space=pltpu.SMEM)
    vmem = pl.BlockSpec(memory_space=pltpu.VMEM)
    mine = pl.pallas_call(
        share_kernel,
        out_shape=jax.ShapeDtypeStruct((share, width), centroids.dtype),
        in_specs=[smem, pl.BlockSpec(memory_space=pltpu.HBM)],
        out_specs=vmem,
        scratch_shapes=[pltpu.SemaphoreType.DMA(())],
        compiler_params=pltpu.CompilerParams(vmem_limit_bytes=8 << 20),
        name="share",
    )(samp.astype(jnp.int32).reshape(1), centroids)
    other = swap_cores(mine)
    line = jnp.concatenate([embeddings] + [fetch(embeddings, 0, step) for step in (1, 2, 3)])
    late, spot, _ = lax.optimization_barrier((destination, spot, line))
    start = core * 4096 + ((spot[2] * 4 + spot[1]) * 4 + spot[0]) * UNIT
    spots = lax.broadcasted_iota(jnp.int32, (UNIT, 8192), 1)
    keys = (start + jnp.arange(UNIT, dtype=jnp.int32))[:, None]
    spread = jnp.sum(jnp.where(spots == late[:, None], keys, 0), axis=0)
    arrived = lax.all_to_all(spread.reshape(128, UNIT), BOTH, split_axis=0, concat_axis=0, tiled=True)
    keys = jnp.sum(arrived, axis=0)

    near, across, back = [fetch(line, 1, step) for step in (1, 2, 3)]
    upper, lower = jnp.concatenate([line, near]), jnp.concatenate([across, back])
    upper, lower, other, keys = lax.optimization_barrier((upper, lower, other, keys))
    after_upper, before_lower = fetch(upper, 2, 1), fetch(lower, 2, 3)

    p_upper, stat_upper = scores_call(mine, other, [upper])
    upper_again, lower_again, _ = lax.optimization_barrier((upper, lower, stat_upper))
    after_lower, before_upper = fetch(lower_again, 2, 1), fetch(upper_again, 2, 3)
    p_lower, stat_lower = scores_call(mine, other, [lower])
    passed_up, passed_down, _ = lax.optimization_barrier((after_upper, before_lower, stat_lower))
    far_upper, far_lower = fetch(passed_up, 2, 1), fetch(passed_down, 2, 3)
    p_first, stat_first = scores_call(mine, other, [after_upper, before_lower])
    p_second, stat_second = scores_call(mine, other, [after_lower, before_upper])
    p_far, stat_far = scores_call(mine, other, [far_upper, far_lower])
    chunks = [upper, lower, after_upper, after_lower, far_upper, far_lower, before_upper, before_lower]
    ps = p_upper + p_lower + [p_first[0], p_second[0]] + p_far + [p_second[1], p_first[1]]
    order = ((0, 0), (1, 0), (2, 0), (3, 0), (4, 0), (4, 1), (3, 1), (2, 1))

    local, tops = pl.pallas_call(
        functools.partial(first_kernel, order),
        out_shape=(
            jax.ShapeDtypeStruct((64, 8, 512), jnp.float32),
            jax.ShapeDtypeStruct((2, 4096), jnp.float32),
        ),
        in_specs=[smem] + [vmem] * 5,
        compiler_params=pltpu.CompilerParams(vmem_limit_bytes=8 << 20),
        name="first",
    )(spot, stat_upper, stat_lower, stat_first, stat_second, stat_far)
    chips = [
        [place(i // 16, i // 4 % 4, i % 4, side) for i in range(64)] for side in range(2)
    ]
    shared = lax.all_to_all(local, BOTH, split_axis=0, concat_axis=0, tiled=True, axis_index_groups=chips)
    whole, lse = pl.pallas_call(
        merge_kernel,
        out_shape=(
            jax.ShapeDtypeStruct((8, 512), jnp.float32),
            jax.ShapeDtypeStruct((1, 4096), jnp.float32),
        ),
        in_specs=[smem, vmem],
        compiler_params=pltpu.CompilerParams(vmem_limit_bytes=8 << 20),
        name="merge",
    )(spot, shared)
    theirs = sums_call(1, lse, tops, ps, chunks)
    received = swap_cores(theirs)
    ours = sums_call(0, lse, tops, ps, chunks)
    whole = whole.reshape(4096)
    partner = swap_cores(whole)
    every = jnp.where(core == 0, jnp.concatenate([whole, partner]), jnp.concatenate([partner, whole]))
    row_lse = jnp.sum(jnp.where(spots == keys[:, None], every[None, :], 0.0), axis=1) * math.log(2.0)
    new_centers = pl.pallas_call(
        final_kernel, out_shape=jax.ShapeDtypeStruct((share, width), jnp.float32), name="final",
        compiler_params=pltpu.CompilerParams(vmem_limit_bytes=8 << 20),
    )(ours, received, mine)
    return new_centers, row_lse


def solution(mesh):
    in_specs = (P(BOTH, None), P(BOTH), P("cent", None))
    out_specs = (P(("cent", "samp"), None), P(BOTH))
    return jax.shard_map(shards, mesh=mesh, in_specs=in_specs, out_specs=out_specs, check_vma=False)
```

```python
import functools
import math

import jax
import jax.numpy as jnp
from jax import lax
from jax.experimental import pallas as pl
from jax.experimental.pallas import tpu as pltpu
from jax.sharding import PartitionSpec as P

inv_temp = 2.5
prior_mass = 0.25
BOTH = ("samp", "cent")
UNIT = 64
X, Y, Z = 0, 1, 2
ORDERS = ((X, Y, Z), (Z, X, Y))


def place(x, y, z, core):
    return ((x // 2) * 4 + z) * 16 + (x % 2) * 8 + y * 2 + core


def fetch(value, stage, offset):
    pairs = []
    for x in range(4):
        for y in range(4):
            for z in range(4):
                for core in range(2):
                    at = [x, y, z]
                    axis = ORDERS[core][stage]
                    at[axis] = (at[axis] + offset) % 4
                    pairs.append((place(*at, core), place(x, y, z, core)))
    return lax.ppermute(value, BOTH, pairs)


def swap_cores(value):
    pairs = [(i, i ^ 1) for i in range(128)]
    return lax.ppermute(value, BOTH, pairs)


def scores_kernel(factor, count, mine_ref, other_ref, *refs):
    rows = refs[:count]
    ps = refs[count : 2 * count]
    stat_ref = refs[2 * count]
    tiles = [(k, part, half) for k in range(count) for part in range(2) for half in range(2)]

    def product(tile):
        k, part, half = tile
        return lax.dot_general(
            (mine_ref, other_ref)[half][...],
            rows[k][part * 256 : (part + 1) * 256, :],
            (((1,), (1,)), ((), ())),
            preferred_element_type=jnp.float32,
        )

    following = product(tiles[0])
    for i, (k, part, half) in enumerate(tiles):
        s = following * factor
        if i + 1 < len(tiles):
            following = product(tiles[i + 1])
        top = jnp.max(s, axis=0, keepdims=True)
        e = jnp.exp2(s - top)
        ps[k][half, :, part * 256 : (part + 1) * 256] = e
        lanes = slice(k * 512 + part * 256, k * 512 + (part + 1) * 256)
        stat_ref[half : half + 1, lanes] = top
        stat_ref[2 + half : 3 + half, lanes] = jnp.sum(e, axis=0, keepdims=True)


def scores_call(mine, other, rows):
    count = len(rows)
    n, width = rows[0].shape
    factor = inv_temp / math.sqrt(width) * math.log2(math.e)
    vmem = pl.BlockSpec(memory_space=pltpu.VMEM)
    *ps, stat = pl.pallas_call(
        functools.partial(scores_kernel, factor, count),
        out_shape=tuple([jax.ShapeDtypeStruct((2, 512, n), jnp.float32)] * count)
        + (jax.ShapeDtypeStruct((4, count * n), jnp.float32),),
        in_specs=[vmem] * (2 + count),
        out_specs=tuple([vmem] * (count + 1)),
        compiler_params=pltpu.CompilerParams(vmem_limit_bytes=12 << 20),
        cost_estimate=pl.CostEstimate(
            flops=4 * 1024 * n * width * count,
            bytes_accessed=count * n * 6144 + (2 << 20),
            transcendentals=1024 * n * count,
        ),
        name="scores",
    )(mine, other, *rows)
    return ps, stat


def roll_within(value, dim, step):
    inner = UNIT * 4**dim
    group = inner * 4
    size = value.shape[1]
    lane = lax.broadcasted_iota(jnp.int32, value.shape, 1) % group
    ahead = pltpu.roll(value, step * inner, 1)
    back = pltpu.roll(value, size - group + step * inner, 1)
    return jnp.where(lane >= step * inner, ahead, back)


def first_kernel(order, spot_ref, ids_ref, *refs):
    *stats, out_ref, top_ref = refs
    parts = []
    for k, (ref, piece) in enumerate(order):
        lanes = slice(piece * 512, (piece + 1) * 512)
        tops = stats[ref][0:2, lanes]
        top = jnp.max(tops, axis=0, keepdims=True)
        total = jnp.sum(stats[ref][2:4, lanes] * jnp.exp2(tops - top), axis=0, keepdims=True)
        parts.append(top + jnp.log2(total))
        top_ref[:, k * 512 : (k + 1) * 512] = tops
    value = jnp.concatenate(parts, axis=1)
    for dim in range(3):
        value = roll_within(value, dim, spot_ref[dim])
    for line in range(8):
        piece = value[:, line * 512 : (line + 1) * 512]
        out_ref[:, line, 0:512] = jnp.broadcast_to(piece, (64, 512))
    lane = lax.broadcasted_iota(jnp.int32, (1, 128), 1)
    ids = jnp.where(lane // UNIT == spot_ref[0] % 2, ids_ref[...], -1.0)
    out_ref[:, :, 512:640] = jnp.broadcast_to(ids.reshape(1, 1, 128), (64, 8, 128))


def merge_kernel(spot_ref, all_ref, whole_ref, own_ref):
    values = all_ref[:, :, 0:512]
    top = jnp.max(values, axis=0)
    total = jnp.sum(jnp.exp2(values - top[None]), axis=0)
    lse = top + jnp.log2(total)
    whole_ref[...] = lse
    value = jnp.concatenate([lse[line : line + 1, :] for line in range(8)], axis=1)
    for dim in range(3):
        value = roll_within(value, dim, (4 - spot_ref[dim]) % 4)
    own_ref[...] = value


def pack_kernel(whole_ref, all_ref, out_ref):
    for line in range(32):
        tile = line % 4
        out_ref[line : line + 1, :] = whole_ref[line // 4 : line // 4 + 1, tile * 128 : (tile + 1) * 128]
        pair = jnp.maximum(all_ref[2 * line, 0:1, 512:640], all_ref[2 * line + 1, 0:1, 512:640])
        out_ref[32 + line : 33 + line, :] = pair


def route_kernel(at_ref, mine_ref, other_ref, out_ref):
    first = (at_ref[0] * 16 + at_ref[1]) * UNIT
    rows = (lax.broadcasted_iota(jnp.int32, (UNIT, 128), 0) + first).astype(jnp.float32)
    total = jnp.zeros((UNIT, 128), jnp.float32)
    for ref in (mine_ref, other_ref):
        for line in range(32):
            hit = ref[32 + line : 33 + line, :] == rows
            total = total + jnp.where(hit, ref[line : line + 1, :], 0.0)
    out_ref[...] = total


def join_kernel(*refs):
    *parts, out_ref = refs
    at = 0
    for part in parts:
        out_ref[at : at + part.shape[0], :] = part[...]
        at += part.shape[0]


def join(*parts):
    vmem = pl.BlockSpec(memory_space=pltpu.VMEM)
    shape = (sum(part.shape[0] for part in parts), parts[0].shape[1])
    return pl.pallas_call(
        join_kernel,
        out_shape=jax.ShapeDtypeStruct(shape, parts[0].dtype),
        in_specs=[vmem] * len(parts),
        out_specs=vmem,
        compiler_params=pltpu.CompilerParams(vmem_limit_bytes=8 << 20),
        name="join",
    )(*parts)


def sums_kernel(half, count, lse_ref, top_ref, *refs):
    ps = refs[:count]
    rows = refs[count : 2 * count]
    out_ref = refs[2 * count]
    n, width = rows[0].shape

    def weights(k):
        lanes = slice(k * n, (k + 1) * n)
        f = jnp.exp2(top_ref[half : half + 1, lanes] - lse_ref[:, lanes])
        w = (ps[k][half] * f).astype(jnp.bfloat16)
        wide = w.astype(jnp.float32)
        return w, sum(wide[:, c : c + 128] for c in range(0, n, 128))

    w, mass = weights(0)
    for k in range(count):
        now = w
        if k + 1 < count:
            w, more = weights(k + 1)
            mass = mass + more
        add = jnp.dot(now, rows[k][...], preferred_element_type=jnp.float32)
        if k == 0:
            out_ref[:, :width] = add
        else:
            out_ref[:, :width] += add
    out_ref[:, width:] = mass


def sums_call(half, lse, tops, ps, rows):
    count = len(rows)
    width = rows[0].shape[1]
    vmem = pl.BlockSpec(memory_space=pltpu.VMEM)
    return pl.pallas_call(
        functools.partial(sums_kernel, half, count),
        out_shape=jax.ShapeDtypeStruct((512, width + 128), jnp.float32),
        in_specs=[vmem] * (2 + 2 * count),
        compiler_params=pltpu.CompilerParams(vmem_limit_bytes=10 << 20),
        cost_estimate=pl.CostEstimate(
            flops=2 * 512 * 4096 * width, bytes_accessed=18 << 20, transcendentals=8192
        ),
        name="sums",
    )(lse, tops, *ps, *rows)


def final_kernel(ours_ref, theirs_ref, mine_ref, out_ref):
    width = out_ref.shape[1]
    mass = jnp.sum(ours_ref[:, width:] + theirs_ref[:, width:], axis=1, keepdims=True) + prior_mass
    total = ours_ref[:, :width] + theirs_ref[:, :width] + prior_mass * mine_ref[...].astype(jnp.float32)
    out_ref[...] = total * (1.0 / mass)


def share_kernel(at_ref, cents_ref, out_ref, sem):
    size = out_ref.shape[0]
    first = pl.multiple_of(at_ref[0] * size, size)
    copy = pltpu.make_async_copy(cents_ref.at[pl.ds(first, size)], out_ref, sem)
    copy.start()
    copy.wait()


def shards(embeddings, destination, centroids):
    samp, cent = lax.axis_index("samp"), lax.axis_index("cent")
    core = lax.bitwise_and(cent, 1)
    x = lax.shift_right_logical(samp, 2) * 2 + lax.shift_right_logical(cent, 3)
    y, z = lax.bitwise_and(lax.shift_right_logical(cent, 1), 3), lax.bitwise_and(samp, 3)
    spot = jnp.where(core == 0, jnp.stack([x, y, z]), jnp.stack([z, x, y])).astype(jnp.int32)
    share = centroids.shape[0] // 8
    width = embeddings.shape[1]
    smem = pl.BlockSpec(memory_space=pltpu.SMEM)
    vmem = pl.BlockSpec(memory_space=pltpu.VMEM)
    small = pltpu.CompilerParams(vmem_limit_bytes=8 << 20)
    line = join(embeddings, *[fetch(embeddings, 0, step) for step in (1, 2, 3)])
    spot, destination, _ = lax.optimization_barrier((spot, destination, line))
    mine = pl.pallas_call(
        share_kernel,
        out_shape=jax.ShapeDtypeStruct((share, width), centroids.dtype),
        in_specs=[smem, pl.BlockSpec(memory_space=pltpu.HBM)],
        out_specs=vmem,
        scratch_shapes=[pltpu.SemaphoreType.DMA(())],
        compiler_params=pltpu.CompilerParams(vmem_limit_bytes=56 << 20),
        name="share",
    )(samp.astype(jnp.int32).reshape(1), centroids)
    other = swap_cores(mine)
    ids = jnp.tile(destination.astype(jnp.float32), 2).reshape(1, 128)
    near, across, back = [fetch(line, 1, step) for step in (1, 2, 3)]
    upper, lower = join(line, near), join(across, back)
    upper, lower, other, ids = lax.optimization_barrier((upper, lower, other, ids))
    after_upper, before_lower = fetch(upper, 2, 1), fetch(lower, 2, 3)

    p_upper, stat_upper = scores_call(mine, other, [upper])
    upper_again, lower_again, _ = lax.optimization_barrier((upper, lower, stat_upper))
    after_lower, before_upper = fetch(lower_again, 2, 1), fetch(upper_again, 2, 3)
    p_lower, stat_lower = scores_call(mine, other, [lower])
    passed_up, passed_down, _ = lax.optimization_barrier((after_upper, before_lower, stat_lower))
    far_upper, far_lower = fetch(passed_up, 2, 1), fetch(passed_down, 2, 3)
    p_first, stat_first = scores_call(mine, other, [after_upper, before_lower])
    p_second, stat_second = scores_call(mine, other, [after_lower, before_upper])
    p_third, stat_third = scores_call(mine, other, [far_upper])
    p_fourth, stat_fourth = scores_call(mine, other, [far_lower])
    chunks = [upper, lower, after_upper, after_lower, far_upper, far_lower, before_upper, before_lower]
    ps = p_upper + p_lower + [p_first[0], p_second[0]] + p_third + p_fourth + [p_second[1], p_first[1]]
    order = ((0, 0), (1, 0), (2, 0), (3, 0), (4, 0), (5, 0), (3, 1), (2, 1))

    local, tops = pl.pallas_call(
        functools.partial(first_kernel, order),
        out_shape=(
            jax.ShapeDtypeStruct((64, 8, 640), jnp.float32),
            jax.ShapeDtypeStruct((2, 4096), jnp.float32),
        ),
        in_specs=[smem] + [vmem] * 7,
        compiler_params=small,
        name="first",
    )(spot, ids, stat_upper, stat_lower, stat_first, stat_second, stat_third, stat_fourth)
    chips = []
    for side in range(2):
        group = []
        for i in range(64):
            at = [0, 0, 0]
            for dim in range(3):
                at[ORDERS[side][dim]] = i // 4**dim % 4
            group.append(place(*at, side))
        chips.append(group)
    shared = lax.all_to_all(local, BOTH, split_axis=0, concat_axis=0, tiled=True, axis_index_groups=chips)
    whole, lse = pl.pallas_call(
        merge_kernel,
        out_shape=(
            jax.ShapeDtypeStruct((8, 512), jnp.float32),
            jax.ShapeDtypeStruct((1, 4096), jnp.float32),
        ),
        in_specs=[smem, vmem],
        compiler_params=small,
        name="merge",
    )(spot, shared)
    theirs = sums_call(1, lse, tops, ps, chunks)
    received = swap_cores(theirs)
    whole, shared, _ = lax.optimization_barrier((whole, shared, theirs))
    pack = pl.pallas_call(
        pack_kernel,
        out_shape=jax.ShapeDtypeStruct((64, 128), jnp.float32),
        in_specs=[vmem] * 2,
        compiler_params=small,
        name="pack",
    )(whole, shared)
    partner = swap_cores(pack)
    ours = sums_call(0, lse, tops, ps, chunks)
    spread = pl.pallas_call(
        route_kernel,
        out_shape=jax.ShapeDtypeStruct((UNIT, 128), jnp.float32),
        in_specs=[smem, vmem, vmem],
        compiler_params=small,
        name="route",
    )(jnp.stack([samp, cent]).astype(jnp.int32), pack, partner)
    row_lse = jnp.sum(spread, axis=1) * math.log(2.0)
    new_centers = pl.pallas_call(
        final_kernel, out_shape=jax.ShapeDtypeStruct((share, width), jnp.float32), name="final",
        compiler_params=pltpu.CompilerParams(vmem_limit_bytes=8 << 20),
    )(ours, received, mine)
    return new_centers, row_lse


def solution(mesh):
    in_specs = (P(BOTH, None), P(BOTH), P("cent", None))
    out_specs = (P(("cent", "samp"), None), P(BOTH))
    return jax.shard_map(shards, mesh=mesh, in_specs=in_specs, out_specs=out_specs, check_vma=False)
```

```python
import functools
import math

import jax
import jax.numpy as jnp
from jax import lax
from jax.experimental import pallas as pl
from jax.experimental.pallas import tpu as pltpu
from jax.sharding import PartitionSpec as P

inv_temp = 2.5
prior_mass = 0.25
BOTH = ("samp", "cent")
UNIT = 64
X, Y, Z = 0, 1, 2
ORDERS = ((X, Y, Z), (X, Z, Y))


def place(x, y, z, core):
    return ((x // 2) * 4 + z) * 16 + (x % 2) * 8 + y * 2 + core


def fetch(value, stage, offset):
    pairs = []
    for x in range(4):
        for y in range(4):
            for z in range(4):
                for core in range(2):
                    at = [x, y, z]
                    axis = ORDERS[core][stage]
                    at[axis] = (at[axis] + offset) % 4
                    pairs.append((place(*at, core), place(x, y, z, core)))
    return lax.ppermute(value, BOTH, pairs)


def swap_cores(value):
    pairs = [(i, i ^ 1) for i in range(128)]
    return lax.ppermute(value, BOTH, pairs)


def swap_sides(value):
    pairs = []
    for x in range(4):
        for y in range(4):
            for z in range(4):
                for core in range(2):
                    other = (x + (1 if x % 2 == core else 3)) % 4
                    pairs.append((place(other, y, z, core), place(x, y, z, core)))
    return lax.ppermute(value, BOTH, pairs)


def scores_kernel(factor, count, mine_ref, other_ref, *refs):
    rows = refs[:count]
    ps = refs[count : 2 * count]
    stat_ref = refs[2 * count]
    tiles = [(k, part, half) for k in range(count) for part in range(2) for half in range(2)]

    def product(tile):
        k, part, half = tile
        return lax.dot_general(
            (mine_ref, other_ref)[half][...],
            rows[k][part * 256 : (part + 1) * 256, :],
            (((1,), (1,)), ((), ())),
            preferred_element_type=jnp.float32,
        )

    following = product(tiles[0])
    for i, (k, part, half) in enumerate(tiles):
        s = following * factor
        if i + 1 < len(tiles):
            following = product(tiles[i + 1])
        top = jnp.max(s, axis=0, keepdims=True)
        e = jnp.exp2(s - top)
        ps[k][half, :, part * 256 : (part + 1) * 256] = e
        lanes = slice(k * 512 + part * 256, k * 512 + (part + 1) * 256)
        stat_ref[half : half + 1, lanes] = top
        stat_ref[2 + half : 3 + half, lanes] = jnp.sum(e, axis=0, keepdims=True)


def scores_call(mine, other, rows):
    count = len(rows)
    n, width = rows[0].shape
    factor = inv_temp / math.sqrt(width) * math.log2(math.e)
    vmem = pl.BlockSpec(memory_space=pltpu.VMEM)
    *ps, stat = pl.pallas_call(
        functools.partial(scores_kernel, factor, count),
        out_shape=tuple([jax.ShapeDtypeStruct((2, 512, n), jnp.float32)] * count)
        + (jax.ShapeDtypeStruct((4, count * n), jnp.float32),),
        in_specs=[vmem] * (2 + count),
        out_specs=tuple([vmem] * (count + 1)),
        compiler_params=pltpu.CompilerParams(vmem_limit_bytes=12 << 20),
        cost_estimate=pl.CostEstimate(
            flops=4 * 1024 * n * width * count,
            bytes_accessed=count * n * 6144 + (2 << 20),
            transcendentals=1024 * n * count,
        ),
        name="scores",
    )(mine, other, *rows)
    return ps, stat


def roll_within(value, dim, step):
    inner = UNIT * 4**dim
    group = inner * 4
    size = value.shape[1]
    lane = lax.broadcasted_iota(jnp.int32, value.shape, 1) % group
    ahead = pltpu.roll(value, step * inner, 1)
    back = pltpu.roll(value, size - group + step * inner, 1)
    return jnp.where(lane >= step * inner, ahead, back)


def first_kernel(swapped, spot_ref, ids_ref, *refs):
    *stats, out_ref, top_ref = refs
    parts = []
    for k, ref in enumerate(stats):
        tops = ref[0:2, :]
        top = jnp.max(tops, axis=0, keepdims=True)
        total = jnp.sum(ref[2:4, :] * jnp.exp2(tops - top), axis=0, keepdims=True)
        part = top + jnp.log2(total)
        parts.append(roll_within(part, 0, spot_ref[3]) if k in swapped else part)
        top_ref[:, k * 512 : (k + 1) * 512] = tops
    value = jnp.concatenate(parts, axis=1)
    for dim in range(3):
        value = roll_within(value, dim, spot_ref[dim])
    for line in range(8):
        piece = value[:, line * 512 : (line + 1) * 512]
        out_ref[:, line, 0:512] = jnp.broadcast_to(piece, (64, 512))
    lane = lax.broadcasted_iota(jnp.int32, (1, 128), 1)
    ids = jnp.where(lane // UNIT == spot_ref[0] % 2, ids_ref[...], -1.0)
    out_ref[:, :, 512:640] = jnp.broadcast_to(ids.reshape(1, 1, 128), (64, 8, 128))


def merge_kernel(swapped, spot_ref, all_ref, whole_ref, own_ref):
    values = all_ref[:, :, 0:512]
    top = jnp.max(values, axis=0)
    total = jnp.sum(jnp.exp2(values - top[None]), axis=0)
    lse = top + jnp.log2(total)
    whole_ref[...] = lse
    value = jnp.concatenate([lse[line : line + 1, :] for line in range(8)], axis=1)
    for dim in range(3):
        value = roll_within(value, dim, (4 - spot_ref[dim]) % 4)
    own_ref[...] = value
    for k in swapped:
        lanes = slice(k * 512, (k + 1) * 512)
        own_ref[:, lanes] = roll_within(value[:, lanes], 0, 4 - spot_ref[3])


def pack_kernel(whole_ref, all_ref, out_ref):
    for line in range(32):
        tile = line % 4
        out_ref[line : line + 1, :] = whole_ref[line // 4 : line // 4 + 1, tile * 128 : (tile + 1) * 128]
        pair = jnp.maximum(all_ref[2 * line, 0:1, 512:640], all_ref[2 * line + 1, 0:1, 512:640])
        out_ref[32 + line : 33 + line, :] = pair


def route_kernel(at_ref, mine_ref, other_ref, out_ref):
    first = (at_ref[0] * 16 + at_ref[1]) * UNIT
    rows = (lax.broadcasted_iota(jnp.int32, (UNIT, 128), 0) + first).astype(jnp.float32)
    total = jnp.zeros((UNIT, 128), jnp.float32)
    for ref in (mine_ref, other_ref):
        for line in range(32):
            hit = ref[32 + line : 33 + line, :] == rows
            total = total + jnp.where(hit, ref[line : line + 1, :], 0.0)
    out_ref[...] = jnp.sum(total.T, axis=0, keepdims=True) * math.log(2.0)


def join_kernel(*refs):
    *parts, out_ref = refs
    at = 0
    for part in parts:
        out_ref[at : at + part.shape[0], :] = part[...]
        at += part.shape[0]


def halves_kernel(spot_ref, *refs):
    *parts, first_ref, second_ref = refs
    rows = parts[0].shape[0]
    for side in range(2):

        @pl.when(spot_ref[4] == side)
        def _():
            for k, part in enumerate(parts):
                out_ref = (first_ref, second_ref)[(k // 2 + side) % 2]
                out_ref[k % 2 * rows : (k % 2 + 1) * rows, :] = part[...]


def join(*parts):
    vmem = pl.BlockSpec(memory_space=pltpu.VMEM)
    shape = (sum(part.shape[0] for part in parts), parts[0].shape[1])
    return pl.pallas_call(
        join_kernel,
        out_shape=jax.ShapeDtypeStruct(shape, parts[0].dtype),
        in_specs=[vmem] * len(parts),
        out_specs=vmem,
        compiler_params=pltpu.CompilerParams(vmem_limit_bytes=8 << 20),
        name="join",
    )(*parts)


def sums_kernel(half, count, lse_ref, top_ref, *refs):
    ps = refs[:count]
    rows = refs[count : 2 * count]
    out_ref = refs[2 * count]
    n, width = rows[0].shape

    def weights(k):
        lanes = slice(k * n, (k + 1) * n)
        f = jnp.exp2(top_ref[half : half + 1, lanes] - lse_ref[:, lanes])
        w = (ps[k][half] * f).astype(jnp.bfloat16)
        wide = w.astype(jnp.float32)
        return w, sum(wide[:, c : c + 128] for c in range(0, n, 128))

    w, mass = weights(0)
    for k in range(count):
        now = w
        if k + 1 < count:
            w, more = weights(k + 1)
            mass = mass + more
        add = jnp.dot(now, rows[k][...], preferred_element_type=jnp.float32)
        if k == 0:
            out_ref[:, :width] = add
        else:
            out_ref[:, :width] += add
    out_ref[:, width:] = mass


def sums_call(half, lse, tops, ps, rows):
    count = len(rows)
    width = rows[0].shape[1]
    vmem = pl.BlockSpec(memory_space=pltpu.VMEM)
    return pl.pallas_call(
        functools.partial(sums_kernel, half, count),
        out_shape=jax.ShapeDtypeStruct((512, width + 128), jnp.float32),
        in_specs=[vmem] * (2 + 2 * count),
        compiler_params=pltpu.CompilerParams(vmem_limit_bytes=12 << 20),
        cost_estimate=pl.CostEstimate(
            flops=2 * 512 * 4096 * width, bytes_accessed=18 << 20, transcendentals=8192
        ),
        name="sums",
    )(lse, tops, *ps, *rows)


def final_kernel(ours_ref, theirs_ref, mine_ref, out_ref):
    width = out_ref.shape[1]
    mass = jnp.sum(ours_ref[:, width:] + theirs_ref[:, width:], axis=1, keepdims=True) + prior_mass
    total = ours_ref[:, :width] + theirs_ref[:, :width] + prior_mass * mine_ref[...].astype(jnp.float32)
    out_ref[...] = total * (1.0 / mass)


def share_kernel(at_ref, cents_ref, out_ref, sem):
    size = out_ref.shape[0]
    first = pl.multiple_of(at_ref[0] * size, size)
    part = size // 8
    copies = [
        pltpu.make_async_copy(
            cents_ref.at[pl.ds(first + k * part, part)], out_ref.at[pl.ds(k * part, part)], sem.at[k]
        )
        for k in range(8)
    ]
    for copy in copies:
        copy.start()
    for copy in copies:
        copy.wait()


def shards(embeddings, destination, centroids):
    samp, cent = lax.axis_index("samp"), lax.axis_index("cent")
    core = lax.bitwise_and(cent, 1)
    x = lax.shift_right_logical(samp, 2) * 2 + lax.shift_right_logical(cent, 3)
    y, z = lax.bitwise_and(lax.shift_right_logical(cent, 1), 3), lax.bitwise_and(samp, 3)
    side = lax.bitwise_and(x, 1)
    second = lax.bitwise_and(jnp.where(core == 0, y, z) + 2 * side, 3)
    step = jnp.where(side == core, 1, 3)
    spot = jnp.stack([x, second, jnp.where(core == 0, z, y), step, side]).astype(jnp.int32)
    share = centroids.shape[0] // 8
    width = embeddings.shape[1]
    smem = pl.BlockSpec(memory_space=pltpu.SMEM)
    vmem = pl.BlockSpec(memory_space=pltpu.VMEM)
    small = pltpu.CompilerParams(vmem_limit_bytes=8 << 20)
    line = join(embeddings, *[fetch(embeddings, 0, step) for step in (1, 2, 3)])
    near, across, back = [fetch(line, 1, step) for step in (1, 2, 3)]
    destination, _ = lax.optimization_barrier((destination, line))
    ids = jnp.tile(destination.astype(jnp.float32), 2).reshape(1, 128)
    first, second = pl.pallas_call(
        halves_kernel,
        out_shape=[jax.ShapeDtypeStruct((512, width), embeddings.dtype)] * 2,
        in_specs=[smem] + [vmem] * 4,
        out_specs=[vmem] * 2,
        compiler_params=small,
        name="halves",
    )(spot, line, near, across, back)
    at_word = jnp.stack([samp, cent]).astype(jnp.int32)
    first, second, ids, spot, at_word = lax.optimization_barrier((first, second, ids, spot, at_word))
    far_first = fetch(first, 2, 2)
    mine = pl.pallas_call(
        share_kernel,
        out_shape=jax.ShapeDtypeStruct((share, width), centroids.dtype),
        in_specs=[smem, pl.BlockSpec(memory_space=pltpu.HBM)],
        out_specs=vmem,
        scratch_shapes=[pltpu.SemaphoreType.DMA((8,))],
        compiler_params=pltpu.CompilerParams(vmem_limit_bytes=54 << 20),
        name="share",
    )(at_word, centroids)
    other = swap_cores(mine)
    first_again, mine = lax.optimization_barrier((first, mine))
    after_first, before_first = fetch(first_again, 2, 1), fetch(first_again, 2, 3)
    score = functools.partial(scores_call, mine, other)
    own_first = score([first])
    second_again, _ = lax.optimization_barrier((second, own_first[1]))
    own_second = score([second])
    after_second, before_second = fetch(second_again, 2, 1), fetch(second_again, 2, 3)
    far_second = swap_sides(far_first)
    chunks = [first, second, after_first, after_second, far_first, far_second, before_first, before_second]
    swapped = (5,)
    pairs = [own_first, own_second] + [score([chunk]) for chunk in chunks[2:]]
    ps = [p[0] for p, _ in pairs]
    stats = [stat for _, stat in pairs]

    local, tops = pl.pallas_call(
        functools.partial(first_kernel, swapped),
        out_shape=(
            jax.ShapeDtypeStruct((64, 8, 640), jnp.float32),
            jax.ShapeDtypeStruct((2, 4096), jnp.float32),
        ),
        in_specs=[smem] + [vmem] * 9,
        compiler_params=small,
        name="first",
    )(spot, ids, *stats)
    chips = []
    for side in range(2):
        group = []
        for i in range(64):
            at = [0, 0, 0]
            for dim in range(3):
                at[ORDERS[side][dim]] = i // 4**dim % 4
            group.append(place(*at, side))
        chips.append(group)
    shared = lax.all_to_all(local, BOTH, split_axis=0, concat_axis=0, tiled=True, axis_index_groups=chips)
    whole, lse = pl.pallas_call(
        functools.partial(merge_kernel, swapped),
        out_shape=(
            jax.ShapeDtypeStruct((8, 512), jnp.float32),
            jax.ShapeDtypeStruct((1, 4096), jnp.float32),
        ),
        in_specs=[smem, vmem],
        compiler_params=small,
        name="merge",
    )(spot, shared)
    theirs = sums_call(1, lse, tops, ps, chunks)
    received = swap_cores(theirs)
    whole, shared, _ = lax.optimization_barrier((whole, shared, theirs))
    pack = pl.pallas_call(
        pack_kernel,
        out_shape=jax.ShapeDtypeStruct((64, 128), jnp.float32),
        in_specs=[vmem] * 2,
        compiler_params=small,
        name="pack",
    )(whole, shared)
    partner = swap_cores(pack)
    ours = sums_call(0, lse, tops, ps, chunks)
    row_lse = pl.pallas_call(
        route_kernel,
        out_shape=jax.ShapeDtypeStruct((1, UNIT), jnp.float32),
        in_specs=[smem, vmem, vmem],
        compiler_params=small,
        name="route",
    )(at_word, pack, partner)
    new_centers = pl.pallas_call(
        final_kernel, out_shape=jax.ShapeDtypeStruct((share, width), jnp.float32), name="final",
        compiler_params=pltpu.CompilerParams(vmem_limit_bytes=8 << 20),
    )(ours, received, mine)
    return new_centers, row_lse.reshape(UNIT)


def solution(mesh):
    in_specs = (P(BOTH, None), P(BOTH), P("cent", None))
    out_specs = (P(("cent", "samp"), None), P(BOTH))
    return jax.shard_map(shards, mesh=mesh, in_specs=in_specs, out_specs=out_specs, check_vma=False)
```

```python
import functools
import math

import jax
import jax.numpy as jnp
from jax import lax
from jax.experimental import pallas as pl
from jax.experimental.pallas import tpu as pltpu
from jax.sharding import PartitionSpec as P

inv_temp = 2.5
prior_mass = 0.25
BOTH = ("samp", "cent")
UNIT = 64
X, Y, Z = 0, 1, 2
ORDERS = ((X, Y, Z), (X, Z, Y))


def place(x, y, z, core):
    return ((x // 2) * 4 + z) * 16 + (x % 2) * 8 + y * 2 + core


def fetch(value, stage, offset):
    pairs = []
    for x in range(4):
        for y in range(4):
            for z in range(4):
                for core in range(2):
                    at = [x, y, z]
                    axis = ORDERS[core][stage]
                    at[axis] = (at[axis] + offset) % 4
                    pairs.append((place(*at, core), place(x, y, z, core)))
    return lax.ppermute(value, BOTH, pairs)


def swap_cores(value):
    pairs = [(i, i ^ 1) for i in range(128)]
    return lax.ppermute(value, BOTH, pairs)


def swap_sides(value):
    pairs = []
    for x in range(4):
        for y in range(4):
            for z in range(4):
                for core in range(2):
                    other = (x + (1 if x % 2 == core else 3)) % 4
                    pairs.append((place(other, y, z, core), place(x, y, z, core)))
    return lax.ppermute(value, BOTH, pairs)


def scores_kernel(factor, count, mine_ref, other_ref, *refs):
    rows = refs[:count]
    ps = refs[count : 2 * count]
    stat_ref = refs[2 * count]
    tiles = [(k, part, half) for k in range(count) for part in range(2) for half in range(2)]

    def product(tile):
        k, part, half = tile
        return lax.dot_general(
            (mine_ref, other_ref)[half][...],
            rows[k][part * 256 : (part + 1) * 256, :],
            (((1,), (1,)), ((), ())),
            preferred_element_type=jnp.float32,
        )

    following = product(tiles[0])
    for i, (k, part, half) in enumerate(tiles):
        s = following * factor
        if i + 1 < len(tiles):
            following = product(tiles[i + 1])
        top = jnp.max(s, axis=0, keepdims=True)
        e = jnp.exp2(s - top)
        ps[k][half, :, part * 256 : (part + 1) * 256] = e
        lanes = slice(k * 512 + part * 256, k * 512 + (part + 1) * 256)
        stat_ref[half : half + 1, lanes] = top
        stat_ref[2 + half : 3 + half, lanes] = jnp.sum(e, axis=0, keepdims=True)


def scores_call(mine, other, rows):
    count = len(rows)
    n, width = rows[0].shape
    factor = inv_temp / math.sqrt(width) * math.log2(math.e)
    vmem = pl.BlockSpec(memory_space=pltpu.VMEM)
    *ps, stat = pl.pallas_call(
        functools.partial(scores_kernel, factor, count),
        out_shape=tuple([jax.ShapeDtypeStruct((2, 512, n), jnp.float32)] * count)
        + (jax.ShapeDtypeStruct((4, count * n), jnp.float32),),
        in_specs=[vmem] * (2 + count),
        out_specs=tuple([vmem] * (count + 1)),
        compiler_params=pltpu.CompilerParams(vmem_limit_bytes=12 << 20),
        cost_estimate=pl.CostEstimate(
            flops=4 * 1024 * n * width * count,
            bytes_accessed=count * n * 6144 + (2 << 20),
            transcendentals=1024 * n * count,
        ),
        name="scores",
    )(mine, other, *rows)
    return ps, stat


def roll_within(value, dim, step):
    inner = UNIT * 4**dim
    group = inner * 4
    size = value.shape[1]
    lane = lax.broadcasted_iota(jnp.int32, value.shape, 1) % group
    ahead = pltpu.roll(value, step * inner, 1)
    back = pltpu.roll(value, size - group + step * inner, 1)
    return jnp.where(lane >= step * inner, ahead, back)


def first_kernel(swapped, spot_ref, ids_ref, *refs):
    *stats, out_ref, top_ref = refs
    parts = []
    for k, ref in enumerate(stats):
        tops = ref[0:2, :]
        top = jnp.max(tops, axis=0, keepdims=True)
        total = jnp.sum(ref[2:4, :] * jnp.exp2(tops - top), axis=0, keepdims=True)
        part = top + jnp.log2(total)
        parts.append(roll_within(part, 0, spot_ref[3]) if k in swapped else part)
        top_ref[:, k * 512 : (k + 1) * 512] = tops
    value = jnp.concatenate(parts, axis=1)
    for dim in range(3):
        value = roll_within(value, dim, spot_ref[dim])
    for line in range(8):
        piece = value[:, line * 512 : (line + 1) * 512]
        out_ref[:, line, 0:512] = jnp.broadcast_to(piece, (64, 512))
    lane = lax.broadcasted_iota(jnp.int32, (1, 128), 1)
    ids = jnp.where(lane // UNIT == spot_ref[0] % 2, ids_ref[...], -1.0)
    out_ref[:, :, 512:640] = jnp.broadcast_to(ids.reshape(1, 1, 128), (64, 8, 128))


def merge_kernel(swapped, spot_ref, all_ref, whole_ref, own_ref):
    values = all_ref[:, :, 0:512]
    top = jnp.max(values, axis=0)
    total = jnp.sum(jnp.exp2(values - top[None]), axis=0)
    lse = top + jnp.log2(total)
    whole_ref[...] = lse
    value = jnp.concatenate([lse[line : line + 1, :] for line in range(8)], axis=1)
    for dim in range(3):
        value = roll_within(value, dim, (4 - spot_ref[dim]) % 4)
    own_ref[...] = value
    for k in swapped:
        lanes = slice(k * 512, (k + 1) * 512)
        own_ref[:, lanes] = roll_within(value[:, lanes], 0, 4 - spot_ref[3])


def pack_kernel(at_ref, whole_ref, all_ref, out_ref):
    first_core = at_ref[1] % 2 == 0
    for line in range(32):
        tile = line % 4
        out_ref[line : line + 1, :] = whole_ref[line // 4 : line // 4 + 1, tile * 128 : (tile + 1) * 128]
        low, high = line // 2 % 4, line // 8
        chip = line % 2 * 32 + jnp.where(first_core, low * 4 + high, high * 4 + low)
        pair = jnp.maximum(all_ref[chip, 0:1, 512:640], all_ref[chip + 16, 0:1, 512:640])
        out_ref[32 + line : 33 + line, :] = pair


def route_kernel(at_ref, mine_ref, other_ref, out_ref):
    first = (at_ref[0] * 16 + at_ref[1]) * UNIT
    rows = (lax.broadcasted_iota(jnp.int32, (UNIT, 128), 0) + first).astype(jnp.float32)
    total = jnp.zeros((UNIT, 128), jnp.float32)
    for ref in (mine_ref, other_ref):
        for line in range(32):
            hit = ref[32 + line : 33 + line, :] == rows
            total = total + jnp.where(hit, ref[line : line + 1, :], 0.0)
    out_ref[...] = jnp.sum(total.T, axis=0, keepdims=True) * math.log(2.0)


def join_kernel(*refs):
    *parts, out_ref = refs
    at = 0
    for part in parts:
        out_ref[at : at + part.shape[0], :] = part[...]
        at += part.shape[0]


def halves_kernel(spot_ref, *refs):
    *parts, first_ref, second_ref = refs
    rows = parts[0].shape[0]
    for side in range(2):

        @pl.when(spot_ref[4] == side)
        def _():
            for k, part in enumerate(parts):
                out_ref = (first_ref, second_ref)[(k // 2 + side) % 2]
                out_ref[k % 2 * rows : (k % 2 + 1) * rows, :] = part[...]


def join(*parts):
    vmem = pl.BlockSpec(memory_space=pltpu.VMEM)
    shape = (sum(part.shape[0] for part in parts), parts[0].shape[1])
    return pl.pallas_call(
        join_kernel,
        out_shape=jax.ShapeDtypeStruct(shape, parts[0].dtype),
        in_specs=[vmem] * len(parts),
        out_specs=vmem,
        compiler_params=pltpu.CompilerParams(vmem_limit_bytes=8 << 20),
        name="join",
    )(*parts)


def sums_kernel(half, count, lse_ref, top_ref, *refs):
    ps = refs[:count]
    rows = refs[count : 2 * count]
    out_ref = refs[2 * count]
    n, width = rows[0].shape

    def weights(k):
        lanes = slice(k * n, (k + 1) * n)
        f = jnp.exp2(top_ref[half : half + 1, lanes] - lse_ref[:, lanes])
        w = (ps[k][half] * f).astype(jnp.bfloat16)
        wide = w.astype(jnp.float32)
        return w, sum(wide[:, c : c + 128] for c in range(0, n, 128))

    w, mass = weights(0)
    for k in range(count):
        now = w
        if k + 1 < count:
            w, more = weights(k + 1)
            mass = mass + more
        add = jnp.dot(now, rows[k][...], preferred_element_type=jnp.float32)
        if k == 0:
            out_ref[:, :width] = add
        else:
            out_ref[:, :width] += add
    out_ref[:, width:] = mass


def sums_call(half, lse, tops, ps, rows):
    count = len(rows)
    width = rows[0].shape[1]
    vmem = pl.BlockSpec(memory_space=pltpu.VMEM)
    return pl.pallas_call(
        functools.partial(sums_kernel, half, count),
        out_shape=jax.ShapeDtypeStruct((512, width + 128), jnp.float32),
        in_specs=[vmem] * (2 + 2 * count),
        compiler_params=pltpu.CompilerParams(vmem_limit_bytes=12 << 20),
        cost_estimate=pl.CostEstimate(
            flops=2 * 512 * 4096 * width, bytes_accessed=18 << 20, transcendentals=8192
        ),
        name="sums",
    )(lse, tops, *ps, *rows)


def final_kernel(ours_ref, theirs_ref, mine_ref, out_ref):
    width = out_ref.shape[1]
    mass = jnp.sum(ours_ref[:, width:] + theirs_ref[:, width:], axis=1, keepdims=True) + prior_mass
    total = ours_ref[:, :width] + theirs_ref[:, :width] + prior_mass * mine_ref[...].astype(jnp.float32)
    out_ref[...] = total * (1.0 / mass)


def share_kernel(at_ref, cents_ref, out_ref, sem):
    size = out_ref.shape[0]
    first = pl.multiple_of(at_ref[0] * size, size)
    part = size // 8
    copies = [
        pltpu.make_async_copy(
            cents_ref.at[pl.ds(first + k * part, part)], out_ref.at[pl.ds(k * part, part)], sem.at[k]
        )
        for k in range(8)
    ]
    for copy in copies:
        copy.start()
    for copy in copies:
        copy.wait()


def shards(embeddings, destination, centroids):
    samp, cent = lax.axis_index("samp"), lax.axis_index("cent")
    core = lax.bitwise_and(cent, 1)
    x = lax.shift_right_logical(samp, 2) * 2 + lax.shift_right_logical(cent, 3)
    y, z = lax.bitwise_and(lax.shift_right_logical(cent, 1), 3), lax.bitwise_and(samp, 3)
    side = lax.bitwise_and(x, 1)
    second = lax.bitwise_and(jnp.where(core == 0, y, z) + 2 * side, 3)
    step = jnp.where(side == core, 1, 3)
    spot = jnp.stack([x, second, jnp.where(core == 0, z, y), step, side]).astype(jnp.int32)
    share = centroids.shape[0] // 8
    width = embeddings.shape[1]
    smem = pl.BlockSpec(memory_space=pltpu.SMEM)
    vmem = pl.BlockSpec(memory_space=pltpu.VMEM)
    small = pltpu.CompilerParams(vmem_limit_bytes=8 << 20)
    ids = jnp.tile(destination.astype(jnp.float32), 2).reshape(1, 128)
    at_word = jnp.stack([samp, cent]).astype(jnp.int32)
    line = join(embeddings, *[fetch(embeddings, 0, step) for step in (1, 2, 3)])
    spot, ids, at_word, line = lax.optimization_barrier((spot, ids, at_word, line))
    near, across, back = [fetch(line, 1, step) for step in (1, 2, 3)]
    first, second = pl.pallas_call(
        halves_kernel,
        out_shape=[jax.ShapeDtypeStruct((512, width), embeddings.dtype)] * 2,
        in_specs=[smem] + [vmem] * 4,
        out_specs=[vmem] * 2,
        compiler_params=small,
        name="halves",
    )(spot, line, near, across, back)
    far_first = fetch(first, 2, 2)
    after_first, before_first = fetch(first, 2, 1), fetch(first, 2, 3)
    after_second, before_second = fetch(second, 2, 1), fetch(second, 2, 3)
    at_word, first, second = lax.optimization_barrier((at_word, first, second))
    mine = pl.pallas_call(
        share_kernel,
        out_shape=jax.ShapeDtypeStruct((share, width), centroids.dtype),
        in_specs=[smem, pl.BlockSpec(memory_space=pltpu.HBM)],
        out_specs=vmem,
        scratch_shapes=[pltpu.SemaphoreType.DMA((8,))],
        compiler_params=small,
        name="share",
    )(at_word, centroids)
    other = swap_cores(mine)
    score = functools.partial(scores_call, mine, other)
    far_second = swap_sides(far_first)
    chunks = [first, second, after_first, after_second, far_first, far_second, before_first, before_second]
    swapped = (5,)
    pairs = [score([chunk]) for chunk in chunks]
    ps = [p[0] for p, _ in pairs]
    stats = [stat for _, stat in pairs]

    local, tops = pl.pallas_call(
        functools.partial(first_kernel, swapped),
        out_shape=(
            jax.ShapeDtypeStruct((64, 8, 640), jnp.float32),
            jax.ShapeDtypeStruct((2, 4096), jnp.float32),
        ),
        in_specs=[smem] + [vmem] * 9,
        compiler_params=small,
        name="first",
    )(spot, ids, *stats)
    chips = [[place(i // 16, i // 4 % 4, i % 4, side) for i in range(64)] for side in range(2)]
    shared = lax.all_to_all(local, BOTH, split_axis=0, concat_axis=0, tiled=True, axis_index_groups=chips)
    whole, lse = pl.pallas_call(
        functools.partial(merge_kernel, swapped),
        out_shape=(
            jax.ShapeDtypeStruct((8, 512), jnp.float32),
            jax.ShapeDtypeStruct((1, 4096), jnp.float32),
        ),
        in_specs=[smem, vmem],
        compiler_params=small,
        name="merge",
    )(spot, shared)
    theirs = sums_call(1, lse, tops, ps, chunks)
    received = swap_cores(theirs)
    whole, shared, _ = lax.optimization_barrier((whole, shared, theirs))
    pack = pl.pallas_call(
        pack_kernel,
        out_shape=jax.ShapeDtypeStruct((64, 128), jnp.float32),
        in_specs=[smem] + [vmem] * 2,
        compiler_params=small,
        name="pack",
    )(at_word, whole, shared)
    partner = swap_cores(pack)
    ours = sums_call(0, lse, tops, ps, chunks)
    row_lse = pl.pallas_call(
        route_kernel,
        out_shape=jax.ShapeDtypeStruct((1, UNIT), jnp.float32),
        in_specs=[smem, vmem, vmem],
        compiler_params=small,
        name="route",
    )(at_word, pack, partner)
    new_centers = pl.pallas_call(
        final_kernel, out_shape=jax.ShapeDtypeStruct((share, width), jnp.float32), name="final",
        compiler_params=pltpu.CompilerParams(vmem_limit_bytes=8 << 20),
    )(ours, received, mine)
    return new_centers, row_lse.reshape(UNIT)


def solution(mesh):
    in_specs = (P(BOTH, None), P(BOTH), P("cent", None))
    out_specs = (P(("cent", "samp"), None), P(BOTH))
    return jax.shard_map(shards, mesh=mesh, in_specs=in_specs, out_specs=out_specs, check_vma=False)
```

```python
import functools
import math

import jax
import jax.numpy as jnp
from jax import lax
from jax.experimental import pallas as pl
from jax.experimental.pallas import tpu as pltpu
from jax.sharding import PartitionSpec as P

inv_temp = 2.5
prior_mass = 0.25
BOTH = ("samp", "cent")
UNIT = 64
X, Y, Z = 0, 1, 2
ORDERS = ((X, Y, Z), (X, Z, Y))


def place(x, y, z, core):
    return ((x // 2) * 4 + z) * 16 + (x % 2) * 8 + y * 2 + core


def fetch(value, stage, offset):
    pairs = []
    for x in range(4):
        for y in range(4):
            for z in range(4):
                for core in range(2):
                    at = [x, y, z]
                    axis = ORDERS[core][stage]
                    at[axis] = (at[axis] + offset) % 4
                    pairs.append((place(*at, core), place(x, y, z, core)))
    return lax.ppermute(value, BOTH, pairs)


def swap_cores(value):
    pairs = [(i, i ^ 1) for i in range(128)]
    return lax.ppermute(value, BOTH, pairs)


def swap_sides(value):
    pairs = []
    for x in range(4):
        for y in range(4):
            for z in range(4):
                for core in range(2):
                    other = (x + (1 if x % 2 == core else 3)) % 4
                    pairs.append((place(other, y, z, core), place(x, y, z, core)))
    return lax.ppermute(value, BOTH, pairs)


def scores_kernel(factor, count, mine_ref, other_ref, *refs):
    rows = refs[:count]
    ps = refs[count : 2 * count]
    stat_ref = refs[2 * count]
    tiles = [(k, part, half) for k in range(count) for part in range(2) for half in range(2)]

    def product(tile):
        k, part, half = tile
        return lax.dot_general(
            (mine_ref, other_ref)[half][...],
            rows[k][part * 256 : (part + 1) * 256, :],
            (((1,), (1,)), ((), ())),
            preferred_element_type=jnp.float32,
        )

    following = product(tiles[0])
    for i, (k, part, half) in enumerate(tiles):
        s = following * factor
        if i + 1 < len(tiles):
            following = product(tiles[i + 1])
        top = jnp.max(s, axis=0, keepdims=True)
        e = jnp.exp2(s - top)
        ps[k][half, :, part * 256 : (part + 1) * 256] = e
        lanes = slice(k * 512 + part * 256, k * 512 + (part + 1) * 256)
        stat_ref[half : half + 1, lanes] = top
        stat_ref[2 + half : 3 + half, lanes] = jnp.sum(e, axis=0, keepdims=True)


def scores_call(mine, other, rows):
    count = len(rows)
    n, width = rows[0].shape
    factor = inv_temp / math.sqrt(width) * math.log2(math.e)
    vmem = pl.BlockSpec(memory_space=pltpu.VMEM)
    *ps, stat = pl.pallas_call(
        functools.partial(scores_kernel, factor, count),
        out_shape=tuple([jax.ShapeDtypeStruct((2, 512, n), jnp.float32)] * count)
        + (jax.ShapeDtypeStruct((4, count * n), jnp.float32),),
        in_specs=[vmem] * (2 + count),
        out_specs=tuple([vmem] * (count + 1)),
        compiler_params=pltpu.CompilerParams(vmem_limit_bytes=12 << 20),
        cost_estimate=pl.CostEstimate(
            flops=4 * 1024 * n * width * count,
            bytes_accessed=count * n * 6144 + (2 << 20),
            transcendentals=1024 * n * count,
        ),
        name="scores",
    )(mine, other, *rows)
    return ps, stat


def roll_within(value, dim, step):
    inner = UNIT * 4**dim
    group = inner * 4
    size = value.shape[1]
    lane = lax.broadcasted_iota(jnp.int32, value.shape, 1) % group
    ahead = pltpu.roll(value, step * inner, 1)
    back = pltpu.roll(value, size - group + step * inner, 1)
    return jnp.where(lane >= step * inner, ahead, back)


def first_kernel(swapped, order, spot_ref, ids_ref, *refs):
    *stats, out_ref, top_ref = refs
    parts = []
    for k, (ref, piece) in enumerate(order):
        lanes = slice(piece * 512, (piece + 1) * 512)
        tops = stats[ref][0:2, lanes]
        top = jnp.max(tops, axis=0, keepdims=True)
        total = jnp.sum(stats[ref][2:4, lanes] * jnp.exp2(tops - top), axis=0, keepdims=True)
        part = top + jnp.log2(total)
        parts.append(roll_within(part, 0, spot_ref[3]) if k in swapped else part)
        top_ref[:, k * 512 : (k + 1) * 512] = tops
    value = jnp.concatenate(parts, axis=1)
    for dim in range(3):
        value = roll_within(value, dim, spot_ref[dim])
    for line in range(8):
        piece = value[:, line * 512 : (line + 1) * 512]
        out_ref[:, line, 0:512] = jnp.broadcast_to(piece, (64, 512))
    lane = lax.broadcasted_iota(jnp.int32, (1, 128), 1)
    ids = jnp.where(lane // UNIT == spot_ref[0] % 2, ids_ref[...], -1.0)
    out_ref[:, :, 512:640] = jnp.broadcast_to(ids.reshape(1, 1, 128), (64, 8, 128))


def merge_kernel(swapped, spot_ref, all_ref, whole_ref, own_ref):
    values = all_ref[:, :, 0:512]
    top = jnp.max(values, axis=0)
    total = jnp.sum(jnp.exp2(values - top[None]), axis=0)
    lse = top + jnp.log2(total)
    whole_ref[...] = lse
    value = jnp.concatenate([lse[line : line + 1, :] for line in range(8)], axis=1)
    for dim in range(3):
        value = roll_within(value, dim, (4 - spot_ref[dim]) % 4)
    own_ref[...] = value
    for k in swapped:
        lanes = slice(k * 512, (k + 1) * 512)
        own_ref[:, lanes] = roll_within(value[:, lanes], 0, 4 - spot_ref[3])


def pack_kernel(at_ref, whole_ref, all_ref, out_ref):
    first_core = at_ref[1] % 2 == 0
    for line in range(32):
        tile = line % 4
        out_ref[line : line + 1, :] = whole_ref[line // 4 : line // 4 + 1, tile * 128 : (tile + 1) * 128]
        low, high = line // 2 % 4, line // 8
        even = jnp.where(first_core, 2 * line, high * 16 + line % 2 * 8 + low)
        odd = jnp.where(first_core, 2 * line + 1, high * 16 + line % 2 * 8 + 4 + low)
        pair = jnp.maximum(all_ref[even, 0:1, 512:640], all_ref[odd, 0:1, 512:640])
        out_ref[32 + line : 33 + line, :] = pair


def route_kernel(at_ref, mine_ref, other_ref, out_ref):
    first = (at_ref[0] * 16 + at_ref[1]) * UNIT
    rows = (lax.broadcasted_iota(jnp.int32, (UNIT, 128), 0) + first).astype(jnp.float32)
    total = jnp.zeros((UNIT, 128), jnp.float32)
    for ref in (mine_ref, other_ref):
        for line in range(32):
            hit = ref[32 + line : 33 + line, :] == rows
            total = total + jnp.where(hit, ref[line : line + 1, :], 0.0)
    out_ref[...] = jnp.sum(total.T, axis=0, keepdims=True) * math.log(2.0)


def join_kernel(*refs):
    *parts, out_ref = refs
    at = 0
    for part in parts:
        out_ref[at : at + part.shape[0], :] = part[...]
        at += part.shape[0]


def halves_kernel(spot_ref, *refs):
    *parts, first_ref, second_ref = refs
    rows = parts[0].shape[0]
    for side in range(2):

        @pl.when(spot_ref[4] == side)
        def _():
            for k, part in enumerate(parts):
                out_ref = (first_ref, second_ref)[(k // 2 + side) % 2]
                out_ref[k % 2 * rows : (k % 2 + 1) * rows, :] = part[...]


def join(*parts):
    vmem = pl.BlockSpec(memory_space=pltpu.VMEM)
    shape = (sum(part.shape[0] for part in parts), parts[0].shape[1])
    return pl.pallas_call(
        join_kernel,
        out_shape=jax.ShapeDtypeStruct(shape, parts[0].dtype),
        in_specs=[vmem] * len(parts),
        out_specs=vmem,
        compiler_params=pltpu.CompilerParams(vmem_limit_bytes=8 << 20),
        name="join",
    )(*parts)


def sums_kernel(half, count, lse_ref, top_ref, *refs):
    ps = refs[:count]
    rows = refs[count : 2 * count]
    out_ref = refs[2 * count]
    n, width = rows[0].shape

    def weights(k):
        lanes = slice(k * n, (k + 1) * n)
        f = jnp.exp2(top_ref[half : half + 1, lanes] - lse_ref[:, lanes])
        w = (ps[k][half] * f).astype(jnp.bfloat16)
        wide = w.astype(jnp.float32)
        return w, sum(wide[:, c : c + 128] for c in range(0, n, 128))

    w, mass = weights(0)
    for k in range(count):
        now = w
        if k + 1 < count:
            w, more = weights(k + 1)
            mass = mass + more
        add = jnp.dot(now, rows[k][...], preferred_element_type=jnp.float32)
        if k == 0:
            out_ref[:, :width] = add
        else:
            out_ref[:, :width] += add
    out_ref[:, width:] = mass


def sums_call(half, lse, tops, ps, rows):
    count = len(rows)
    width = rows[0].shape[1]
    vmem = pl.BlockSpec(memory_space=pltpu.VMEM)
    return pl.pallas_call(
        functools.partial(sums_kernel, half, count),
        out_shape=jax.ShapeDtypeStruct((512, width + 128), jnp.float32),
        in_specs=[vmem] * (2 + 2 * count),
        compiler_params=pltpu.CompilerParams(vmem_limit_bytes=12 << 20),
        cost_estimate=pl.CostEstimate(
            flops=2 * 512 * 4096 * width, bytes_accessed=18 << 20, transcendentals=8192
        ),
        name="sums",
    )(lse, tops, *ps, *rows)


def final_kernel(ours_ref, theirs_ref, mine_ref, out_ref):
    width = out_ref.shape[1]
    mass = jnp.sum(ours_ref[:, width:] + theirs_ref[:, width:], axis=1, keepdims=True) + prior_mass
    total = ours_ref[:, :width] + theirs_ref[:, :width] + prior_mass * mine_ref[...].astype(jnp.float32)
    out_ref[...] = total * (1.0 / mass)


def share_kernel(at_ref, cents_ref, out_ref, sem):
    size = out_ref.shape[0]
    first = pl.multiple_of(at_ref[0] * size, size)
    part = size // 8
    copies = [
        pltpu.make_async_copy(
            cents_ref.at[pl.ds(first + k * part, part)], out_ref.at[pl.ds(k * part, part)], sem.at[k]
        )
        for k in range(8)
    ]
    for copy in copies:
        copy.start()
    for copy in copies:
        copy.wait()


def shards(embeddings, destination, centroids):
    samp, cent = lax.axis_index("samp"), lax.axis_index("cent")
    core = lax.bitwise_and(cent, 1)
    x = lax.shift_right_logical(samp, 2) * 2 + lax.shift_right_logical(cent, 3)
    y, z = lax.bitwise_and(lax.shift_right_logical(cent, 1), 3), lax.bitwise_and(samp, 3)
    side = lax.bitwise_and(x, 1)
    second = lax.bitwise_and(jnp.where(core == 0, y, z) + 2 * side, 3)
    step = jnp.where(side == core, 1, 3)
    spot = jnp.stack([x, second, jnp.where(core == 0, z, y), step, side]).astype(jnp.int32)
    share = centroids.shape[0] // 8
    width = embeddings.shape[1]
    smem = pl.BlockSpec(memory_space=pltpu.SMEM)
    vmem = pl.BlockSpec(memory_space=pltpu.VMEM)
    small = pltpu.CompilerParams(vmem_limit_bytes=8 << 20)
    ids = jnp.tile(destination.astype(jnp.float32), 2).reshape(1, 128)
    at_word = jnp.stack([samp, cent]).astype(jnp.int32)
    line = join(embeddings, *[fetch(embeddings, 0, step) for step in (1, 2, 3)])
    spot, ids, at_word, line = lax.optimization_barrier((spot, ids, at_word, line))
    near, across, back = [fetch(line, 1, step) for step in (1, 2, 3)]
    first, second = pl.pallas_call(
        halves_kernel,
        out_shape=[jax.ShapeDtypeStruct((512, width), embeddings.dtype)] * 2,
        in_specs=[smem] + [vmem] * 4,
        out_specs=[vmem] * 2,
        compiler_params=small,
        name="halves",
    )(spot, line, near, across, back)
    far_first = fetch(first, 2, 2)
    after_first, before_first = fetch(first, 2, 1), fetch(first, 2, 3)
    after_second, before_second = fetch(second, 2, 1), fetch(second, 2, 3)
    at_word, first, second = lax.optimization_barrier((at_word, first, second))
    mine = pl.pallas_call(
        share_kernel,
        out_shape=jax.ShapeDtypeStruct((share, width), centroids.dtype),
        in_specs=[smem, pl.BlockSpec(memory_space=pltpu.HBM)],
        out_specs=vmem,
        scratch_shapes=[pltpu.SemaphoreType.DMA((8,))],
        compiler_params=small,
        name="share",
    )(at_word, centroids)
    other = swap_cores(mine)
    score = functools.partial(scores_call, mine, other)
    far_second = swap_sides(far_first)
    chunks = [first, second, after_first, after_second, far_first, far_second, before_first, before_second]
    swapped = (5,)
    early_ps, early_stat = score([far_first, first, second])
    chunks[3], _ = lax.optimization_barrier((chunks[3], early_stat))
    calls = {k: score([chunks[k]]) for k in (2, 3, 5, 6, 7)}
    ps = early_ps[1:] + [calls[2][0][0], calls[3][0][0], early_ps[0]] + [calls[k][0][0] for k in (5, 6, 7)]
    stats = [early_stat] + [calls[k][1] for k in (2, 3, 5, 6, 7)]
    order = ((0, 1), (0, 2), (1, 0), (2, 0), (0, 0), (3, 0), (4, 0), (5, 0))

    local, tops = pl.pallas_call(
        functools.partial(first_kernel, swapped, order),
        out_shape=(
            jax.ShapeDtypeStruct((64, 8, 640), jnp.float32),
            jax.ShapeDtypeStruct((2, 4096), jnp.float32),
        ),
        in_specs=[smem] + [vmem] * 7,
        compiler_params=small,
        name="first",
    )(spot, ids, *stats)
    chips = [
        [place(i % 4, i // 4 % 4, i // 16, 0) for i in range(64)],
        [place(i // 4 % 4, i // 16, i % 4, 1) for i in range(64)],
    ]
    shared = lax.all_to_all(local, BOTH, split_axis=0, concat_axis=0, tiled=True, axis_index_groups=chips)
    whole, lse = pl.pallas_call(
        functools.partial(merge_kernel, swapped),
        out_shape=(
            jax.ShapeDtypeStruct((8, 512), jnp.float32),
            jax.ShapeDtypeStruct((1, 4096), jnp.float32),
        ),
        in_specs=[smem, vmem],
        compiler_params=small,
        name="merge",
    )(spot, shared)
    theirs = sums_call(1, lse, tops, ps, chunks)
    received = swap_cores(theirs)
    whole, shared, _ = lax.optimization_barrier((whole, shared, theirs))
    pack = pl.pallas_call(
        pack_kernel,
        out_shape=jax.ShapeDtypeStruct((64, 128), jnp.float32),
        in_specs=[smem] + [vmem] * 2,
        compiler_params=small,
        name="pack",
    )(at_word, whole, shared)
    partner = swap_cores(pack)
    ours = sums_call(0, lse, tops, ps, chunks)
    row_lse = pl.pallas_call(
        route_kernel,
        out_shape=jax.ShapeDtypeStruct((1, UNIT), jnp.float32),
        in_specs=[smem, vmem, vmem],
        compiler_params=small,
        name="route",
    )(at_word, pack, partner)
    new_centers = pl.pallas_call(
        final_kernel, out_shape=jax.ShapeDtypeStruct((share, width), jnp.float32), name="final",
        compiler_params=pltpu.CompilerParams(vmem_limit_bytes=8 << 20),
    )(ours, received, mine)
    return new_centers, row_lse.reshape(UNIT)


def solution(mesh):
    in_specs = (P(BOTH, None), P(BOTH), P("cent", None))
    out_specs = (P(("cent", "samp"), None), P(BOTH))
    return jax.shard_map(shards, mesh=mesh, in_specs=in_specs, out_specs=out_specs, check_vma=False)
```

```python
import functools
import math

import jax
import jax.numpy as jnp
from jax import lax
from jax.experimental import pallas as pl
from jax.experimental.pallas import tpu as pltpu
from jax.sharding import PartitionSpec as P

inv_temp = 2.5
prior_mass = 0.25
BOTH = ("samp", "cent")
UNIT = 64
X, Y, Z = 0, 1, 2
ORDERS = ((X, Y, Z), (X, Z, Y))


def place(x, y, z, core):
    return ((x // 2) * 4 + z) * 16 + (x % 2) * 8 + y * 2 + core


def fetch(value, stage, offset):
    pairs = []
    for x in range(4):
        for y in range(4):
            for z in range(4):
                for core in range(2):
                    at = [x, y, z]
                    axis = ORDERS[core][stage]
                    at[axis] = (at[axis] + offset) % 4
                    pairs.append((place(*at, core), place(x, y, z, core)))
    return lax.ppermute(value, BOTH, pairs)


def swap_cores(value):
    pairs = [(i, i ^ 1) for i in range(128)]
    return lax.ppermute(value, BOTH, pairs)


def swap_sides(value):
    pairs = []
    for x in range(4):
        for y in range(4):
            for z in range(4):
                for core in range(2):
                    other = (x + (1 if x % 2 == core else 3)) % 4
                    pairs.append((place(other, y, z, core), place(x, y, z, core)))
    return lax.ppermute(value, BOTH, pairs)


def scores_kernel(factor, count, mine_ref, other_ref, *refs):
    rows = refs[:count]
    ps = refs[count : 2 * count]
    stat_ref = refs[2 * count]
    tiles = [(k, part, half) for k in range(count) for part in range(2) for half in range(2)]

    def product(tile):
        k, part, half = tile
        return lax.dot_general(
            (mine_ref, other_ref)[half][...],
            rows[k][part * 256 : (part + 1) * 256, :],
            (((1,), (1,)), ((), ())),
            preferred_element_type=jnp.float32,
        )

    following = product(tiles[0])
    for i, (k, part, half) in enumerate(tiles):
        s = following * factor
        if i + 1 < len(tiles):
            following = product(tiles[i + 1])
        top = jnp.max(s, axis=0, keepdims=True)
        e = jnp.exp2(s - top)
        ps[k][half, :, part * 256 : (part + 1) * 256] = e
        lanes = slice(k * 512 + part * 256, k * 512 + (part + 1) * 256)
        stat_ref[half : half + 1, lanes] = top
        stat_ref[2 + half : 3 + half, lanes] = jnp.sum(e, axis=0, keepdims=True)


def scores_call(mine, other, rows):
    count = len(rows)
    n, width = rows[0].shape
    factor = inv_temp / math.sqrt(width) * math.log2(math.e)
    vmem = pl.BlockSpec(memory_space=pltpu.VMEM)
    *ps, stat = pl.pallas_call(
        functools.partial(scores_kernel, factor, count),
        out_shape=tuple([jax.ShapeDtypeStruct((2, 512, n), jnp.float32)] * count)
        + (jax.ShapeDtypeStruct((4, count * n), jnp.float32),),
        in_specs=[vmem] * (2 + count),
        out_specs=tuple([vmem] * (count + 1)),
        compiler_params=pltpu.CompilerParams(vmem_limit_bytes=12 << 20),
        cost_estimate=pl.CostEstimate(
            flops=4 * 1024 * n * width * count,
            bytes_accessed=count * n * 6144 + (2 << 20),
            transcendentals=1024 * n * count,
        ),
        name="scores",
    )(mine, other, *rows)
    return ps, stat


def roll_within(value, dim, step):
    inner = UNIT * 4**dim
    group = inner * 4
    size = value.shape[1]
    lane = lax.broadcasted_iota(jnp.int32, value.shape, 1) % group
    ahead = pltpu.roll(value, step * inner, 1)
    back = pltpu.roll(value, size - group + step * inner, 1)
    return jnp.where(lane >= step * inner, ahead, back)


def first_kernel(swapped, order, spot_ref, ids_ref, *refs):
    *stats, out_ref, top_ref = refs
    parts = []
    for k, (ref, piece) in enumerate(order):
        lanes = slice(piece * 512, (piece + 1) * 512)
        tops = stats[ref][0:2, lanes]
        top = jnp.max(tops, axis=0, keepdims=True)
        total = jnp.sum(stats[ref][2:4, lanes] * jnp.exp2(tops - top), axis=0, keepdims=True)
        part = top + jnp.log2(total)
        parts.append(roll_within(part, 0, spot_ref[3]) if k in swapped else part)
        top_ref[:, k * 512 : (k + 1) * 512] = tops
    value = jnp.concatenate(parts, axis=1)
    for dim in range(3):
        value = roll_within(value, dim, spot_ref[dim])
    for line in range(8):
        piece = value[:, line * 512 : (line + 1) * 512]
        out_ref[:, line, 0:512] = jnp.broadcast_to(piece, (16, 512))
    lane = lax.broadcasted_iota(jnp.int32, (1, 128), 1)
    ids = jnp.where(lane // UNIT == spot_ref[0] % 2, ids_ref[...], -1.0)
    out_ref[:, :, 512:640] = jnp.broadcast_to(ids.reshape(1, 1, 128), (16, 8, 128))


def combine(values):
    top = functools.reduce(jnp.maximum, values)
    return top + jnp.log2(sum(jnp.exp2(value - top) for value in values))


def plane_kernel(all_ref, out_ref):
    out_ref[:, 0:512] = combine([all_ref[k, :, 0:512] for k in range(16)])
    for line in range(8):
        pair = jnp.maximum(all_ref[2 * line, 0:1, 512:640], all_ref[2 * line + 1, 0:1, 512:640])
        out_ref[line : line + 1, 512:640] = pair


def merge_kernel(swapped, spot_ref, *refs):
    *planes, pack_ref, own_ref = refs
    lse = combine([plane[:, 0:512] for plane in planes])
    value = jnp.concatenate([lse[line : line + 1, :] for line in range(8)], axis=1)
    for tile in range(32):
        pack_ref[tile : tile + 1, :] = value[:, tile * 128 : (tile + 1) * 128]
    for k, plane in enumerate(planes):
        first = pl.multiple_of(32 + (spot_ref[2] + k) % 4 * 8, 8)
        pack_ref[pl.ds(first, 8), :] = plane[:, 512:640]
    for dim in range(3):
        value = roll_within(value, dim, (4 - spot_ref[dim]) % 4)
    own_ref[...] = value
    for k in swapped:
        lanes = slice(k * 512, (k + 1) * 512)
        own_ref[:, lanes] = roll_within(value[:, lanes], 0, 4 - spot_ref[3])


def route_kernel(at_ref, mine_ref, other_ref, out_ref):
    first = (at_ref[0] * 16 + at_ref[1]) * UNIT
    rows = (lax.broadcasted_iota(jnp.int32, (UNIT, 128), 0) + first).astype(jnp.float32)
    total = jnp.zeros((UNIT, 128), jnp.float32)
    for ref in (mine_ref, other_ref):
        for line in range(32):
            hit = ref[32 + line : 33 + line, :] == rows
            total = total + jnp.where(hit, ref[line : line + 1, :], 0.0)
    out_ref[...] = jnp.sum(total.T, axis=0, keepdims=True) * math.log(2.0)


def join_kernel(*refs):
    *parts, out_ref = refs
    at = 0
    for part in parts:
        out_ref[at : at + part.shape[0], :] = part[...]
        at += part.shape[0]


def halves_kernel(spot_ref, *refs):
    *parts, first_ref, second_ref = refs
    rows = parts[0].shape[0]
    for side in range(2):

        @pl.when(spot_ref[4] == side)
        def _():
            for k, part in enumerate(parts):
                out_ref = (first_ref, second_ref)[(k // 2 + side) % 2]
                out_ref[k % 2 * rows : (k % 2 + 1) * rows, :] = part[...]


def join(*parts):
    vmem = pl.BlockSpec(memory_space=pltpu.VMEM)
    shape = (sum(part.shape[0] for part in parts), parts[0].shape[1])
    return pl.pallas_call(
        join_kernel,
        out_shape=jax.ShapeDtypeStruct(shape, parts[0].dtype),
        in_specs=[vmem] * len(parts),
        out_specs=vmem,
        compiler_params=pltpu.CompilerParams(vmem_limit_bytes=8 << 20),
        name="join",
    )(*parts)


def sums_kernel(half, count, lse_ref, top_ref, *refs):
    ps = refs[:count]
    rows = refs[count : 2 * count]
    out_ref = refs[2 * count]
    n, width = rows[0].shape

    def weights(k):
        lanes = slice(k * n, (k + 1) * n)
        f = jnp.exp2(top_ref[half : half + 1, lanes] - lse_ref[:, lanes])
        w = (ps[k][half] * f).astype(jnp.bfloat16)
        wide = w.astype(jnp.float32)
        return w, sum(wide[:, c : c + 128] for c in range(0, n, 128))

    w, mass = weights(0)
    for k in range(count):
        now = w
        if k + 1 < count:
            w, more = weights(k + 1)
            mass = mass + more
        add = jnp.dot(now, rows[k][...], preferred_element_type=jnp.float32)
        if k == 0:
            out_ref[:, :width] = add
        else:
            out_ref[:, :width] += add
    out_ref[:, width:] = mass


def sums_call(half, lse, tops, ps, rows):
    count = len(rows)
    width = rows[0].shape[1]
    vmem = pl.BlockSpec(memory_space=pltpu.VMEM)
    return pl.pallas_call(
        functools.partial(sums_kernel, half, count),
        out_shape=jax.ShapeDtypeStruct((512, width + 128), jnp.float32),
        in_specs=[vmem] * (2 + 2 * count),
        compiler_params=pltpu.CompilerParams(vmem_limit_bytes=12 << 20),
        cost_estimate=pl.CostEstimate(
            flops=2 * 512 * 4096 * width, bytes_accessed=18 << 20, transcendentals=8192
        ),
        name="sums",
    )(lse, tops, *ps, *rows)


def final_kernel(ours_ref, theirs_ref, mine_ref, out_ref):
    width = out_ref.shape[1]
    mass = jnp.sum(ours_ref[:, width:] + theirs_ref[:, width:], axis=1, keepdims=True) + prior_mass
    total = ours_ref[:, :width] + theirs_ref[:, :width] + prior_mass * mine_ref[...].astype(jnp.float32)
    out_ref[...] = total * (1.0 / mass)


def share_kernel(at_ref, cents_ref, out_ref, sem):
    size = out_ref.shape[0]
    first = pl.multiple_of(at_ref[0] * size, size)
    part = size // 8
    copies = [
        pltpu.make_async_copy(
            cents_ref.at[pl.ds(first + k * part, part)], out_ref.at[pl.ds(k * part, part)], sem.at[k]
        )
        for k in range(8)
    ]
    for copy in copies:
        copy.start()
    for copy in copies:
        copy.wait()


def shards(embeddings, destination, centroids):
    samp, cent = lax.axis_index("samp"), lax.axis_index("cent")
    core = lax.bitwise_and(cent, 1)
    x = lax.shift_right_logical(samp, 2) * 2 + lax.shift_right_logical(cent, 3)
    y, z = lax.bitwise_and(lax.shift_right_logical(cent, 1), 3), lax.bitwise_and(samp, 3)
    side = lax.bitwise_and(x, 1)
    second = lax.bitwise_and(jnp.where(core == 0, y, z) + 2 * side, 3)
    step = jnp.where(side == core, 1, 3)
    spot = jnp.stack([x, second, jnp.where(core == 0, z, y), step, side]).astype(jnp.int32)
    share = centroids.shape[0] // 8
    width = embeddings.shape[1]
    smem = pl.BlockSpec(memory_space=pltpu.SMEM)
    vmem = pl.BlockSpec(memory_space=pltpu.VMEM)
    small = pltpu.CompilerParams(vmem_limit_bytes=8 << 20)
    ids = jnp.tile(destination.astype(jnp.float32), 2).reshape(1, 128)
    at_word = jnp.stack([samp, cent]).astype(jnp.int32)
    line = join(embeddings, *[fetch(embeddings, 0, step) for step in (1, 2, 3)])
    spot, ids, at_word, line = lax.optimization_barrier((spot, ids, at_word, line))
    near, across, back = [fetch(line, 1, step) for step in (1, 2, 3)]
    first, second = pl.pallas_call(
        halves_kernel,
        out_shape=[jax.ShapeDtypeStruct((512, width), embeddings.dtype)] * 2,
        in_specs=[smem] + [vmem] * 4,
        out_specs=[vmem] * 2,
        compiler_params=small,
        name="halves",
    )(spot, line, near, across, back)
    far_first = fetch(first, 2, 2)
    after_first, before_first = fetch(first, 2, 1), fetch(first, 2, 3)
    after_second, before_second = fetch(second, 2, 1), fetch(second, 2, 3)
    at_word, first, second = lax.optimization_barrier((at_word, first, second))
    mine = pl.pallas_call(
        share_kernel,
        out_shape=jax.ShapeDtypeStruct((share, width), centroids.dtype),
        in_specs=[smem, pl.BlockSpec(memory_space=pltpu.HBM)],
        out_specs=vmem,
        scratch_shapes=[pltpu.SemaphoreType.DMA((8,))],
        compiler_params=small,
        name="share",
    )(at_word, centroids)
    other = swap_cores(mine)
    score = functools.partial(scores_call, mine, other)
    far_second = swap_sides(far_first)
    chunks = [first, second, after_first, after_second, far_first, far_second, before_first, before_second]
    swapped = (5,)
    early_ps, early_stat = score([far_first, first, second])
    chunks[3], _ = lax.optimization_barrier((chunks[3], early_stat))
    calls = {k: score([chunks[k]]) for k in (2, 3, 5, 6, 7)}
    ps = early_ps[1:] + [calls[2][0][0], calls[3][0][0], early_ps[0]] + [calls[k][0][0] for k in (5, 6, 7)]
    stats = [early_stat] + [calls[k][1] for k in (2, 3, 5, 6, 7)]
    order = ((0, 1), (0, 2), (1, 0), (2, 0), (0, 0), (3, 0), (4, 0), (5, 0))

    local, tops = pl.pallas_call(
        functools.partial(first_kernel, swapped, order),
        out_shape=(
            jax.ShapeDtypeStruct((16, 8, 640), jnp.float32),
            jax.ShapeDtypeStruct((2, 4096), jnp.float32),
        ),
        in_specs=[smem] + [vmem] * 7,
        compiler_params=small,
        name="first",
    )(spot, ids, *stats)
    planes = [[place(i % 4, i // 4, z, 0) for i in range(16)] for z in range(4)]
    planes += [[place(i % 4, y, i // 4, 1) for i in range(16)] for y in range(4)]
    shared = lax.all_to_all(local, BOTH, split_axis=0, concat_axis=0, tiled=True, axis_index_groups=planes)
    plane = pl.pallas_call(
        plane_kernel,
        out_shape=jax.ShapeDtypeStruct((8, 640), jnp.float32),
        in_specs=[vmem],
        out_specs=vmem,
        compiler_params=small,
        name="plane",
    )(shared)
    pack, lse = pl.pallas_call(
        functools.partial(merge_kernel, swapped),
        out_shape=(
            jax.ShapeDtypeStruct((64, 128), jnp.float32),
            jax.ShapeDtypeStruct((1, 4096), jnp.float32),
        ),
        in_specs=[smem] + [vmem] * 4,
        compiler_params=small,
        name="merge",
    )(spot, plane, *[fetch(plane, 2, offset) for offset in (1, 2, 3)])
    theirs = sums_call(1, lse, tops, ps, chunks)
    received = swap_cores(theirs)
    partner = swap_cores(pack)
    ours = sums_call(0, lse, tops, ps, chunks)
    row_lse = pl.pallas_call(
        route_kernel,
        out_shape=jax.ShapeDtypeStruct((1, UNIT), jnp.float32),
        in_specs=[smem, vmem, vmem],
        compiler_params=small,
        name="route",
    )(at_word, pack, partner)
    new_centers = pl.pallas_call(
        final_kernel, out_shape=jax.ShapeDtypeStruct((share, width), jnp.float32), name="final",
        compiler_params=pltpu.CompilerParams(vmem_limit_bytes=8 << 20),
    )(ours, received, mine)
    return new_centers, row_lse.reshape(UNIT)


def solution(mesh):
    in_specs = (P(BOTH, None), P(BOTH), P("cent", None))
    out_specs = (P(("cent", "samp"), None), P(BOTH))
    return jax.shard_map(shards, mesh=mesh, in_specs=in_specs, out_specs=out_specs, check_vma=False)
```

```python
import functools
import math

import jax
import jax.numpy as jnp
from jax import lax
from jax.experimental import pallas as pl
from jax.experimental.pallas import tpu as pltpu
from jax.sharding import PartitionSpec as P

inv_temp = 2.5
prior_mass = 0.25
BOTH = ("samp", "cent")
UNIT = 64
X, Y, Z = 0, 1, 2
ORDERS = ((X, Y, Z), (X, Z, Y))


def place(x, y, z, core):
    return ((x // 2) * 4 + z) * 16 + (x % 2) * 8 + y * 2 + core


def fetch(value, stage, offset):
    pairs = []
    for x in range(4):
        for y in range(4):
            for z in range(4):
                for core in range(2):
                    at = [x, y, z]
                    axis = ORDERS[core][stage]
                    at[axis] = (at[axis] + offset) % 4
                    pairs.append((place(*at, core), place(x, y, z, core)))
    return lax.ppermute(value, BOTH, pairs)


def swap_cores(value):
    pairs = [(i, i ^ 1) for i in range(128)]
    return lax.ppermute(value, BOTH, pairs)


def swap_sides(value):
    pairs = []
    for x in range(4):
        for y in range(4):
            for z in range(4):
                for core in range(2):
                    other = (x + (1 if x % 2 == core else 3)) % 4
                    pairs.append((place(other, y, z, core), place(x, y, z, core)))
    return lax.ppermute(value, BOTH, pairs)


def scores_kernel(factor, count, mine_ref, other_ref, *refs):
    rows = refs[:count]
    ps = refs[count : 2 * count]
    stat_ref = refs[2 * count]
    tiles = [(k, part, half) for k in range(count) for part in range(2) for half in range(2)]

    def product(tile):
        k, part, half = tile
        return lax.dot_general(
            (mine_ref, other_ref)[half][...],
            rows[k][part * 256 : (part + 1) * 256, :],
            (((1,), (1,)), ((), ())),
            preferred_element_type=jnp.float32,
        )

    following = product(tiles[0])
    for i, (k, part, half) in enumerate(tiles):
        s = following * factor
        if i + 1 < len(tiles):
            following = product(tiles[i + 1])
        top = jnp.max(s, axis=0, keepdims=True)
        e = jnp.exp2(s - top)
        ps[k][half, :, part * 256 : (part + 1) * 256] = e
        lanes = slice(k * 512 + part * 256, k * 512 + (part + 1) * 256)
        stat_ref[half : half + 1, lanes] = top
        stat_ref[2 + half : 3 + half, lanes] = jnp.sum(e, axis=0, keepdims=True)


def scores_call(mine, other, rows):
    count = len(rows)
    n, width = rows[0].shape
    factor = inv_temp / math.sqrt(width) * math.log2(math.e)
    vmem = pl.BlockSpec(memory_space=pltpu.VMEM)
    *ps, stat = pl.pallas_call(
        functools.partial(scores_kernel, factor, count),
        out_shape=tuple([jax.ShapeDtypeStruct((2, 512, n), jnp.float32)] * count)
        + (jax.ShapeDtypeStruct((4, count * n), jnp.float32),),
        in_specs=[vmem] * (2 + count),
        out_specs=tuple([vmem] * (count + 1)),
        compiler_params=pltpu.CompilerParams(vmem_limit_bytes=12 << 20),
        cost_estimate=pl.CostEstimate(
            flops=4 * 1024 * n * width * count,
            bytes_accessed=count * n * 6144 + (2 << 20),
            transcendentals=1024 * n * count,
        ),
        name="scores",
    )(mine, other, *rows)
    return ps, stat


def roll_within(value, dim, step):
    inner = UNIT * 4**dim
    group = inner * 4
    size = value.shape[1]
    lane = lax.broadcasted_iota(jnp.int32, value.shape, 1) % group
    ahead = pltpu.roll(value, step * inner, 1)
    back = pltpu.roll(value, size - group + step * inner, 1)
    return jnp.where(lane >= step * inner, ahead, back)


def first_kernel(swapped, order, spot_ref, ids_ref, *refs):
    *stats, out_ref, top_ref = refs
    parts = []
    for k, (ref, piece) in enumerate(order):
        lanes = slice(piece * 512, (piece + 1) * 512)
        tops = stats[ref][0:2, lanes]
        top = jnp.max(tops, axis=0, keepdims=True)
        total = jnp.sum(stats[ref][2:4, lanes] * jnp.exp2(tops - top), axis=0, keepdims=True)
        part = top + jnp.log2(total)
        parts.append(roll_within(part, 0, spot_ref[3]) if k in swapped else part)
        top_ref[:, k * 512 : (k + 1) * 512] = tops
    value = jnp.concatenate(parts, axis=1)
    for dim in range(3):
        value = roll_within(value, dim, spot_ref[dim])
    for line in range(8):
        piece = value[:, line * 512 : (line + 1) * 512]
        out_ref[:, line, 0:512] = jnp.broadcast_to(piece, (16, 512))
    lane = lax.broadcasted_iota(jnp.int32, (1, 128), 1)
    ids = jnp.where(lane // UNIT == spot_ref[0] % 2, ids_ref[...], -1.0)
    out_ref[:, :, 512:640] = jnp.broadcast_to(ids.reshape(1, 1, 128), (16, 8, 128))


def combine(values):
    top = functools.reduce(jnp.maximum, values)
    return top + jnp.log2(sum(jnp.exp2(value - top) for value in values))


def plane_kernel(all_ref, out_ref):
    out_ref[:, 0:512] = combine([all_ref[k, :, 0:512] for k in range(16)])
    for line in range(8):
        pair = jnp.maximum(all_ref[2 * line, 0:1, 512:640], all_ref[2 * line + 1, 0:1, 512:640])
        out_ref[line : line + 1, 512:640] = pair


def merge_kernel(swapped, spot_ref, *refs):
    *planes, pack_ref, own_ref = refs
    lse = combine([plane[:, 0:512] for plane in planes])
    value = jnp.concatenate([lse[line : line + 1, :] for line in range(8)], axis=1)
    for tile in range(32):
        pack_ref[tile : tile + 1, :] = value[:, tile * 128 : (tile + 1) * 128]
    for k, plane in enumerate(planes):
        first = pl.multiple_of(32 + (spot_ref[2] + k) % 4 * 8, 8)
        pack_ref[pl.ds(first, 8), :] = plane[:, 512:640]
    for dim in range(3):
        value = roll_within(value, dim, (4 - spot_ref[dim]) % 4)
    own_ref[...] = value
    for k in swapped:
        lanes = slice(k * 512, (k + 1) * 512)
        own_ref[:, lanes] = roll_within(value[:, lanes], 0, 4 - spot_ref[3])


def route_kernel(at_ref, mine_ref, other_ref, out_ref):
    first = (at_ref[0] * 16 + at_ref[1]) * UNIT
    rows = (lax.broadcasted_iota(jnp.int32, (UNIT, 128), 0) + first).astype(jnp.float32)
    total = jnp.zeros((UNIT, 128), jnp.float32)
    for ref in (mine_ref, other_ref):
        for line in range(32):
            hit = ref[32 + line : 33 + line, :] == rows
            total = total + jnp.where(hit, ref[line : line + 1, :], 0.0)
    out_ref[...] = jnp.sum(total.T, axis=0, keepdims=True) * math.log(2.0)


def join_kernel(*refs):
    *parts, out_ref = refs
    at = 0
    for part in parts:
        out_ref[at : at + part.shape[0], :] = part[...]
        at += part.shape[0]


def halves_kernel(spot_ref, *refs):
    *parts, first_ref, second_ref = refs
    rows = parts[0].shape[0]
    for side in range(2):

        @pl.when(spot_ref[4] == side)
        def _():
            for k, part in enumerate(parts):
                out_ref = (first_ref, second_ref)[(k // 2 + side) % 2]
                out_ref[k % 2 * rows : (k % 2 + 1) * rows, :] = part[...]


def join(*parts):
    vmem = pl.BlockSpec(memory_space=pltpu.VMEM)
    shape = (sum(part.shape[0] for part in parts), parts[0].shape[1])
    return pl.pallas_call(
        join_kernel,
        out_shape=jax.ShapeDtypeStruct(shape, parts[0].dtype),
        in_specs=[vmem] * len(parts),
        out_specs=vmem,
        compiler_params=pltpu.CompilerParams(vmem_limit_bytes=8 << 20),
        name="join",
    )(*parts)


def sums_kernel(half, count, lse_ref, top_ref, *refs):
    ps = refs[:count]
    rows = refs[count : 2 * count]
    out_ref = refs[2 * count]
    n, width = rows[0].shape

    def weights(k):
        lanes = slice(k * n, (k + 1) * n)
        f = jnp.exp2(top_ref[half : half + 1, lanes] - lse_ref[:, lanes])
        w = (ps[k][half] * f).astype(jnp.bfloat16)
        wide = w.astype(jnp.float32)
        return w, sum(wide[:, c : c + 128] for c in range(0, n, 128))

    w, mass = weights(0)
    for k in range(count):
        now = w
        if k + 1 < count:
            w, more = weights(k + 1)
            mass = mass + more
        add = jnp.dot(now, rows[k][...], preferred_element_type=jnp.float32)
        if k == 0:
            out_ref[:, :width] = add
        else:
            out_ref[:, :width] += add
    out_ref[:, width:] = mass


def sums_call(half, lse, tops, ps, rows):
    count = len(rows)
    width = rows[0].shape[1]
    vmem = pl.BlockSpec(memory_space=pltpu.VMEM)
    return pl.pallas_call(
        functools.partial(sums_kernel, half, count),
        out_shape=jax.ShapeDtypeStruct((512, width + 128), jnp.float32),
        in_specs=[vmem] * (2 + 2 * count),
        compiler_params=pltpu.CompilerParams(vmem_limit_bytes=12 << 20),
        cost_estimate=pl.CostEstimate(
            flops=2 * 512 * 4096 * width, bytes_accessed=18 << 20, transcendentals=8192
        ),
        name="sums",
    )(lse, tops, *ps, *rows)


def final_kernel(ours_ref, theirs_ref, mine_ref, out_ref):
    width = out_ref.shape[1]
    mass = jnp.sum(ours_ref[:, width:] + theirs_ref[:, width:], axis=1, keepdims=True) + prior_mass
    total = ours_ref[:, :width] + theirs_ref[:, :width] + prior_mass * mine_ref[...].astype(jnp.float32)
    out_ref[...] = total * (1.0 / mass)


def share_kernel(at_ref, cents_ref, out_ref, sem):
    size = out_ref.shape[0]
    first = pl.multiple_of(at_ref[0] * size, size)
    part = size // 8
    copies = [
        pltpu.make_async_copy(
            cents_ref.at[pl.ds(first + k * part, part)], out_ref.at[pl.ds(k * part, part)], sem.at[k]
        )
        for k in range(8)
    ]
    for copy in copies:
        copy.start()
    for copy in copies:
        copy.wait()


def shards(embeddings, destination, centroids):
    samp, cent = lax.axis_index("samp"), lax.axis_index("cent")
    core = lax.bitwise_and(cent, 1)
    x = lax.shift_right_logical(samp, 2) * 2 + lax.shift_right_logical(cent, 3)
    y, z = lax.bitwise_and(lax.shift_right_logical(cent, 1), 3), lax.bitwise_and(samp, 3)
    side = lax.bitwise_and(x, 1)
    second = lax.bitwise_and(jnp.where(core == 0, y, z) + 2 * side, 3)
    step = jnp.where(side == core, 1, 3)
    spot = jnp.stack([x, second, jnp.where(core == 0, z, y), step, side]).astype(jnp.int32)
    share = centroids.shape[0] // 8
    width = embeddings.shape[1]
    smem = pl.BlockSpec(memory_space=pltpu.SMEM)
    vmem = pl.BlockSpec(memory_space=pltpu.VMEM)
    small = pltpu.CompilerParams(vmem_limit_bytes=8 << 20)
    ids = jnp.tile(destination.astype(jnp.float32), 2).reshape(1, 128)
    at_word = jnp.stack([samp, cent]).astype(jnp.int32)
    line = join(embeddings, *[fetch(embeddings, 0, step) for step in (1, 2, 3)])
    spot, ids, at_word, line = lax.optimization_barrier((spot, ids, at_word, line))
    near, across, back = [fetch(line, 1, step) for step in (1, 2, 3)]
    first, second = pl.pallas_call(
        halves_kernel,
        out_shape=[jax.ShapeDtypeStruct((512, width), embeddings.dtype)] * 2,
        in_specs=[smem] + [vmem] * 4,
        out_specs=[vmem] * 2,
        compiler_params=small,
        name="halves",
    )(spot, line, near, across, back)
    far_first = fetch(first, 2, 2)
    after_first, before_first = fetch(first, 2, 1), fetch(first, 2, 3)
    after_second, before_second = fetch(second, 2, 1), fetch(second, 2, 3)
    at_word, first, second = lax.optimization_barrier((at_word, first, second))
    mine = pl.pallas_call(
        share_kernel,
        out_shape=jax.ShapeDtypeStruct((share, width), centroids.dtype),
        in_specs=[smem, pl.BlockSpec(memory_space=pltpu.HBM)],
        out_specs=vmem,
        scratch_shapes=[pltpu.SemaphoreType.DMA((8,))],
        compiler_params=small,
        name="share",
    )(at_word, centroids)
    other = swap_cores(mine)
    score = functools.partial(scores_call, mine, other)
    far_second = swap_sides(far_first)
    chunks = [first, second, after_first, after_second, far_first, far_second, before_first, before_second]
    swapped = (5,)
    early_ps, early_stat = score([far_first, first, second])
    calls, last = {}, early_stat
    for k in (3, 6, 5, 7, 2):
        chunks[k], _ = lax.optimization_barrier((chunks[k], last))
        calls[k] = score([chunks[k]])
        last = calls[k][1]
    ps = early_ps[1:] + [calls[2][0][0], calls[3][0][0], early_ps[0]] + [calls[k][0][0] for k in (5, 6, 7)]
    stats = [early_stat] + [calls[k][1] for k in (2, 3, 5, 6, 7)]
    order = ((0, 1), (0, 2), (1, 0), (2, 0), (0, 0), (3, 0), (4, 0), (5, 0))

    local, tops = pl.pallas_call(
        functools.partial(first_kernel, swapped, order),
        out_shape=(
            jax.ShapeDtypeStruct((16, 8, 640), jnp.float32),
            jax.ShapeDtypeStruct((2, 4096), jnp.float32),
        ),
        in_specs=[smem] + [vmem] * 7,
        compiler_params=small,
        name="first",
    )(spot, ids, *stats)
    planes = [[place(i % 4, i // 4, z, 0) for i in range(16)] for z in range(4)]
    planes += [[place(i % 4, y, i // 4, 1) for i in range(16)] for y in range(4)]
    shared = lax.all_to_all(local, BOTH, split_axis=0, concat_axis=0, tiled=True, axis_index_groups=planes)
    plane = pl.pallas_call(
        plane_kernel,
        out_shape=jax.ShapeDtypeStruct((8, 640), jnp.float32),
        in_specs=[vmem],
        out_specs=vmem,
        compiler_params=small,
        name="plane",
    )(shared)
    pack, lse = pl.pallas_call(
        functools.partial(merge_kernel, swapped),
        out_shape=(
            jax.ShapeDtypeStruct((64, 128), jnp.float32),
            jax.ShapeDtypeStruct((1, 4096), jnp.float32),
        ),
        in_specs=[smem] + [vmem] * 4,
        compiler_params=small,
        name="merge",
    )(spot, plane, *[fetch(plane, 2, offset) for offset in (1, 2, 3)])
    theirs = sums_call(1, lse, tops, ps, chunks)
    received = swap_cores(theirs)
    partner = swap_cores(pack)
    ours = sums_call(0, lse, tops, ps, chunks)
    row_lse = pl.pallas_call(
        route_kernel,
        out_shape=jax.ShapeDtypeStruct((1, UNIT), jnp.float32),
        in_specs=[smem, vmem, vmem],
        compiler_params=small,
        name="route",
    )(at_word, pack, partner)
    new_centers = pl.pallas_call(
        final_kernel, out_shape=jax.ShapeDtypeStruct((share, width), jnp.float32), name="final",
        compiler_params=pltpu.CompilerParams(vmem_limit_bytes=8 << 20),
    )(ours, received, mine)
    return new_centers, row_lse.reshape(UNIT)


def solution(mesh):
    in_specs = (P(BOTH, None), P(BOTH), P("cent", None))
    out_specs = (P(("cent", "samp"), None), P(BOTH))
    return jax.shard_map(shards, mesh=mesh, in_specs=in_specs, out_specs=out_specs, check_vma=False)
```

```python
import functools
import math

import jax
import jax.numpy as jnp
from jax import lax
from jax.experimental import pallas as pl
from jax.experimental.pallas import tpu as pltpu
from jax.sharding import PartitionSpec as P

inv_temp = 2.5
prior_mass = 0.25
BOTH = ("samp", "cent")
UNIT = 64
X, Y, Z = 0, 1, 2
ORDERS = ((X, Y, Z), (X, Z, Y))


def place(x, y, z, core):
    return ((x // 2) * 4 + z) * 16 + (x % 2) * 8 + y * 2 + core


def fetch(value, stage, offset):
    pairs = []
    for x in range(4):
        for y in range(4):
            for z in range(4):
                for core in range(2):
                    at = [x, y, z]
                    axis = ORDERS[core][stage]
                    at[axis] = (at[axis] + offset) % 4
                    pairs.append((place(*at, core), place(x, y, z, core)))
    return lax.ppermute(value, BOTH, pairs)


def swap_cores(value):
    pairs = [(i, i ^ 1) for i in range(128)]
    return lax.ppermute(value, BOTH, pairs)


def swap_sides(value):
    pairs = []
    for x in range(4):
        for y in range(4):
            for z in range(4):
                for core in range(2):
                    other = (x + (1 if x % 2 == core else 3)) % 4
                    pairs.append((place(other, y, z, core), place(x, y, z, core)))
    return lax.ppermute(value, BOTH, pairs)


def scores_kernel(factor, count, mine_ref, other_ref, *refs):
    rows = refs[:count]
    ps = refs[count : 2 * count]
    stat_ref = refs[2 * count]
    tiles = [(k, part, half) for k in range(count) for part in range(2) for half in range(2)]

    def product(tile):
        k, part, half = tile
        return lax.dot_general(
            (mine_ref, other_ref)[half][...],
            rows[k][part * 256 : (part + 1) * 256, :],
            (((1,), (1,)), ((), ())),
            preferred_element_type=jnp.float32,
        )

    following = product(tiles[0])
    for i, (k, part, half) in enumerate(tiles):
        s = following * factor
        if i + 1 < len(tiles):
            following = product(tiles[i + 1])
        top = jnp.max(s, axis=0, keepdims=True)
        e = jnp.exp2(s - top)
        ps[k][half, :, part * 256 : (part + 1) * 256] = e
        lanes = slice(k * 512 + part * 256, k * 512 + (part + 1) * 256)
        stat_ref[half : half + 1, lanes] = top
        stat_ref[2 + half : 3 + half, lanes] = jnp.sum(e, axis=0, keepdims=True)


def scores_call(mine, other, rows):
    count = len(rows)
    n, width = rows[0].shape
    factor = inv_temp / math.sqrt(width) * math.log2(math.e)
    vmem = pl.BlockSpec(memory_space=pltpu.VMEM)
    *ps, stat = pl.pallas_call(
        functools.partial(scores_kernel, factor, count),
        out_shape=tuple([jax.ShapeDtypeStruct((2, 512, n), jnp.float32)] * count)
        + (jax.ShapeDtypeStruct((4, count * n), jnp.float32),),
        in_specs=[vmem] * (2 + count),
        out_specs=tuple([vmem] * (count + 1)),
        compiler_params=pltpu.CompilerParams(vmem_limit_bytes=12 << 20),
        cost_estimate=pl.CostEstimate(
            flops=4 * 1024 * n * width * count,
            bytes_accessed=count * n * 6144 + (2 << 20),
            transcendentals=1024 * n * count,
        ),
        name="scores",
    )(mine, other, *rows)
    return ps, stat


def roll_within(value, dim, step):
    inner = UNIT * 4**dim
    group = inner * 4
    size = value.shape[1]
    lane = lax.broadcasted_iota(jnp.int32, value.shape, 1) % group
    ahead = pltpu.roll(value, step * inner, 1)
    back = pltpu.roll(value, size - group + step * inner, 1)
    return jnp.where(lane >= step * inner, ahead, back)


def first_kernel(swapped, order, spot_ref, ids_ref, *refs):
    *stats, out_ref, top_ref = refs
    parts = []
    for k, (ref, piece) in enumerate(order):
        lanes = slice(piece * 512, (piece + 1) * 512)
        tops = stats[ref][0:2, lanes]
        top = jnp.max(tops, axis=0, keepdims=True)
        total = jnp.sum(stats[ref][2:4, lanes] * jnp.exp2(tops - top), axis=0, keepdims=True)
        part = top + jnp.log2(total)
        parts.append(roll_within(part, 0, spot_ref[3]) if k in swapped else part)
        top_ref[:, k * 512 : (k + 1) * 512] = tops
    value = jnp.concatenate(parts, axis=1)
    for dim in range(3):
        value = roll_within(value, dim, spot_ref[dim])
    for line in range(8):
        piece = value[:, line * 512 : (line + 1) * 512]
        out_ref[:, line, 0:512] = jnp.broadcast_to(piece, (16, 512))
    lane = lax.broadcasted_iota(jnp.int32, (1, 128), 1)
    ids = jnp.where(lane // UNIT == spot_ref[0] % 2, ids_ref[...], -1.0)
    out_ref[:, :, 512:640] = jnp.broadcast_to(ids.reshape(1, 1, 128), (16, 8, 128))


def combine(values):
    top = functools.reduce(jnp.maximum, values)
    return top + jnp.log2(sum(jnp.exp2(value - top) for value in values))


def plane_kernel(all_ref, out_ref):
    out_ref[:, 0:512] = combine([all_ref[k, :, 0:512] for k in range(16)])
    for line in range(8):
        pair = jnp.maximum(all_ref[2 * line, 0:1, 512:640], all_ref[2 * line + 1, 0:1, 512:640])
        out_ref[line : line + 1, 512:640] = pair


def merge_kernel(swapped, spot_ref, *refs):
    *planes, pack_ref, own_ref = refs
    lse = combine([plane[:, 0:512] for plane in planes])
    value = jnp.concatenate([lse[line : line + 1, :] for line in range(8)], axis=1)
    for tile in range(32):
        pack_ref[tile : tile + 1, :] = value[:, tile * 128 : (tile + 1) * 128]
    for k, plane in enumerate(planes):
        first = pl.multiple_of(32 + (spot_ref[2] + k) % 4 * 8, 8)
        pack_ref[pl.ds(first, 8), :] = plane[:, 512:640]
    for dim in range(3):
        value = roll_within(value, dim, (4 - spot_ref[dim]) % 4)
    own_ref[...] = value
    for k in swapped:
        lanes = slice(k * 512, (k + 1) * 512)
        own_ref[:, lanes] = roll_within(value[:, lanes], 0, 4 - spot_ref[3])


def route_kernel(at_ref, mine_ref, other_ref, out_ref):
    first = (at_ref[0] * 16 + at_ref[1]) * UNIT
    rows = (lax.broadcasted_iota(jnp.int32, (UNIT, 128), 0) + first).astype(jnp.float32)
    totals = [jnp.zeros((UNIT, 128), jnp.float32)] * 4
    for ref in (mine_ref, other_ref):
        for line in range(32):
            hit = ref[32 + line : 33 + line, :] == rows
            totals[line % 4] = totals[line % 4] + jnp.where(hit, ref[line : line + 1, :], 0.0)
    total = (totals[0] + totals[1]) + (totals[2] + totals[3])
    out_ref[...] = jnp.sum(total.T, axis=0, keepdims=True) * math.log(2.0)


def join_kernel(*refs):
    *parts, out_ref = refs
    at = 0
    for part in parts:
        out_ref[at : at + part.shape[0], :] = part[...]
        at += part.shape[0]


def halves_kernel(spot_ref, *refs):
    *parts, first_ref, second_ref = refs
    rows = parts[0].shape[0]
    for side in range(2):

        @pl.when(spot_ref[4] == side)
        def _():
            for k, part in enumerate(parts):
                out_ref = (first_ref, second_ref)[(k // 2 + side) % 2]
                out_ref[k % 2 * rows : (k % 2 + 1) * rows, :] = part[...]


def join(*parts):
    vmem = pl.BlockSpec(memory_space=pltpu.VMEM)
    shape = (sum(part.shape[0] for part in parts), parts[0].shape[1])
    return pl.pallas_call(
        join_kernel,
        out_shape=jax.ShapeDtypeStruct(shape, parts[0].dtype),
        in_specs=[vmem] * len(parts),
        out_specs=vmem,
        compiler_params=pltpu.CompilerParams(vmem_limit_bytes=8 << 20),
        name="join",
    )(*parts)


def sums_kernel(half, count, lse_ref, top_ref, *refs):
    ps = refs[:count]
    rows = refs[count : 2 * count]
    out_ref = refs[2 * count]
    n, width = rows[0].shape

    def weights(k):
        lanes = slice(k * n, (k + 1) * n)
        f = jnp.exp2(top_ref[half : half + 1, lanes] - lse_ref[:, lanes])
        w = (ps[k][half] * f).astype(jnp.bfloat16)
        wide = w.astype(jnp.float32)
        return w, sum(wide[:, c : c + 128] for c in range(0, n, 128))

    w, mass = weights(0)
    for k in range(count):
        now = w
        if k + 1 < count:
            w, more = weights(k + 1)
            mass = mass + more
        add = jnp.dot(now, rows[k][...], preferred_element_type=jnp.float32)
        if k == 0:
            out_ref[:, :width] = add
        else:
            out_ref[:, :width] += add
    out_ref[:, width:] = mass


def sums_call(half, lse, tops, ps, rows):
    count = len(rows)
    width = rows[0].shape[1]
    vmem = pl.BlockSpec(memory_space=pltpu.VMEM)
    return pl.pallas_call(
        functools.partial(sums_kernel, half, count),
        out_shape=jax.ShapeDtypeStruct((512, width + 128), jnp.float32),
        in_specs=[vmem] * (2 + 2 * count),
        compiler_params=pltpu.CompilerParams(vmem_limit_bytes=12 << 20),
        cost_estimate=pl.CostEstimate(
            flops=2 * 512 * 512 * count * width, bytes_accessed=18 << 20, transcendentals=8192
        ),
        name="sums",
    )(lse, tops, *ps, *rows)


def final_kernel(skip, count, lse_ref, top_ref, ours_ref, theirs_ref, mine_ref, *refs):
    ps = refs[:count]
    rows = refs[count : 2 * count]
    out_ref, buf, sems = refs[2 * count :]
    n, width = rows[0].shape
    mass = ours_ref[:, width:] + theirs_ref[:, width:]
    ws = []
    for k in range(count):
        lanes = slice((skip + k) * n, (skip + k + 1) * n)
        f = jnp.exp2(top_ref[0:1, lanes] - lse_ref[:, lanes])
        w = (ps[k][0] * f).astype(jnp.bfloat16)
        wide = w.astype(jnp.float32)
        mass = mass + sum(wide[:, c : c + 128] for c in range(0, n, 128))
        ws.append(w)
    inverse = 1.0 / (jnp.sum(mass, axis=1, keepdims=True) + prior_mass)
    copies = []
    for block in range(4):
        columns = slice(block * width // 4, (block + 1) * width // 4)
        total = ours_ref[:, columns] + theirs_ref[:, columns]
        total = total + prior_mass * mine_ref[:, columns].astype(jnp.float32)
        for k in range(count):
            total = total + jnp.dot(ws[k], rows[k][:, columns], preferred_element_type=jnp.float32)
        buf[:, columns] = total * inverse
        copy = pltpu.make_async_copy(buf.at[:, columns], out_ref.at[:, columns], sems.at[block])
        copy.start()
        copies.append(copy)
    for copy in copies:
        copy.wait()


def share_kernel(at_ref, cents_ref, out_ref, sem):
    size = out_ref.shape[0]
    first = pl.multiple_of(at_ref[0] * size, size)
    part = size // 8
    copies = [
        pltpu.make_async_copy(
            cents_ref.at[pl.ds(first + k * part, part)], out_ref.at[pl.ds(k * part, part)], sem.at[k]
        )
        for k in range(8)
    ]
    for copy in copies:
        copy.start()
    for copy in copies:
        copy.wait()


def shards(embeddings, destination, centroids):
    samp, cent = lax.axis_index("samp"), lax.axis_index("cent")
    core = lax.bitwise_and(cent, 1)
    x = lax.shift_right_logical(samp, 2) * 2 + lax.shift_right_logical(cent, 3)
    y, z = lax.bitwise_and(lax.shift_right_logical(cent, 1), 3), lax.bitwise_and(samp, 3)
    side = lax.bitwise_and(x, 1)
    second = lax.bitwise_and(jnp.where(core == 0, y, z) + 2 * side, 3)
    step = jnp.where(side == core, 1, 3)
    spot = jnp.stack([x, second, jnp.where(core == 0, z, y), step, side]).astype(jnp.int32)
    share = centroids.shape[0] // 8
    width = embeddings.shape[1]
    smem = pl.BlockSpec(memory_space=pltpu.SMEM)
    vmem = pl.BlockSpec(memory_space=pltpu.VMEM)
    small = pltpu.CompilerParams(vmem_limit_bytes=8 << 20)
    ids = jnp.tile(destination.astype(jnp.float32), 2).reshape(1, 128)
    at_word = jnp.stack([samp, cent]).astype(jnp.int32)
    line = join(embeddings, *[fetch(embeddings, 0, step) for step in (1, 2, 3)])
    spot, ids, at_word, line = lax.optimization_barrier((spot, ids, at_word, line))
    near, across, back = [fetch(line, 1, step) for step in (1, 2, 3)]
    first, second = pl.pallas_call(
        halves_kernel,
        out_shape=[jax.ShapeDtypeStruct((512, width), embeddings.dtype)] * 2,
        in_specs=[smem] + [vmem] * 4,
        out_specs=[vmem] * 2,
        compiler_params=small,
        name="halves",
    )(spot, line, near, across, back)
    far_first = fetch(first, 2, 2)
    after_first, before_first = fetch(first, 2, 1), fetch(first, 2, 3)
    after_second, before_second = fetch(second, 2, 1), fetch(second, 2, 3)
    at_word, first, second = lax.optimization_barrier((at_word, first, second))
    mine = pl.pallas_call(
        share_kernel,
        out_shape=jax.ShapeDtypeStruct((share, width), centroids.dtype),
        in_specs=[smem, pl.BlockSpec(memory_space=pltpu.HBM)],
        out_specs=vmem,
        scratch_shapes=[pltpu.SemaphoreType.DMA((8,))],
        compiler_params=small,
        name="share",
    )(at_word, centroids)
    other = swap_cores(mine)
    score = functools.partial(scores_call, mine, other)
    far_second = swap_sides(far_first)
    chunks = [first, second, after_first, after_second, far_first, far_second, before_first, before_second]
    swapped = (5,)
    early_ps, early_stat = score([far_first, first, second])
    calls, last = {}, early_stat
    for k in (3, 6, 5, 7, 2):
        chunks[k], _ = lax.optimization_barrier((chunks[k], last))
        calls[k] = score([chunks[k]])
        last = calls[k][1]
    ps = early_ps[1:] + [calls[2][0][0], calls[3][0][0], early_ps[0]] + [calls[k][0][0] for k in (5, 6, 7)]
    stats = [early_stat] + [calls[k][1] for k in (2, 3, 5, 6, 7)]
    order = ((0, 1), (0, 2), (1, 0), (2, 0), (0, 0), (3, 0), (4, 0), (5, 0))

    local, tops = pl.pallas_call(
        functools.partial(first_kernel, swapped, order),
        out_shape=(
            jax.ShapeDtypeStruct((16, 8, 640), jnp.float32),
            jax.ShapeDtypeStruct((2, 4096), jnp.float32),
        ),
        in_specs=[smem] + [vmem] * 7,
        compiler_params=small,
        name="first",
    )(spot, ids, *stats)
    planes = [[place(i % 4, i // 4, z, 0) for i in range(16)] for z in range(4)]
    planes += [[place(i % 4, y, i // 4, 1) for i in range(16)] for y in range(4)]
    shared = lax.all_to_all(local, BOTH, split_axis=0, concat_axis=0, tiled=True, axis_index_groups=planes)
    plane = pl.pallas_call(
        plane_kernel,
        out_shape=jax.ShapeDtypeStruct((8, 640), jnp.float32),
        in_specs=[vmem],
        out_specs=vmem,
        compiler_params=small,
        name="plane",
    )(shared)
    pack, lse = pl.pallas_call(
        functools.partial(merge_kernel, swapped),
        out_shape=(
            jax.ShapeDtypeStruct((64, 128), jnp.float32),
            jax.ShapeDtypeStruct((1, 4096), jnp.float32),
        ),
        in_specs=[smem] + [vmem] * 4,
        compiler_params=small,
        name="merge",
    )(spot, plane, *[fetch(plane, 2, offset) for offset in (1, 2, 3)])
    theirs = sums_call(1, lse, tops, ps, chunks)
    received = swap_cores(theirs)
    partner = swap_cores(pack)
    ours = sums_call(0, lse, tops, ps[:6], chunks[:6])
    row_lse = pl.pallas_call(
        route_kernel,
        out_shape=jax.ShapeDtypeStruct((1, UNIT), jnp.float32),
        in_specs=[smem, vmem, vmem],
        compiler_params=small,
        name="route",
    )(at_word, pack, partner)
    new_centers = pl.pallas_call(
        functools.partial(final_kernel, 6, 2),
        out_shape=jax.ShapeDtypeStruct((share, width), jnp.float32),
        in_specs=[vmem] * 9,
        out_specs=pl.BlockSpec(memory_space=pl.ANY),
        scratch_shapes=[pltpu.VMEM((share, width), jnp.float32), pltpu.SemaphoreType.DMA((4,))],
        compiler_params=pltpu.CompilerParams(vmem_limit_bytes=12 << 20),
        name="final",
    )(lse, tops, ours, received, mine, *ps[6:], *chunks[6:])
    return new_centers, row_lse.reshape(UNIT)


def solution(mesh):
    in_specs = (P(BOTH, None), P(BOTH), P("cent", None))
    out_specs = (P(("cent", "samp"), None), P(BOTH))
    return jax.shard_map(shards, mesh=mesh, in_specs=in_specs, out_specs=out_specs, check_vma=False)
```

```python
import functools
import math

import jax
import jax.numpy as jnp
from jax import lax
from jax.experimental import pallas as pl
from jax.experimental.pallas import tpu as pltpu
from jax.sharding import PartitionSpec as P

inv_temp = 2.5
prior_mass = 0.25
BOTH = ("samp", "cent")
UNIT = 64
X, Y, Z = 0, 1, 2
ORDERS = ((X, Y, Z), (X, Z, Y))


def place(x, y, z, core):
    return ((x // 2) * 4 + z) * 16 + (x % 2) * 8 + y * 2 + core


def fetch(value, stage, offset):
    pairs = []
    for x in range(4):
        for y in range(4):
            for z in range(4):
                for core in range(2):
                    at = [x, y, z]
                    axis = ORDERS[core][stage]
                    at[axis] = (at[axis] + offset) % 4
                    pairs.append((place(*at, core), place(x, y, z, core)))
    return lax.ppermute(value, BOTH, pairs)


def swap_cores(value):
    pairs = [(i, i ^ 1) for i in range(128)]
    return lax.ppermute(value, BOTH, pairs)


def swap_sides(value):
    pairs = []
    for x in range(4):
        for y in range(4):
            for z in range(4):
                for core in range(2):
                    other = (x + (1 if x % 2 == core else 3)) % 4
                    pairs.append((place(other, y, z, core), place(x, y, z, core)))
    return lax.ppermute(value, BOTH, pairs)


def scores_kernel(factor, count, mine_ref, other_ref, *refs):
    rows = refs[:count]
    ps = refs[count : 2 * count]
    stat_ref = refs[2 * count]
    tiles = [(k, part, half) for k in range(count) for part in range(2) for half in range(2)]

    def product(tile):
        k, part, half = tile
        return lax.dot_general(
            (mine_ref, other_ref)[half][...],
            rows[k][part * 256 : (part + 1) * 256, :],
            (((1,), (1,)), ((), ())),
            preferred_element_type=jnp.float32,
        )

    following = product(tiles[0])
    for i, (k, part, half) in enumerate(tiles):
        s = following * factor
        if i + 1 < len(tiles):
            following = product(tiles[i + 1])
        top = jnp.max(s, axis=0, keepdims=True)
        e = jnp.exp2(s - top)
        ps[k][half, :, part * 256 : (part + 1) * 256] = e
        lanes = slice(k * 512 + part * 256, k * 512 + (part + 1) * 256)
        stat_ref[half : half + 1, lanes] = top
        stat_ref[2 + half : 3 + half, lanes] = jnp.sum(e, axis=0, keepdims=True)


def scores_call(mine, other, rows):
    count = len(rows)
    n, width = rows[0].shape
    factor = inv_temp / math.sqrt(width) * math.log2(math.e)
    vmem = pl.BlockSpec(memory_space=pltpu.VMEM)
    *ps, stat = pl.pallas_call(
        functools.partial(scores_kernel, factor, count),
        out_shape=tuple([jax.ShapeDtypeStruct((2, 512, n), jnp.float32)] * count)
        + (jax.ShapeDtypeStruct((4, count * n), jnp.float32),),
        in_specs=[vmem] * (2 + count),
        out_specs=tuple([vmem] * (count + 1)),
        compiler_params=pltpu.CompilerParams(vmem_limit_bytes=12 << 20),
        cost_estimate=pl.CostEstimate(
            flops=4 * 1024 * n * width * count,
            bytes_accessed=count * n * 6144 + (2 << 20),
            transcendentals=1024 * n * count,
        ),
        name="scores",
    )(mine, other, *rows)
    return ps, stat


def roll_within(value, dim, step):
    inner = UNIT * 4**dim
    group = inner * 4
    size = value.shape[1]
    lane = lax.broadcasted_iota(jnp.int32, value.shape, 1) % group
    ahead = pltpu.roll(value, step * inner, 1)
    back = pltpu.roll(value, size - group + step * inner, 1)
    return jnp.where(lane >= step * inner, ahead, back)


def first_kernel(swapped, order, spot_ref, ids_ref, *refs):
    *stats, out_ref, top_ref = refs
    parts = []
    for k, (ref, piece) in enumerate(order):
        lanes = slice(piece * 512, (piece + 1) * 512)
        tops = stats[ref][0:2, lanes]
        top = jnp.max(tops, axis=0, keepdims=True)
        total = jnp.sum(stats[ref][2:4, lanes] * jnp.exp2(tops - top), axis=0, keepdims=True)
        part = top + jnp.log2(total)
        parts.append(roll_within(part, 0, spot_ref[3]) if k in swapped else part)
        top_ref[:, k * 512 : (k + 1) * 512] = tops
    value = jnp.concatenate(parts, axis=1)
    for dim in range(3):
        value = roll_within(value, dim, spot_ref[dim])
    for line in range(8):
        piece = value[:, line * 512 : (line + 1) * 512]
        out_ref[:, line, 0:512] = jnp.broadcast_to(piece, (16, 512))
    lane = lax.broadcasted_iota(jnp.int32, (1, 128), 1)
    ids = jnp.where(lane // UNIT == spot_ref[0] % 2, ids_ref[...], -1.0)
    out_ref[:, :, 512:640] = jnp.broadcast_to(ids.reshape(1, 1, 128), (16, 8, 128))


def combine(values):
    top = functools.reduce(jnp.maximum, values)
    return top + jnp.log2(sum(jnp.exp2(value - top) for value in values))


def plane_kernel(all_ref, out_ref):
    out_ref[:, 0:512] = combine([all_ref[k, :, 0:512] for k in range(16)])
    for line in range(8):
        pair = jnp.maximum(all_ref[2 * line, 0:1, 512:640], all_ref[2 * line + 1, 0:1, 512:640])
        out_ref[line : line + 1, 512:640] = pair


def merge_kernel(swapped, spot_ref, *refs):
    *planes, pack_ref, own_ref = refs
    lse = combine([plane[:, 0:512] for plane in planes])
    value = jnp.concatenate([lse[line : line + 1, :] for line in range(8)], axis=1)
    for tile in range(32):
        pack_ref[tile : tile + 1, :] = value[:, tile * 128 : (tile + 1) * 128]
    for k, plane in enumerate(planes):
        first = pl.multiple_of(32 + (spot_ref[2] + k) % 4 * 8, 8)
        pack_ref[pl.ds(first, 8), :] = plane[:, 512:640]
    for dim in range(3):
        value = roll_within(value, dim, (4 - spot_ref[dim]) % 4)
    own_ref[...] = value
    for k in swapped:
        lanes = slice(k * 512, (k + 1) * 512)
        own_ref[:, lanes] = roll_within(value[:, lanes], 0, 4 - spot_ref[3])


def join_kernel(*refs):
    *parts, out_ref = refs
    at = 0
    for part in parts:
        out_ref[at : at + part.shape[0], :] = part[...]
        at += part.shape[0]


def halves_kernel(spot_ref, *refs):
    *parts, first_ref, second_ref = refs
    rows = parts[0].shape[0]
    for side in range(2):

        @pl.when(spot_ref[4] == side)
        def _():
            for k, part in enumerate(parts):
                out_ref = (first_ref, second_ref)[(k // 2 + side) % 2]
                out_ref[k % 2 * rows : (k % 2 + 1) * rows, :] = part[...]


def join(*parts):
    vmem = pl.BlockSpec(memory_space=pltpu.VMEM)
    shape = (sum(part.shape[0] for part in parts), parts[0].shape[1])
    return pl.pallas_call(
        join_kernel,
        out_shape=jax.ShapeDtypeStruct(shape, parts[0].dtype),
        in_specs=[vmem] * len(parts),
        out_specs=vmem,
        compiler_params=pltpu.CompilerParams(vmem_limit_bytes=8 << 20),
        name="join",
    )(*parts)


def sums_kernel(half, count, lse_ref, top_ref, *refs):
    ps = refs[:count]
    rows = refs[count : 2 * count]
    out_ref = refs[2 * count]
    n, width = rows[0].shape

    def weights(k):
        lanes = slice(k * n, (k + 1) * n)
        f = jnp.exp2(top_ref[half : half + 1, lanes] - lse_ref[:, lanes])
        w = (ps[k][half] * f).astype(jnp.bfloat16)
        wide = w.astype(jnp.float32)
        return w, sum(wide[:, c : c + 128] for c in range(0, n, 128))

    w, mass = weights(0)
    for k in range(count):
        now = w
        if k + 1 < count:
            w, more = weights(k + 1)
            mass = mass + more
        add = jnp.dot(now, rows[k][...], preferred_element_type=jnp.float32)
        if k == 0:
            out_ref[:, :width] = add
        else:
            out_ref[:, :width] += add
    out_ref[:, width:] = mass


def sums_call(half, lse, tops, ps, rows):
    count = len(rows)
    width = rows[0].shape[1]
    vmem = pl.BlockSpec(memory_space=pltpu.VMEM)
    return pl.pallas_call(
        functools.partial(sums_kernel, half, count),
        out_shape=jax.ShapeDtypeStruct((512, width + 128), jnp.float32),
        in_specs=[vmem] * (2 + 2 * count),
        compiler_params=pltpu.CompilerParams(vmem_limit_bytes=12 << 20),
        cost_estimate=pl.CostEstimate(
            flops=2 * 512 * 512 * count * width, bytes_accessed=18 << 20, transcendentals=8192
        ),
        name="sums",
    )(lse, tops, *ps, *rows)


def final_kernel(skip, count, at_ref, lse_ref, top_ref, ours_ref, theirs_ref, mine_ref, pack_ref, other_ref, *refs):
    ps = refs[:count]
    rows = refs[count : 2 * count]
    out_ref, row_ref, buf, sems = refs[2 * count :]
    n, width = rows[0].shape
    mass = ours_ref[:, width:] + theirs_ref[:, width:]
    ws = []
    for k in range(count):
        lanes = slice((skip + k) * n, (skip + k + 1) * n)
        f = jnp.exp2(top_ref[0:1, lanes] - lse_ref[:, lanes])
        w = (ps[k][0] * f).astype(jnp.bfloat16)
        wide = w.astype(jnp.float32)
        mass = mass + sum(wide[:, c : c + 128] for c in range(0, n, 128))
        ws.append(w)
    inverse = 1.0 / (jnp.sum(mass, axis=1, keepdims=True) + prior_mass)
    base = (at_ref[0] * 16 + at_ref[1]) * UNIT
    logical = (lax.broadcasted_iota(jnp.int32, (UNIT, 128), 0) + base).astype(jnp.float32)
    routed = []
    copies = []
    for block in range(4):
        found = jnp.zeros((UNIT, 128), jnp.float32)
        for line in range(block * 8, block * 8 + 8):
            for ref in (pack_ref, other_ref):
                hit = ref[32 + line : 33 + line, :] == logical
                found = found + jnp.where(hit, ref[line : line + 1, :], 0.0)
        routed.append(found)
        columns = slice(block * width // 4, (block + 1) * width // 4)
        total = ours_ref[:, columns] + theirs_ref[:, columns]
        total = total + prior_mass * mine_ref[:, columns].astype(jnp.float32)
        for k in range(count):
            total = total + jnp.dot(ws[k], rows[k][:, columns], preferred_element_type=jnp.float32)
        buf[:, columns] = total * inverse
        copy = pltpu.make_async_copy(buf.at[:, columns], out_ref.at[:, columns], sems.at[block])
        copy.start()
        copies.append(copy)
    found = (routed[0] + routed[1]) + (routed[2] + routed[3])
    row_ref[...] = jnp.sum(found.T, axis=0, keepdims=True) * math.log(2.0)
    for copy in copies:
        copy.wait()


def share_kernel(at_ref, cents_ref, out_ref, sem):
    size = out_ref.shape[0]
    first = pl.multiple_of(at_ref[0] * size, size)
    part = size // 8
    copies = [
        pltpu.make_async_copy(
            cents_ref.at[pl.ds(first + k * part, part)], out_ref.at[pl.ds(k * part, part)], sem.at[k]
        )
        for k in range(8)
    ]
    for copy in copies:
        copy.start()
    for copy in copies:
        copy.wait()


def shards(embeddings, destination, centroids):
    samp, cent = lax.axis_index("samp"), lax.axis_index("cent")
    core = lax.bitwise_and(cent, 1)
    x = lax.shift_right_logical(samp, 2) * 2 + lax.shift_right_logical(cent, 3)
    y, z = lax.bitwise_and(lax.shift_right_logical(cent, 1), 3), lax.bitwise_and(samp, 3)
    side = lax.bitwise_and(x, 1)
    second = lax.bitwise_and(jnp.where(core == 0, y, z) + 2 * side, 3)
    step = jnp.where(side == core, 1, 3)
    spot = jnp.stack([x, second, jnp.where(core == 0, z, y), step, side]).astype(jnp.int32)
    share = centroids.shape[0] // 8
    width = embeddings.shape[1]
    smem = pl.BlockSpec(memory_space=pltpu.SMEM)
    vmem = pl.BlockSpec(memory_space=pltpu.VMEM)
    small = pltpu.CompilerParams(vmem_limit_bytes=8 << 20)
    ids = jnp.tile(destination.astype(jnp.float32), 2).reshape(1, 128)
    at_word = jnp.stack([samp, cent]).astype(jnp.int32)
    line = join(embeddings, *[fetch(embeddings, 0, step) for step in (1, 2, 3)])
    spot, ids, at_word, line = lax.optimization_barrier((spot, ids, at_word, line))
    near, across, back = [fetch(line, 1, step) for step in (1, 2, 3)]
    first, second = pl.pallas_call(
        halves_kernel,
        out_shape=[jax.ShapeDtypeStruct((512, width), embeddings.dtype)] * 2,
        in_specs=[smem] + [vmem] * 4,
        out_specs=[vmem] * 2,
        compiler_params=small,
        name="halves",
    )(spot, line, near, across, back)
    far_first = fetch(first, 2, 2)
    after_first, before_first = fetch(first, 2, 1), fetch(first, 2, 3)
    after_second, before_second = fetch(second, 2, 1), fetch(second, 2, 3)
    at_word, first, second = lax.optimization_barrier((at_word, first, second))
    mine = pl.pallas_call(
        share_kernel,
        out_shape=jax.ShapeDtypeStruct((share, width), centroids.dtype),
        in_specs=[smem, pl.BlockSpec(memory_space=pltpu.HBM)],
        out_specs=vmem,
        scratch_shapes=[pltpu.SemaphoreType.DMA((8,))],
        compiler_params=small,
        name="share",
    )(at_word, centroids)
    other = swap_cores(mine)
    score = functools.partial(scores_call, mine, other)
    far_second = swap_sides(far_first)
    chunks = [first, second, after_first, after_second, far_first, far_second, before_first, before_second]
    swapped = (5,)
    early_ps, early_stat = score([far_first, first, second])
    calls, last = {}, early_stat
    for k in (3, 6, 5, 7, 2):
        chunks[k], _ = lax.optimization_barrier((chunks[k], last))
        calls[k] = score([chunks[k]])
        last = calls[k][1]
    ps = early_ps[1:] + [calls[2][0][0], calls[3][0][0], early_ps[0]] + [calls[k][0][0] for k in (5, 6, 7)]
    stats = [early_stat] + [calls[k][1] for k in (2, 3, 5, 6, 7)]
    order = ((0, 1), (0, 2), (1, 0), (2, 0), (0, 0), (3, 0), (4, 0), (5, 0))

    local, tops = pl.pallas_call(
        functools.partial(first_kernel, swapped, order),
        out_shape=(
            jax.ShapeDtypeStruct((16, 8, 640), jnp.float32),
            jax.ShapeDtypeStruct((2, 4096), jnp.float32),
        ),
        in_specs=[smem] + [vmem] * 7,
        compiler_params=small,
        name="first",
    )(spot, ids, *stats)
    planes = [[place(i % 4, i // 4, z, 0) for i in range(16)] for z in range(4)]
    planes += [[place(i % 4, y, i // 4, 1) for i in range(16)] for y in range(4)]
    shared = lax.all_to_all(local, BOTH, split_axis=0, concat_axis=0, tiled=True, axis_index_groups=planes)
    plane = pl.pallas_call(
        plane_kernel,
        out_shape=jax.ShapeDtypeStruct((8, 640), jnp.float32),
        in_specs=[vmem],
        out_specs=vmem,
        compiler_params=small,
        name="plane",
    )(shared)
    pack, lse = pl.pallas_call(
        functools.partial(merge_kernel, swapped),
        out_shape=(
            jax.ShapeDtypeStruct((64, 128), jnp.float32),
            jax.ShapeDtypeStruct((1, 4096), jnp.float32),
        ),
        in_specs=[smem] + [vmem] * 4,
        compiler_params=small,
        name="merge",
    )(spot, plane, *[fetch(plane, 2, offset) for offset in (1, 2, 3)])
    theirs = sums_call(1, lse, tops, ps, chunks)
    received = swap_cores(theirs)
    partner = swap_cores(pack)
    ours = sums_call(0, lse, tops, ps[:7], chunks[:7])
    new_centers, row_lse = pl.pallas_call(
        functools.partial(final_kernel, 7, 1),
        out_shape=(
            jax.ShapeDtypeStruct((share, width), jnp.float32),
            jax.ShapeDtypeStruct((1, UNIT), jnp.float32),
        ),
        in_specs=[smem] + [vmem] * 9,
        out_specs=(pl.BlockSpec(memory_space=pl.ANY), vmem),
        scratch_shapes=[pltpu.VMEM((share, width), jnp.float32), pltpu.SemaphoreType.DMA((4,))],
        compiler_params=pltpu.CompilerParams(vmem_limit_bytes=12 << 20),
        name="final",
    )(at_word, lse, tops, ours, received, mine, pack, partner, *ps[7:], *chunks[7:])
    return new_centers, row_lse.reshape(UNIT)


def solution(mesh):
    in_specs = (P(BOTH, None), P(BOTH), P("cent", None))
    out_specs = (P(("cent", "samp"), None), P(BOTH))
    return jax.shard_map(shards, mesh=mesh, in_specs=in_specs, out_specs=out_specs, check_vma=False)
```

```python
import functools
import math

import jax
import jax.numpy as jnp
from jax import lax
from jax.experimental import pallas as pl
from jax.experimental.pallas import tpu as pltpu
from jax.sharding import PartitionSpec as P

inv_temp = 2.5
prior_mass = 0.25
BOTH = ("samp", "cent")
UNIT = 64
X, Y, Z = 0, 1, 2
ORDERS = ((X, Y, Z), (X, Z, Y))


def place(x, y, z, core):
    return ((x // 2) * 4 + z) * 16 + (x % 2) * 8 + y * 2 + core


def fetch(value, stage, offset):
    pairs = []
    for x in range(4):
        for y in range(4):
            for z in range(4):
                for core in range(2):
                    at = [x, y, z]
                    axis = ORDERS[core][stage]
                    at[axis] = (at[axis] + offset) % 4
                    pairs.append((place(*at, core), place(x, y, z, core)))
    return lax.ppermute(value, BOTH, pairs)


def swap_cores(value):
    pairs = [(i, i ^ 1) for i in range(128)]
    return lax.ppermute(value, BOTH, pairs)


def swap_sides(value):
    pairs = []
    for x in range(4):
        for y in range(4):
            for z in range(4):
                for core in range(2):
                    other = (x + (1 if x % 2 == core else 3)) % 4
                    pairs.append((place(other, y, z, core), place(x, y, z, core)))
    return lax.ppermute(value, BOTH, pairs)


def scores_kernel(factor, count, mine_ref, other_ref, *refs):
    rows = refs[:count]
    ps = refs[count : 2 * count]
    stat_ref = refs[2 * count]
    tiles = [(k, part, half) for k in range(count) for part in range(2) for half in range(2)]

    def product(tile):
        k, part, half = tile
        return lax.dot_general(
            (mine_ref, other_ref)[half][...],
            rows[k][part * 256 : (part + 1) * 256, :],
            (((1,), (1,)), ((), ())),
            preferred_element_type=jnp.float32,
        )

    following = product(tiles[0])
    for i, (k, part, half) in enumerate(tiles):
        s = following * factor
        if i + 1 < len(tiles):
            following = product(tiles[i + 1])
        top = jnp.max(s, axis=0, keepdims=True)
        e = jnp.exp2(s - top)
        ps[k][half, :, part * 256 : (part + 1) * 256] = e
        lanes = slice(k * 512 + part * 256, k * 512 + (part + 1) * 256)
        stat_ref[half : half + 1, lanes] = top
        stat_ref[2 + half : 3 + half, lanes] = jnp.sum(e, axis=0, keepdims=True)


def scores_call(mine, other, rows):
    count = len(rows)
    n, width = rows[0].shape
    factor = inv_temp / math.sqrt(width) * math.log2(math.e)
    vmem = pl.BlockSpec(memory_space=pltpu.VMEM)
    *ps, stat = pl.pallas_call(
        functools.partial(scores_kernel, factor, count),
        out_shape=tuple([jax.ShapeDtypeStruct((2, 512, n), jnp.float32)] * count)
        + (jax.ShapeDtypeStruct((4, count * n), jnp.float32),),
        in_specs=[vmem] * (2 + count),
        out_specs=tuple([vmem] * (count + 1)),
        compiler_params=pltpu.CompilerParams(vmem_limit_bytes=12 << 20),
        cost_estimate=pl.CostEstimate(
            flops=4 * 1024 * n * width * count,
            bytes_accessed=count * n * 6144 + (2 << 20),
            transcendentals=1024 * n * count,
        ),
        name="scores",
    )(mine, other, *rows)
    return ps, stat


def roll_within(value, dim, step):
    inner = UNIT * 4**dim
    group = inner * 4
    size = value.shape[1]
    lane = lax.broadcasted_iota(jnp.int32, value.shape, 1) % group
    ahead = pltpu.roll(value, step * inner, 1)
    back = pltpu.roll(value, size - group + step * inner, 1)
    return jnp.where(lane >= step * inner, ahead, back)


def first_kernel(swapped, order, spot_ref, ids_ref, *refs):
    *stats, out_ref, top_ref = refs
    parts = []
    for k, (ref, piece) in enumerate(order):
        lanes = slice(piece * 512, (piece + 1) * 512)
        tops = stats[ref][0:2, lanes]
        top = jnp.max(tops, axis=0, keepdims=True)
        total = jnp.sum(stats[ref][2:4, lanes] * jnp.exp2(tops - top), axis=0, keepdims=True)
        part = top + jnp.log2(total)
        parts.append(roll_within(part, 0, spot_ref[3]) if k in swapped else part)
        top_ref[:, k * 512 : (k + 1) * 512] = tops
    value = jnp.concatenate(parts, axis=1)
    for dim in range(3):
        value = roll_within(value, dim, spot_ref[dim])
    for line in range(8):
        piece = value[:, line * 512 : (line + 1) * 512]
        out_ref[:, line, 0:512] = jnp.broadcast_to(piece, (16, 512))
    lane = lax.broadcasted_iota(jnp.int32, (1, 128), 1)
    ids = jnp.where(lane // UNIT == spot_ref[0] % 2, ids_ref[...], -1.0)
    out_ref[:, :, 512:640] = jnp.broadcast_to(ids.reshape(1, 1, 128), (16, 8, 128))


def combine(values):
    top = functools.reduce(jnp.maximum, values)
    return top + jnp.log2(sum(jnp.exp2(value - top) for value in values))


def plane_kernel(all_ref, out_ref):
    out_ref[:, 0:512] = combine([all_ref[k, :, 0:512] for k in range(16)])
    for line in range(8):
        pair = jnp.maximum(all_ref[2 * line, 0:1, 512:640], all_ref[2 * line + 1, 0:1, 512:640])
        out_ref[line : line + 1, 512:640] = pair


def merge_kernel(swapped, spot_ref, *refs):
    *planes, pack_ref, own_ref = refs
    lse = combine([plane[:, 0:512] for plane in planes])
    value = jnp.concatenate([lse[line : line + 1, :] for line in range(8)], axis=1)
    for tile in range(32):
        pack_ref[tile : tile + 1, :] = value[:, tile * 128 : (tile + 1) * 128]
    for offset, plane in zip((0, 3, 2, 1), planes):
        first = pl.multiple_of(32 + (spot_ref[2] + offset) % 4 * 8, 8)
        pack_ref[pl.ds(first, 8), :] = plane[:, 512:640]
    for dim in range(3):
        value = roll_within(value, dim, (4 - spot_ref[dim]) % 4)
    own_ref[...] = value
    for k in swapped:
        lanes = slice(k * 512, (k + 1) * 512)
        own_ref[:, lanes] = roll_within(value[:, lanes], 0, 4 - spot_ref[3])


def join_kernel(slots, *refs):
    *parts, out_ref = refs
    rows = parts[0].shape[0]
    for slot, part in zip(slots, parts):
        out_ref[slot * rows : (slot + 1) * rows, :] = part[...]


def halves_kernel(spot_ref, *refs):
    line, back, across, near, first_ref, second_ref = refs
    parts = (line, near, across, back)
    rows = parts[0].shape[0]
    for side in range(2):

        @pl.when(spot_ref[4] == side)
        def _():
            for k, part in enumerate(parts):
                out_ref = (first_ref, second_ref)[(k // 2 + side) % 2]
                out_ref[k % 2 * rows : (k % 2 + 1) * rows, :] = part[...]


def join(slots, *parts):
    vmem = pl.BlockSpec(memory_space=pltpu.VMEM)
    shape = (sum(part.shape[0] for part in parts), parts[0].shape[1])
    return pl.pallas_call(
        functools.partial(join_kernel, slots),
        out_shape=jax.ShapeDtypeStruct(shape, parts[0].dtype),
        in_specs=[vmem] * len(parts),
        out_specs=vmem,
        compiler_params=pltpu.CompilerParams(vmem_limit_bytes=8 << 20),
        name="join",
    )(*parts)


def sums_kernel(half, count, lse_ref, top_ref, *refs):
    ps = refs[:count]
    rows = refs[count : 2 * count]
    out_ref = refs[2 * count]
    n, width = rows[0].shape

    def weights(k):
        lanes = slice(k * n, (k + 1) * n)
        f = jnp.exp2(top_ref[half : half + 1, lanes] - lse_ref[:, lanes])
        w = (ps[k][half] * f).astype(jnp.bfloat16)
        wide = w.astype(jnp.float32)
        return w, sum(wide[:, c : c + 128] for c in range(0, n, 128))

    w, mass = weights(0)
    for k in range(count):
        now = w
        if k + 1 < count:
            w, more = weights(k + 1)
            mass = mass + more
        add = jnp.dot(now, rows[k][...], preferred_element_type=jnp.float32)
        if k == 0:
            out_ref[:, :width] = add
        else:
            out_ref[:, :width] += add
    out_ref[:, width:] = mass


def sums_call(half, lse, tops, ps, rows):
    count = len(rows)
    width = rows[0].shape[1]
    vmem = pl.BlockSpec(memory_space=pltpu.VMEM)
    return pl.pallas_call(
        functools.partial(sums_kernel, half, count),
        out_shape=jax.ShapeDtypeStruct((512, width + 128), jnp.float32),
        in_specs=[vmem] * (2 + 2 * count),
        compiler_params=pltpu.CompilerParams(vmem_limit_bytes=12 << 20),
        cost_estimate=pl.CostEstimate(
            flops=2 * 512 * 512 * count * width, bytes_accessed=18 << 20, transcendentals=8192
        ),
        name="sums",
    )(lse, tops, *ps, *rows)


def final_kernel(skip, count, at_ref, lse_ref, top_ref, ours_ref, theirs_ref, mine_ref, pack_ref, other_ref, *refs):
    ps = refs[:count]
    rows = refs[count : 2 * count]
    out_ref, row_ref, buf, sems = refs[2 * count :]
    n, width = rows[0].shape
    mass = ours_ref[:, width:] + theirs_ref[:, width:]
    ws = []
    for k in range(count):
        lanes = slice((skip + k) * n, (skip + k + 1) * n)
        f = jnp.exp2(top_ref[0:1, lanes] - lse_ref[:, lanes])
        w = (ps[k][0] * f).astype(jnp.bfloat16)
        wide = w.astype(jnp.float32)
        mass = mass + sum(wide[:, c : c + 128] for c in range(0, n, 128))
        ws.append(w)
    inverse = 1.0 / (jnp.sum(mass, axis=1, keepdims=True) + prior_mass)
    base = (at_ref[0] * 16 + at_ref[1]) * UNIT
    logical = (lax.broadcasted_iota(jnp.int32, (UNIT, 128), 0) + base).astype(jnp.float32)
    routed = []
    copies = []
    for block in range(4):
        found = jnp.zeros((UNIT, 128), jnp.float32)
        for line in range(block * 8, block * 8 + 8):
            for ref in (pack_ref, other_ref):
                hit = ref[32 + line : 33 + line, :] == logical
                found = found + jnp.where(hit, ref[line : line + 1, :], 0.0)
        routed.append(found)
        columns = slice(block * width // 4, (block + 1) * width // 4)
        total = ours_ref[:, columns] + theirs_ref[:, columns]
        total = total + prior_mass * mine_ref[:, columns].astype(jnp.float32)
        for k in range(count):
            total = total + jnp.dot(ws[k], rows[k][:, columns], preferred_element_type=jnp.float32)
        buf[:, columns] = total * inverse
        copy = pltpu.make_async_copy(buf.at[:, columns], out_ref.at[:, columns], sems.at[block])
        copy.start()
        copies.append(copy)
    found = (routed[0] + routed[1]) + (routed[2] + routed[3])
    row_ref[...] = jnp.sum(found.T, axis=0, keepdims=True) * math.log(2.0)
    for copy in copies:
        copy.wait()


def share_kernel(at_ref, cents_ref, out_ref, sem):
    size = out_ref.shape[0]
    first = pl.multiple_of(at_ref[0] * size, size)
    part = size // 8
    copies = [
        pltpu.make_async_copy(
            cents_ref.at[pl.ds(first + k * part, part)], out_ref.at[pl.ds(k * part, part)], sem.at[k]
        )
        for k in range(8)
    ]
    for copy in copies:
        copy.start()
    for copy in copies:
        copy.wait()


def shards(embeddings, destination, centroids):
    samp, cent = lax.axis_index("samp"), lax.axis_index("cent")
    core = lax.bitwise_and(cent, 1)
    x = lax.shift_right_logical(samp, 2) * 2 + lax.shift_right_logical(cent, 3)
    y, z = lax.bitwise_and(lax.shift_right_logical(cent, 1), 3), lax.bitwise_and(samp, 3)
    side = lax.bitwise_and(x, 1)
    second = lax.bitwise_and(jnp.where(core == 0, y, z) + 2 * side, 3)
    step = jnp.where(side == core, 1, 3)
    spot = jnp.stack([x, second, jnp.where(core == 0, z, y), step, side]).astype(jnp.int32)
    share = centroids.shape[0] // 8
    width = embeddings.shape[1]
    smem = pl.BlockSpec(memory_space=pltpu.SMEM)
    vmem = pl.BlockSpec(memory_space=pltpu.VMEM)
    small = pltpu.CompilerParams(vmem_limit_bytes=8 << 20)
    ids = jnp.tile(destination.astype(jnp.float32), 2).reshape(1, 128)
    at_word = jnp.stack([samp, cent]).astype(jnp.int32)
    line = join((0, 2, 1, 3), embeddings, *[fetch(embeddings, 0, step) for step in (2, 1, 3)])
    spot, ids, at_word, line = lax.optimization_barrier((spot, ids, at_word, line))
    back, across, near = [fetch(line, 1, step) for step in (3, 2, 1)]
    first, second = pl.pallas_call(
        halves_kernel,
        out_shape=[jax.ShapeDtypeStruct((512, width), embeddings.dtype)] * 2,
        in_specs=[smem] + [vmem] * 4,
        out_specs=[vmem] * 2,
        compiler_params=small,
        name="halves",
    )(spot, line, back, across, near)
    far_first = fetch(first, 2, 2)
    after_first, before_first = fetch(first, 2, 1), fetch(first, 2, 3)
    after_second, before_second = fetch(second, 2, 1), fetch(second, 2, 3)
    at_word, first, second = lax.optimization_barrier((at_word, first, second))
    mine = pl.pallas_call(
        share_kernel,
        out_shape=jax.ShapeDtypeStruct((share, width), centroids.dtype),
        in_specs=[smem, pl.BlockSpec(memory_space=pltpu.HBM)],
        out_specs=vmem,
        scratch_shapes=[pltpu.SemaphoreType.DMA((8,))],
        compiler_params=small,
        name="share",
    )(at_word, centroids)
    other = swap_cores(mine)
    score = functools.partial(scores_call, mine, other)
    far_second = swap_sides(far_first)
    chunks = [first, second, after_first, after_second, far_first, far_second, before_first, before_second]
    swapped = (5,)
    early_ps, early_stat = score([far_first, first, second])
    calls, last = {}, early_stat
    for k in (3, 6, 5, 7, 2):
        chunks[k], _ = lax.optimization_barrier((chunks[k], last))
        calls[k] = score([chunks[k]])
        last = calls[k][1]
    ps = early_ps[1:] + [calls[2][0][0], calls[3][0][0], early_ps[0]] + [calls[k][0][0] for k in (5, 6, 7)]
    stats = [early_stat] + [calls[k][1] for k in (2, 3, 5, 6, 7)]
    order = ((0, 1), (0, 2), (1, 0), (2, 0), (0, 0), (3, 0), (4, 0), (5, 0))

    local, tops = pl.pallas_call(
        functools.partial(first_kernel, swapped, order),
        out_shape=(
            jax.ShapeDtypeStruct((16, 8, 640), jnp.float32),
            jax.ShapeDtypeStruct((2, 4096), jnp.float32),
        ),
        in_specs=[smem] + [vmem] * 7,
        compiler_params=small,
        name="first",
    )(spot, ids, *stats)
    planes = [[place(i % 4, i // 4, z, 0) for i in range(16)] for z in range(4)]
    planes += [[place(i % 4, y, i // 4, 1) for i in range(16)] for y in range(4)]
    shared = lax.all_to_all(local, BOTH, split_axis=0, concat_axis=0, tiled=True, axis_index_groups=planes)
    plane = pl.pallas_call(
        plane_kernel,
        out_shape=jax.ShapeDtypeStruct((8, 640), jnp.float32),
        in_specs=[vmem],
        out_specs=vmem,
        compiler_params=small,
        name="plane",
    )(shared)
    pack, lse = pl.pallas_call(
        functools.partial(merge_kernel, swapped),
        out_shape=(
            jax.ShapeDtypeStruct((64, 128), jnp.float32),
            jax.ShapeDtypeStruct((1, 4096), jnp.float32),
        ),
        in_specs=[smem] + [vmem] * 4,
        compiler_params=small,
        name="merge",
    )(spot, plane, *[fetch(plane, 2, offset) for offset in (3, 2, 1)])
    theirs = sums_call(1, lse, tops, ps, chunks)
    received = swap_cores(theirs)
    partner = swap_cores(pack)
    ours = sums_call(0, lse, tops, ps[:7], chunks[:7])
    new_centers, row_lse = pl.pallas_call(
        functools.partial(final_kernel, 7, 1),
        out_shape=(
            jax.ShapeDtypeStruct((share, width), jnp.float32),
            jax.ShapeDtypeStruct((1, UNIT), jnp.float32),
        ),
        in_specs=[smem] + [vmem] * 9,
        out_specs=(pl.BlockSpec(memory_space=pl.ANY), vmem),
        scratch_shapes=[pltpu.VMEM((share, width), jnp.float32), pltpu.SemaphoreType.DMA((4,))],
        compiler_params=pltpu.CompilerParams(vmem_limit_bytes=12 << 20),
        name="final",
    )(at_word, lse, tops, ours, received, mine, pack, partner, *ps[7:], *chunks[7:])
    return new_centers, row_lse.reshape(UNIT)


def solution(mesh):
    in_specs = (P(BOTH, None), P(BOTH), P("cent", None))
    out_specs = (P(("cent", "samp"), None), P(BOTH))
    return jax.shard_map(shards, mesh=mesh, in_specs=in_specs, out_specs=out_specs, check_vma=False)
```

```python
import functools
import math

import jax
import jax.numpy as jnp
from jax import lax
from jax.experimental import pallas as pl
from jax.experimental.pallas import tpu as pltpu
from jax.sharding import PartitionSpec as P

inv_temp = 2.5
prior_mass = 0.25
BOTH = ("samp", "cent")
UNIT = 64
X, Y, Z = 0, 1, 2
ORDERS = ((X, Y, Z), (X, Z, Y))


def place(x, y, z, core):
    return ((x // 2) * 4 + z) * 16 + (x % 2) * 8 + y * 2 + core


def fetch(value, stage, offset):
    pairs = []
    for x in range(4):
        for y in range(4):
            for z in range(4):
                for core in range(2):
                    at = [x, y, z]
                    axis = ORDERS[core][stage]
                    at[axis] = (at[axis] + offset) % 4
                    pairs.append((place(*at, core), place(x, y, z, core)))
    return lax.ppermute(value, BOTH, pairs)


def swap_cores(value):
    pairs = [(i, i ^ 1) for i in range(128)]
    return lax.ppermute(value, BOTH, pairs)


def swap_sides(value):
    pairs = []
    for x in range(4):
        for y in range(4):
            for z in range(4):
                for core in range(2):
                    other = (x + (1 if x % 2 == core else 3)) % 4
                    pairs.append((place(other, y, z, core), place(x, y, z, core)))
    return lax.ppermute(value, BOTH, pairs)


def scores_kernel(factor, count, mine_ref, other_ref, *refs):
    rows = refs[:count]
    ps = refs[count : 2 * count]
    stat_ref = refs[2 * count]
    tiles = [(k, part, half) for k in range(count) for part in range(2) for half in range(2)]

    def product(tile):
        k, part, half = tile
        return lax.dot_general(
            (mine_ref, other_ref)[half][...],
            rows[k][part * 256 : (part + 1) * 256, :],
            (((1,), (1,)), ((), ())),
            preferred_element_type=jnp.float32,
        )

    following = product(tiles[0])
    for i, (k, part, half) in enumerate(tiles):
        s = following * factor
        if i + 1 < len(tiles):
            following = product(tiles[i + 1])
        top = jnp.max(s, axis=0, keepdims=True)
        e = jnp.exp2(s - top)
        ps[k][half, :, part * 256 : (part + 1) * 256] = e
        lanes = slice(k * 512 + part * 256, k * 512 + (part + 1) * 256)
        stat_ref[half : half + 1, lanes] = top
        stat_ref[2 + half : 3 + half, lanes] = jnp.sum(e, axis=0, keepdims=True)


def scores_call(mine, other, rows):
    count = len(rows)
    n, width = rows[0].shape
    factor = inv_temp / math.sqrt(width) * math.log2(math.e)
    vmem = pl.BlockSpec(memory_space=pltpu.VMEM)
    *ps, stat = pl.pallas_call(
        functools.partial(scores_kernel, factor, count),
        out_shape=tuple([jax.ShapeDtypeStruct((2, 512, n), jnp.float32)] * count)
        + (jax.ShapeDtypeStruct((4, count * n), jnp.float32),),
        in_specs=[vmem] * (2 + count),
        out_specs=tuple([vmem] * (count + 1)),
        compiler_params=pltpu.CompilerParams(vmem_limit_bytes=12 << 20),
        cost_estimate=pl.CostEstimate(
            flops=4 * 1024 * n * width * count,
            bytes_accessed=count * n * 6144 + (2 << 20),
            transcendentals=1024 * n * count,
        ),
        name="scores",
    )(mine, other, *rows)
    return ps, stat


def roll_within(value, dim, step):
    inner = UNIT * 4**dim
    group = inner * 4
    size = value.shape[1]
    lane = lax.broadcasted_iota(jnp.int32, value.shape, 1) % group
    ahead = pltpu.roll(value, step * inner, 1)
    back = pltpu.roll(value, size - group + step * inner, 1)
    return jnp.where(lane >= step * inner, ahead, back)


def first_kernel(swapped, order, spot_ref, ids_ref, *refs):
    *stats, out_ref, top_ref = refs
    parts = []
    for k, (ref, piece) in enumerate(order):
        lanes = slice(piece * 512, (piece + 1) * 512)
        tops = stats[ref][0:2, lanes]
        top = jnp.max(tops, axis=0, keepdims=True)
        total = jnp.sum(stats[ref][2:4, lanes] * jnp.exp2(tops - top), axis=0, keepdims=True)
        part = top + jnp.log2(total)
        parts.append(roll_within(part, 0, spot_ref[3]) if k in swapped else part)
        top_ref[:, k * 512 : (k + 1) * 512] = tops
    value = jnp.concatenate(parts, axis=1)
    for dim in range(3):
        value = roll_within(value, dim, spot_ref[dim])
    for line in range(8):
        piece = value[:, line * 512 : (line + 1) * 512]
        out_ref[:, line, 0:512] = jnp.broadcast_to(piece, (16, 512))
    lane = lax.broadcasted_iota(jnp.int32, (1, 128), 1)
    ids = jnp.where(lane // UNIT == spot_ref[0] % 2, ids_ref[...], -1.0)
    out_ref[:, :, 512:640] = jnp.broadcast_to(ids.reshape(1, 1, 128), (16, 8, 128))


def combine(values):
    top = functools.reduce(jnp.maximum, values)
    return top + jnp.log2(sum(jnp.exp2(value - top) for value in values))


def plane_kernel(all_ref, out_ref):
    out_ref[:, 0:512] = combine([all_ref[k, :, 0:512] for k in range(16)])
    for line in range(8):
        pair = jnp.maximum(all_ref[2 * line, 0:1, 512:640], all_ref[2 * line + 1, 0:1, 512:640])
        out_ref[line : line + 1, 512:640] = pair


def merge_kernel(swapped, spot_ref, *refs):
    *planes, pack_ref, own_ref = refs
    lse = combine([plane[:, 0:512] for plane in planes])
    value = jnp.concatenate([lse[line : line + 1, :] for line in range(8)], axis=1)
    for tile in range(32):
        pack_ref[tile : tile + 1, :] = value[:, tile * 128 : (tile + 1) * 128]
    for offset, plane in zip((0, 2, 1, 3), planes):
        first = pl.multiple_of(32 + (spot_ref[2] + offset) % 4 * 8, 8)
        pack_ref[pl.ds(first, 8), :] = plane[:, 512:640]
    for dim in range(3):
        value = roll_within(value, dim, (4 - spot_ref[dim]) % 4)
    own_ref[...] = value
    for k in swapped:
        lanes = slice(k * 512, (k + 1) * 512)
        own_ref[:, lanes] = roll_within(value[:, lanes], 0, 4 - spot_ref[3])


def join_kernel(slots, *refs):
    *parts, out_ref = refs
    rows = parts[0].shape[0]
    for slot, part in zip(slots, parts):
        out_ref[slot * rows : (slot + 1) * rows, :] = part[...]


def halves_kernel(spot_ref, *refs):
    line, across, near, back, first_ref, second_ref = refs
    parts = (line, near, across, back)
    rows = parts[0].shape[0]
    for side in range(2):

        @pl.when(spot_ref[4] == side)
        def _():
            for k, part in enumerate(parts):
                out_ref = (first_ref, second_ref)[(k // 2 + side) % 2]
                out_ref[k % 2 * rows : (k % 2 + 1) * rows, :] = part[...]


def join(slots, *parts):
    vmem = pl.BlockSpec(memory_space=pltpu.VMEM)
    shape = (sum(part.shape[0] for part in parts), parts[0].shape[1])
    return pl.pallas_call(
        functools.partial(join_kernel, slots),
        out_shape=jax.ShapeDtypeStruct(shape, parts[0].dtype),
        in_specs=[vmem] * len(parts),
        out_specs=vmem,
        compiler_params=pltpu.CompilerParams(vmem_limit_bytes=8 << 20),
        name="join",
    )(*parts)


def sums_kernel(half, count, lse_ref, top_ref, *refs):
    ps = refs[:count]
    rows = refs[count : 2 * count]
    out_ref = refs[2 * count]
    n, width = rows[0].shape

    def weights(k):
        lanes = slice(k * n, (k + 1) * n)
        f = jnp.exp2(top_ref[half : half + 1, lanes] - lse_ref[:, lanes])
        w = (ps[k][half] * f).astype(jnp.bfloat16)
        wide = w.astype(jnp.float32)
        return w, sum(wide[:, c : c + 128] for c in range(0, n, 128))

    w, mass = weights(0)
    for k in range(count):
        now = w
        if k + 1 < count:
            w, more = weights(k + 1)
            mass = mass + more
        add = jnp.dot(now, rows[k][...], preferred_element_type=jnp.float32)
        if k == 0:
            out_ref[:, :width] = add
        else:
            out_ref[:, :width] += add
    out_ref[:, width:] = mass


def sums_call(half, lse, tops, ps, rows):
    count = len(rows)
    width = rows[0].shape[1]
    vmem = pl.BlockSpec(memory_space=pltpu.VMEM)
    return pl.pallas_call(
        functools.partial(sums_kernel, half, count),
        out_shape=jax.ShapeDtypeStruct((512, width + 128), jnp.float32),
        in_specs=[vmem] * (2 + 2 * count),
        compiler_params=pltpu.CompilerParams(vmem_limit_bytes=12 << 20),
        cost_estimate=pl.CostEstimate(
            flops=2 * 512 * 512 * count * width, bytes_accessed=18 << 20, transcendentals=8192
        ),
        name="sums",
    )(lse, tops, *ps, *rows)


def final_kernel(skip, count, at_ref, lse_ref, top_ref, ours_ref, theirs_ref, mine_ref, pack_ref, other_ref, *refs):
    ps = refs[:count]
    rows = refs[count : 2 * count]
    out_ref, row_ref, buf, sems = refs[2 * count :]
    n, width = rows[0].shape
    mass = ours_ref[:, width:] + theirs_ref[:, width:]
    ws = []
    for k in range(count):
        lanes = slice((skip + k) * n, (skip + k + 1) * n)
        f = jnp.exp2(top_ref[0:1, lanes] - lse_ref[:, lanes])
        w = (ps[k][0] * f).astype(jnp.bfloat16)
        wide = w.astype(jnp.float32)
        mass = mass + sum(wide[:, c : c + 128] for c in range(0, n, 128))
        ws.append(w)
    inverse = 1.0 / (jnp.sum(mass, axis=1, keepdims=True) + prior_mass)
    base = (at_ref[0] * 16 + at_ref[1]) * UNIT
    logical = (lax.broadcasted_iota(jnp.int32, (UNIT, 128), 0) + base).astype(jnp.float32)
    routed = []
    copies = []
    for block in range(4):
        found = jnp.zeros((UNIT, 128), jnp.float32)
        for line in range(block * 8, block * 8 + 8):
            for ref in (pack_ref, other_ref):
                hit = ref[32 + line : 33 + line, :] == logical
                found = found + jnp.where(hit, ref[line : line + 1, :], 0.0)
        routed.append(found)
        columns = slice(block * width // 4, (block + 1) * width // 4)
        total = ours_ref[:, columns] + theirs_ref[:, columns]
        total = total + prior_mass * mine_ref[:, columns].astype(jnp.float32)
        for k in range(count):
            total = total + jnp.dot(ws[k], rows[k][:, columns], preferred_element_type=jnp.float32)
        buf[:, columns] = total * inverse
        copy = pltpu.make_async_copy(buf.at[:, columns], out_ref.at[:, columns], sems.at[block])
        copy.start()
        copies.append(copy)
    found = (routed[0] + routed[1]) + (routed[2] + routed[3])
    row_ref[...] = jnp.sum(found.T, axis=0, keepdims=True) * math.log(2.0)
    for copy in copies:
        copy.wait()


def share_kernel(at_ref, cents_ref, out_ref, sem):
    size = out_ref.shape[0]
    first = pl.multiple_of(at_ref[0] * size, size)
    part = size // 8
    copies = [
        pltpu.make_async_copy(
            cents_ref.at[pl.ds(first + k * part, part)], out_ref.at[pl.ds(k * part, part)], sem.at[k]
        )
        for k in range(8)
    ]
    for copy in copies:
        copy.start()
    for copy in copies:
        copy.wait()


def shards(embeddings, destination, centroids):
    samp, cent = lax.axis_index("samp"), lax.axis_index("cent")
    core = lax.bitwise_and(cent, 1)
    x = lax.shift_right_logical(samp, 2) * 2 + lax.shift_right_logical(cent, 3)
    y, z = lax.bitwise_and(lax.shift_right_logical(cent, 1), 3), lax.bitwise_and(samp, 3)
    side = lax.bitwise_and(x, 1)
    second = lax.bitwise_and(jnp.where(core == 0, y, z) + 2 * side, 3)
    step = jnp.where(side == core, 1, 3)
    spot = jnp.stack([x, second, jnp.where(core == 0, z, y), step, side]).astype(jnp.int32)
    share = centroids.shape[0] // 8
    width = embeddings.shape[1]
    smem = pl.BlockSpec(memory_space=pltpu.SMEM)
    vmem = pl.BlockSpec(memory_space=pltpu.VMEM)
    small = pltpu.CompilerParams(vmem_limit_bytes=8 << 20)
    ids = jnp.tile(destination.astype(jnp.float32), 2).reshape(1, 128)
    at_word = jnp.stack([samp, cent]).astype(jnp.int32)
    line = join((0, 2, 1, 3), embeddings, *[fetch(embeddings, 0, step) for step in (2, 1, 3)])
    spot, ids, at_word, line = lax.optimization_barrier((spot, ids, at_word, line))
    back, across, near = [fetch(line, 1, step) for step in (3, 2, 1)]
    first, second = pl.pallas_call(
        halves_kernel,
        out_shape=[jax.ShapeDtypeStruct((512, width), embeddings.dtype)] * 2,
        in_specs=[smem] + [vmem] * 4,
        out_specs=[vmem] * 2,
        compiler_params=small,
        name="halves",
    )(spot, line, across, near, back)
    far_first = fetch(first, 2, 2)
    after_first, before_first = fetch(first, 2, 1), fetch(first, 2, 3)
    after_second, before_second = fetch(second, 2, 1), fetch(second, 2, 3)
    at_word, first, second = lax.optimization_barrier((at_word, first, second))
    mine = pl.pallas_call(
        share_kernel,
        out_shape=jax.ShapeDtypeStruct((share, width), centroids.dtype),
        in_specs=[smem, pl.BlockSpec(memory_space=pltpu.HBM)],
        out_specs=vmem,
        scratch_shapes=[pltpu.SemaphoreType.DMA((8,))],
        compiler_params=small,
        name="share",
    )(at_word, centroids)
    other = swap_cores(mine)
    score = functools.partial(scores_call, mine, other)
    far_second = swap_sides(far_first)
    chunks = [first, second, after_first, after_second, far_first, far_second, before_first, before_second]
    swapped = (5,)
    early_ps, early_stat = score([far_first, first, second])
    calls, last = {}, early_stat
    for k in (3, 6, 5, 7, 2):
        chunks[k], _ = lax.optimization_barrier((chunks[k], last))
        calls[k] = score([chunks[k]])
        last = calls[k][1]
    ps = early_ps[1:] + [calls[2][0][0], calls[3][0][0], early_ps[0]] + [calls[k][0][0] for k in (5, 6, 7)]
    stats = [early_stat] + [calls[k][1] for k in (2, 3, 5, 6, 7)]
    order = ((0, 1), (0, 2), (1, 0), (2, 0), (0, 0), (3, 0), (4, 0), (5, 0))

    local, tops = pl.pallas_call(
        functools.partial(first_kernel, swapped, order),
        out_shape=(
            jax.ShapeDtypeStruct((16, 8, 640), jnp.float32),
            jax.ShapeDtypeStruct((2, 4096), jnp.float32),
        ),
        in_specs=[smem] + [vmem] * 7,
        compiler_params=small,
        name="first",
    )(spot, ids, *stats)
    planes = [[place(i % 4, i // 4, z, 0) for i in range(16)] for z in range(4)]
    planes += [[place(i % 4, y, i // 4, 1) for i in range(16)] for y in range(4)]
    shared = lax.all_to_all(local, BOTH, split_axis=0, concat_axis=0, tiled=True, axis_index_groups=planes)
    plane = pl.pallas_call(
        plane_kernel,
        out_shape=jax.ShapeDtypeStruct((8, 640), jnp.float32),
        in_specs=[vmem],
        out_specs=vmem,
        compiler_params=small,
        name="plane",
    )(shared)
    pack, lse = pl.pallas_call(
        functools.partial(merge_kernel, swapped),
        out_shape=(
            jax.ShapeDtypeStruct((64, 128), jnp.float32),
            jax.ShapeDtypeStruct((1, 4096), jnp.float32),
        ),
        in_specs=[smem] + [vmem] * 4,
        compiler_params=small,
        name="merge",
    )(spot, plane, *[fetch(plane, 2, offset) for offset in (2, 1, 3)])
    theirs = sums_call(1, lse, tops, ps, chunks)
    received = swap_cores(theirs)
    partner = swap_cores(pack)
    ours = sums_call(0, lse, tops, ps[:7], chunks[:7])
    new_centers, row_lse = pl.pallas_call(
        functools.partial(final_kernel, 7, 1),
        out_shape=(
            jax.ShapeDtypeStruct((share, width), jnp.float32),
            jax.ShapeDtypeStruct((1, UNIT), jnp.float32),
        ),
        in_specs=[smem] + [vmem] * 9,
        out_specs=(pl.BlockSpec(memory_space=pl.ANY), vmem),
        scratch_shapes=[pltpu.VMEM((share, width), jnp.float32), pltpu.SemaphoreType.DMA((4,))],
        compiler_params=pltpu.CompilerParams(vmem_limit_bytes=12 << 20),
        name="final",
    )(at_word, lse, tops, ours, received, mine, pack, partner, *ps[7:], *chunks[7:])
    return new_centers, row_lse.reshape(UNIT)


def solution(mesh):
    in_specs = (P(BOTH, None), P(BOTH), P("cent", None))
    out_specs = (P(("cent", "samp"), None), P(BOTH))
    return jax.shard_map(shards, mesh=mesh, in_specs=in_specs, out_specs=out_specs, check_vma=False)
```

```python
import functools
import math

import jax
import jax.numpy as jnp
from jax import lax
from jax.experimental import pallas as pl
from jax.experimental.pallas import tpu as pltpu
from jax.sharding import PartitionSpec as P

inv_temp = 2.5
prior_mass = 0.25
BOTH = ("samp", "cent")
UNIT = 64
X, Y, Z = 0, 1, 2
ORDERS = ((X, Y, Z), (X, Z, Y))


def place(x, y, z, core):
    return ((x // 2) * 4 + z) * 16 + (x % 2) * 8 + y * 2 + core


def fetch(value, stage, offset):
    pairs = []
    for x in range(4):
        for y in range(4):
            for z in range(4):
                for core in range(2):
                    at = [x, y, z]
                    axis = ORDERS[core][stage]
                    at[axis] = (at[axis] + offset) % 4
                    pairs.append((place(*at, core), place(x, y, z, core)))
    return lax.ppermute(value, BOTH, pairs)


def swap_cores(value):
    pairs = [(i, i ^ 1) for i in range(128)]
    return lax.ppermute(value, BOTH, pairs)


def swap_sides(value):
    pairs = []
    for x in range(4):
        for y in range(4):
            for z in range(4):
                for core in range(2):
                    other = (x + (1 if x % 2 == core else 3)) % 4
                    pairs.append((place(other, y, z, core), place(x, y, z, core)))
    return lax.ppermute(value, BOTH, pairs)


def scores_kernel(factor, count, mine_ref, other_ref, *refs):
    rows = refs[:count]
    ps = refs[count : 2 * count]
    stat_ref = refs[2 * count]
    tiles = [(k, part, half) for k in range(count) for part in range(2) for half in range(2)]

    def product(tile):
        k, part, half = tile
        return lax.dot_general(
            (mine_ref, other_ref)[half][...],
            rows[k][part * 256 : (part + 1) * 256, :],
            (((1,), (1,)), ((), ())),
            preferred_element_type=jnp.float32,
        )

    following = product(tiles[0])
    for i, (k, part, half) in enumerate(tiles):
        s = following * factor
        if i + 1 < len(tiles):
            following = product(tiles[i + 1])
        top = jnp.max(s, axis=0, keepdims=True)
        e = jnp.exp2(s - top)
        ps[k][half, :, part * 256 : (part + 1) * 256] = e
        lanes = slice(k * 512 + part * 256, k * 512 + (part + 1) * 256)
        stat_ref[half : half + 1, lanes] = top
        stat_ref[2 + half : 3 + half, lanes] = jnp.sum(e, axis=0, keepdims=True)


def scores_call(mine, other, rows):
    count = len(rows)
    n, width = rows[0].shape
    factor = inv_temp / math.sqrt(width) * math.log2(math.e)
    vmem = pl.BlockSpec(memory_space=pltpu.VMEM)
    *ps, stat = pl.pallas_call(
        functools.partial(scores_kernel, factor, count),
        out_shape=tuple([jax.ShapeDtypeStruct((2, 512, n), jnp.float32)] * count)
        + (jax.ShapeDtypeStruct((4, count * n), jnp.float32),),
        in_specs=[vmem] * (2 + count),
        out_specs=tuple([vmem] * (count + 1)),
        compiler_params=pltpu.CompilerParams(vmem_limit_bytes=12 << 20),
        cost_estimate=pl.CostEstimate(
            flops=4 * 1024 * n * width * count,
            bytes_accessed=count * n * 6144 + (2 << 20),
            transcendentals=1024 * n * count,
        ),
        name="scores",
    )(mine, other, *rows)
    return ps, stat


def roll_within(value, dim, step):
    inner = UNIT * 4**dim
    group = inner * 4
    size = value.shape[1]
    lane = lax.broadcasted_iota(jnp.int32, value.shape, 1) % group
    ahead = pltpu.roll(value, step * inner, 1)
    back = pltpu.roll(value, size - group + step * inner, 1)
    return jnp.where(lane >= step * inner, ahead, back)


def first_kernel(swapped, order, spot_ref, ids_ref, *refs):
    *stats, out_ref, top_ref = refs
    parts = []
    for k, (ref, piece) in enumerate(order):
        lanes = slice(piece * 512, (piece + 1) * 512)
        tops = stats[ref][0:2, lanes]
        top = jnp.max(tops, axis=0, keepdims=True)
        total = jnp.sum(stats[ref][2:4, lanes] * jnp.exp2(tops - top), axis=0, keepdims=True)
        part = top + jnp.log2(total)
        parts.append(roll_within(part, 0, spot_ref[3]) if k in swapped else part)
        top_ref[:, k * 512 : (k + 1) * 512] = tops
    value = jnp.concatenate(parts, axis=1)
    for dim in range(3):
        value = roll_within(value, dim, spot_ref[dim])
    for line in range(8):
        piece = value[:, line * 512 : (line + 1) * 512]
        out_ref[:, line, 0:512] = jnp.broadcast_to(piece, (16, 512))
    lane = lax.broadcasted_iota(jnp.int32, (1, 128), 1)
    ids = jnp.where(lane // UNIT == spot_ref[0] % 2, ids_ref[...], -1.0)
    out_ref[:, :, 512:640] = jnp.broadcast_to(ids.reshape(1, 1, 128), (16, 8, 128))


def combine(values):
    top = functools.reduce(jnp.maximum, values)
    return top + jnp.log2(sum(jnp.exp2(value - top) for value in values))


def plane_kernel(all_ref, out_ref):
    out_ref[:, 0:512] = combine([all_ref[k, :, 0:512] for k in range(16)])
    for line in range(8):
        pair = jnp.maximum(all_ref[2 * line, 0:1, 512:640], all_ref[2 * line + 1, 0:1, 512:640])
        out_ref[line : line + 1, 512:640] = pair


def merge_kernel(swapped, spot_ref, *refs):
    *planes, pack_ref, own_ref = refs
    lse = combine([plane[:, 0:512] for plane in planes])
    value = jnp.concatenate([lse[line : line + 1, :] for line in range(8)], axis=1)
    for tile in range(32):
        pack_ref[tile : tile + 1, :] = value[:, tile * 128 : (tile + 1) * 128]
    for offset, plane in zip((0, 3, 2, 1), planes):
        first = pl.multiple_of(32 + (spot_ref[2] + offset) % 4 * 8, 8)
        pack_ref[pl.ds(first, 8), :] = plane[:, 512:640]
    for dim in range(3):
        value = roll_within(value, dim, (4 - spot_ref[dim]) % 4)
    own_ref[...] = value
    for k in swapped:
        lanes = slice(k * 512, (k + 1) * 512)
        own_ref[:, lanes] = roll_within(value[:, lanes], 0, 4 - spot_ref[3])


def join_kernel(slots, *refs):
    *parts, out_ref = refs
    rows = parts[0].shape[0]
    for slot, part in zip(slots, parts):
        out_ref[slot * rows : (slot + 1) * rows, :] = part[...]


def halves_kernel(spot_ref, *refs):
    line, across, near, back, first_ref, second_ref = refs
    parts = (line, near, across, back)
    rows = parts[0].shape[0]
    for side in range(2):

        @pl.when(spot_ref[4] == side)
        def _():
            for k, part in enumerate(parts):
                out_ref = (first_ref, second_ref)[(k // 2 + side) % 2]
                out_ref[k % 2 * rows : (k % 2 + 1) * rows, :] = part[...]


def join(slots, *parts):
    vmem = pl.BlockSpec(memory_space=pltpu.VMEM)
    shape = (sum(part.shape[0] for part in parts), parts[0].shape[1])
    return pl.pallas_call(
        functools.partial(join_kernel, slots),
        out_shape=jax.ShapeDtypeStruct(shape, parts[0].dtype),
        in_specs=[vmem] * len(parts),
        out_specs=vmem,
        compiler_params=pltpu.CompilerParams(vmem_limit_bytes=8 << 20),
        name="join",
    )(*parts)


def sums_kernel(half, count, lse_ref, top_ref, *refs):
    ps = refs[:count]
    rows = refs[count : 2 * count]
    out_ref = refs[2 * count]
    n, width = rows[0].shape

    def weights(k):
        lanes = slice(k * n, (k + 1) * n)
        f = jnp.exp2(top_ref[half : half + 1, lanes] - lse_ref[:, lanes])
        w = (ps[k][half] * f).astype(jnp.bfloat16)
        wide = w.astype(jnp.float32)
        return w, sum(wide[:, c : c + 128] for c in range(0, n, 128))

    w, mass = weights(0)
    for k in range(count):
        now = w
        if k + 1 < count:
            w, more = weights(k + 1)
            mass = mass + more
        add = jnp.dot(now, rows[k][...], preferred_element_type=jnp.float32)
        if k == 0:
            out_ref[:, :width] = add
        else:
            out_ref[:, :width] += add
    out_ref[:, width:] = mass


def sums_call(half, lse, tops, ps, rows):
    count = len(rows)
    width = rows[0].shape[1]
    vmem = pl.BlockSpec(memory_space=pltpu.VMEM)
    return pl.pallas_call(
        functools.partial(sums_kernel, half, count),
        out_shape=jax.ShapeDtypeStruct((512, width + 128), jnp.float32),
        in_specs=[vmem] * (2 + 2 * count),
        compiler_params=pltpu.CompilerParams(vmem_limit_bytes=12 << 20),
        cost_estimate=pl.CostEstimate(
            flops=2 * 512 * 512 * count * width, bytes_accessed=18 << 20, transcendentals=8192
        ),
        name="sums",
    )(lse, tops, *ps, *rows)


def final_kernel(skip, count, at_ref, lse_ref, top_ref, ours_ref, theirs_ref, mine_ref, pack_ref, other_ref, *refs):
    ps = refs[:count]
    rows = refs[count : 2 * count]
    out_ref, row_ref, buf, sems = refs[2 * count :]
    n, width = rows[0].shape
    mass = ours_ref[:, width:] + theirs_ref[:, width:]
    ws = []
    for k in range(count):
        lanes = slice((skip + k) * n, (skip + k + 1) * n)
        f = jnp.exp2(top_ref[0:1, lanes] - lse_ref[:, lanes])
        w = (ps[k][0] * f).astype(jnp.bfloat16)
        wide = w.astype(jnp.float32)
        mass = mass + sum(wide[:, c : c + 128] for c in range(0, n, 128))
        ws.append(w)
    inverse = 1.0 / (jnp.sum(mass, axis=1, keepdims=True) + prior_mass)
    base = (at_ref[0] * 16 + at_ref[1]) * UNIT
    logical = (lax.broadcasted_iota(jnp.int32, (UNIT, 128), 0) + base).astype(jnp.float32)
    routed = []
    copies = []
    for block in range(4):
        found = jnp.zeros((UNIT, 128), jnp.float32)
        for line in range(block * 8, block * 8 + 8):
            for ref in (pack_ref, other_ref):
                hit = ref[32 + line : 33 + line, :] == logical
                found = found + jnp.where(hit, ref[line : line + 1, :], 0.0)
        routed.append(found)
        columns = slice(block * width // 4, (block + 1) * width // 4)
        total = ours_ref[:, columns] + theirs_ref[:, columns]
        total = total + prior_mass * mine_ref[:, columns].astype(jnp.float32)
        for k in range(count):
            total = total + jnp.dot(ws[k], rows[k][:, columns], preferred_element_type=jnp.float32)
        buf[:, columns] = total * inverse
        copy = pltpu.make_async_copy(buf.at[:, columns], out_ref.at[:, columns], sems.at[block])
        copy.start()
        copies.append(copy)
    found = (routed[0] + routed[1]) + (routed[2] + routed[3])
    row_ref[...] = jnp.sum(found.T, axis=0, keepdims=True) * math.log(2.0)
    for copy in copies:
        copy.wait()


def share_kernel(at_ref, cents_ref, out_ref, sem):
    size = out_ref.shape[0]
    first = pl.multiple_of(at_ref[0] * size, size)
    part = size // 8
    copies = [
        pltpu.make_async_copy(
            cents_ref.at[pl.ds(first + k * part, part)], out_ref.at[pl.ds(k * part, part)], sem.at[k]
        )
        for k in range(8)
    ]
    for copy in copies:
        copy.start()
    for copy in copies:
        copy.wait()


def shards(embeddings, destination, centroids):
    samp, cent = lax.axis_index("samp"), lax.axis_index("cent")
    core = lax.bitwise_and(cent, 1)
    x = lax.shift_right_logical(samp, 2) * 2 + lax.shift_right_logical(cent, 3)
    y, z = lax.bitwise_and(lax.shift_right_logical(cent, 1), 3), lax.bitwise_and(samp, 3)
    side = lax.bitwise_and(x, 1)
    second = lax.bitwise_and(jnp.where(core == 0, y, z) + 2 * side, 3)
    step = jnp.where(side == core, 1, 3)
    spot = jnp.stack([x, second, jnp.where(core == 0, z, y), step, side]).astype(jnp.int32)
    share = centroids.shape[0] // 8
    width = embeddings.shape[1]
    smem = pl.BlockSpec(memory_space=pltpu.SMEM)
    vmem = pl.BlockSpec(memory_space=pltpu.VMEM)
    small = pltpu.CompilerParams(vmem_limit_bytes=8 << 20)
    ids = jnp.tile(destination.astype(jnp.float32), 2).reshape(1, 128)
    at_word = jnp.stack([samp, cent]).astype(jnp.int32)
    line = join((0, 2, 1, 3), embeddings, *[fetch(embeddings, 0, step) for step in (2, 1, 3)])
    spot, ids, at_word, line = lax.optimization_barrier((spot, ids, at_word, line))
    back, across, near = [fetch(line, 1, step) for step in (3, 2, 1)]
    first, second = pl.pallas_call(
        halves_kernel,
        out_shape=[jax.ShapeDtypeStruct((512, width), embeddings.dtype)] * 2,
        in_specs=[smem] + [vmem] * 4,
        out_specs=[vmem] * 2,
        compiler_params=small,
        name="halves",
    )(spot, line, across, near, back)
    far_first = fetch(first, 2, 2)
    after_first, before_first = fetch(first, 2, 1), fetch(first, 2, 3)
    after_second, before_second = fetch(second, 2, 1), fetch(second, 2, 3)
    at_word, first, second = lax.optimization_barrier((at_word, first, second))
    mine = pl.pallas_call(
        share_kernel,
        out_shape=jax.ShapeDtypeStruct((share, width), centroids.dtype),
        in_specs=[smem, pl.BlockSpec(memory_space=pltpu.HBM)],
        out_specs=vmem,
        scratch_shapes=[pltpu.SemaphoreType.DMA((8,))],
        compiler_params=small,
        name="share",
    )(at_word, centroids)
    other = swap_cores(mine)
    score = functools.partial(scores_call, mine, other)
    far_second = swap_sides(far_first)
    chunks = [first, second, after_first, after_second, far_first, far_second, before_first, before_second]
    swapped = (5,)
    early_ps, early_stat = score([far_first, first, second])
    calls, last = {}, early_stat
    for k in (3, 6, 5, 7, 2):
        chunks[k], _ = lax.optimization_barrier((chunks[k], last))
        calls[k] = score([chunks[k]])
        last = calls[k][1]
    ps = early_ps[1:] + [calls[2][0][0], calls[3][0][0], early_ps[0]] + [calls[k][0][0] for k in (5, 6, 7)]
    stats = [early_stat] + [calls[k][1] for k in (2, 3, 5, 6, 7)]
    order = ((0, 1), (0, 2), (1, 0), (2, 0), (0, 0), (3, 0), (4, 0), (5, 0))

    local, tops = pl.pallas_call(
        functools.partial(first_kernel, swapped, order),
        out_shape=(
            jax.ShapeDtypeStruct((16, 8, 640), jnp.float32),
            jax.ShapeDtypeStruct((2, 4096), jnp.float32),
        ),
        in_specs=[smem] + [vmem] * 7,
        compiler_params=small,
        name="first",
    )(spot, ids, *stats)
    planes = [[place(i % 4, i // 4, z, 0) for i in range(16)] for z in range(4)]
    planes += [[place(i % 4, y, i // 4, 1) for i in range(16)] for y in range(4)]
    shared = lax.all_to_all(local, BOTH, split_axis=0, concat_axis=0, tiled=True, axis_index_groups=planes)
    plane = pl.pallas_call(
        plane_kernel,
        out_shape=jax.ShapeDtypeStruct((8, 640), jnp.float32),
        in_specs=[vmem],
        out_specs=vmem,
        compiler_params=small,
        name="plane",
    )(shared)
    pack, lse = pl.pallas_call(
        functools.partial(merge_kernel, swapped),
        out_shape=(
            jax.ShapeDtypeStruct((64, 128), jnp.float32),
            jax.ShapeDtypeStruct((1, 4096), jnp.float32),
        ),
        in_specs=[smem] + [vmem] * 4,
        compiler_params=small,
        name="merge",
    )(spot, plane, *[fetch(plane, 2, offset) for offset in (3, 2, 1)])
    theirs = sums_call(1, lse, tops, ps, chunks)
    received = swap_cores(theirs)
    partner = swap_cores(pack)
    ours = sums_call(0, lse, tops, ps[:7], chunks[:7])
    new_centers, row_lse = pl.pallas_call(
        functools.partial(final_kernel, 7, 1),
        out_shape=(
            jax.ShapeDtypeStruct((share, width), jnp.float32),
            jax.ShapeDtypeStruct((1, UNIT), jnp.float32),
        ),
        in_specs=[smem] + [vmem] * 9,
        out_specs=(pl.BlockSpec(memory_space=pl.ANY), vmem),
        scratch_shapes=[pltpu.VMEM((share, width), jnp.float32), pltpu.SemaphoreType.DMA((4,))],
        compiler_params=pltpu.CompilerParams(vmem_limit_bytes=12 << 20),
        name="final",
    )(at_word, lse, tops, ours, received, mine, pack, partner, *ps[7:], *chunks[7:])
    return new_centers, row_lse.reshape(UNIT)


def solution(mesh):
    in_specs = (P(BOTH, None), P(BOTH), P("cent", None))
    out_specs = (P(("cent", "samp"), None), P(BOTH))
    return jax.shard_map(shards, mesh=mesh, in_specs=in_specs, out_specs=out_specs, check_vma=False)
```

```python
import functools
import math

import jax
import jax.numpy as jnp
from jax import lax
from jax.experimental import pallas as pl
from jax.experimental.pallas import tpu as pltpu
from jax.sharding import PartitionSpec as P

inv_temp = 2.5
prior_mass = 0.25
BOTH = ("samp", "cent")
UNIT = 64
X, Y, Z = 0, 1, 2
ORDERS = ((X, Y, Z), (X, Z, Y))


def place(x, y, z, core):
    return ((x // 2) * 4 + z) * 16 + (x % 2) * 8 + y * 2 + core


def fetch(value, stage, offset):
    pairs = []
    for x in range(4):
        for y in range(4):
            for z in range(4):
                for core in range(2):
                    at = [x, y, z]
                    axis = ORDERS[core][stage]
                    at[axis] = (at[axis] + offset) % 4
                    pairs.append((place(*at, core), place(x, y, z, core)))
    return lax.ppermute(value, BOTH, pairs)


def swap_cores(value):
    pairs = [(i, i ^ 1) for i in range(128)]
    return lax.ppermute(value, BOTH, pairs)


def swap_sides(value):
    pairs = []
    for x in range(4):
        for y in range(4):
            for z in range(4):
                for core in range(2):
                    other = (x + (1 if x % 2 == core else 3)) % 4
                    pairs.append((place(other, y, z, core), place(x, y, z, core)))
    return lax.ppermute(value, BOTH, pairs)


def scores_kernel(factor, count, mine_ref, other_ref, *refs):
    rows = refs[:count]
    ps = refs[count : 2 * count]
    stat_ref = refs[2 * count]
    tiles = [(k, part, half) for k in range(count) for part in range(2) for half in range(2)]

    def product(tile):
        k, part, half = tile
        return lax.dot_general(
            (mine_ref, other_ref)[half][...],
            rows[k][part * 256 : (part + 1) * 256, :],
            (((1,), (1,)), ((), ())),
            preferred_element_type=jnp.float32,
        )

    following = product(tiles[0])
    for i, (k, part, half) in enumerate(tiles):
        s = following * factor
        if i + 1 < len(tiles):
            following = product(tiles[i + 1])
        top = jnp.max(s, axis=0, keepdims=True)
        e = jnp.exp2(s - top)
        ps[k][half, :, part * 256 : (part + 1) * 256] = e
        lanes = slice(k * 512 + part * 256, k * 512 + (part + 1) * 256)
        stat_ref[half : half + 1, lanes] = top
        stat_ref[2 + half : 3 + half, lanes] = jnp.sum(e, axis=0, keepdims=True)


def scores_call(mine, other, rows):
    count = len(rows)
    n, width = rows[0].shape
    factor = inv_temp / math.sqrt(width) * math.log2(math.e)
    vmem = pl.BlockSpec(memory_space=pltpu.VMEM)
    *ps, stat = pl.pallas_call(
        functools.partial(scores_kernel, factor, count),
        out_shape=tuple([jax.ShapeDtypeStruct((2, 512, n), jnp.float32)] * count)
        + (jax.ShapeDtypeStruct((4, count * n), jnp.float32),),
        in_specs=[vmem] * (2 + count),
        out_specs=tuple([vmem] * (count + 1)),
        compiler_params=pltpu.CompilerParams(vmem_limit_bytes=12 << 20),
        cost_estimate=pl.CostEstimate(
            flops=4 * 1024 * n * width * count,
            bytes_accessed=count * n * 6144 + (2 << 20),
            transcendentals=1024 * n * count,
        ),
        name="scores",
    )(mine, other, *rows)
    return ps, stat


def roll_within(value, dim, step):
    inner = UNIT * 4**dim
    group = inner * 4
    size = value.shape[1]
    lane = lax.broadcasted_iota(jnp.int32, value.shape, 1) % group
    ahead = pltpu.roll(value, step * inner, 1)
    back = pltpu.roll(value, size - group + step * inner, 1)
    return jnp.where(lane >= step * inner, ahead, back)


def first_kernel(swapped, order, spot_ref, ids_ref, *refs):
    *stats, out_ref, top_ref = refs
    parts = []
    for k, (ref, piece) in enumerate(order):
        lanes = slice(piece * 512, (piece + 1) * 512)
        tops = stats[ref][0:2, lanes]
        top = jnp.max(tops, axis=0, keepdims=True)
        total = jnp.sum(stats[ref][2:4, lanes] * jnp.exp2(tops - top), axis=0, keepdims=True)
        part = top + jnp.log2(total)
        parts.append(roll_within(part, 0, spot_ref[3]) if k in swapped else part)
        top_ref[:, k * 512 : (k + 1) * 512] = tops
    value = jnp.concatenate(parts, axis=1)
    for dim in range(3):
        value = roll_within(value, dim, spot_ref[dim])
    for line in range(8):
        piece = value[:, line * 512 : (line + 1) * 512]
        out_ref[:, line, 0:512] = jnp.broadcast_to(piece, (16, 512))
    lane = lax.broadcasted_iota(jnp.int32, (1, 128), 1)
    ids = jnp.where(lane // UNIT == spot_ref[0] % 2, ids_ref[...], -1.0)
    out_ref[:, :, 512:640] = jnp.broadcast_to(ids.reshape(1, 1, 128), (16, 8, 128))


def combine(values):
    top = functools.reduce(jnp.maximum, values)
    return top + jnp.log2(sum(jnp.exp2(value - top) for value in values))


def plane_kernel(all_ref, out_ref):
    out_ref[:, 0:512] = combine([all_ref[k, :, 0:512] for k in range(16)])
    for line in range(8):
        pair = jnp.maximum(all_ref[2 * line, 0:1, 512:640], all_ref[2 * line + 1, 0:1, 512:640])
        out_ref[line : line + 1, 512:640] = pair


def merge_kernel(swapped, spot_ref, *refs):
    *planes, pack_ref, own_ref = refs
    lse = combine([plane[:, 0:512] for plane in planes])
    value = jnp.concatenate([lse[line : line + 1, :] for line in range(8)], axis=1)
    for tile in range(32):
        pack_ref[tile : tile + 1, :] = value[:, tile * 128 : (tile + 1) * 128]
    for offset, plane in zip((0, 3, 2, 1), planes):
        first = pl.multiple_of(32 + (spot_ref[2] + offset) % 4 * 8, 8)
        pack_ref[pl.ds(first, 8), :] = plane[:, 512:640]
    for dim in range(3):
        value = roll_within(value, dim, (4 - spot_ref[dim]) % 4)
    own_ref[...] = value
    for k in swapped:
        lanes = slice(k * 512, (k + 1) * 512)
        own_ref[:, lanes] = roll_within(value[:, lanes], 0, 4 - spot_ref[3])


def join_kernel(slots, *refs):
    own_ref, *parts, out_ref, sem = refs
    rows = own_ref.shape[0]
    copy = pltpu.make_async_copy(own_ref, out_ref.at[pl.ds(slots[0] * rows, rows)], sem)
    copy.start()
    for slot, part in zip(slots[1:], parts):
        out_ref[slot * rows : (slot + 1) * rows, :] = part[...]
    copy.wait()


def halves_kernel(spot_ref, *refs):
    line, across, near, back, first_ref, second_ref = refs
    parts = (line, near, across, back)
    rows = parts[0].shape[0]
    for side in range(2):

        @pl.when(spot_ref[4] == side)
        def _():
            for k, part in enumerate(parts):
                out_ref = (first_ref, second_ref)[(k // 2 + side) % 2]
                out_ref[k % 2 * rows : (k % 2 + 1) * rows, :] = part[...]


def join(slots, *parts):
    vmem = pl.BlockSpec(memory_space=pltpu.VMEM)
    shape = (sum(part.shape[0] for part in parts), parts[0].shape[1])
    return pl.pallas_call(
        functools.partial(join_kernel, slots),
        out_shape=jax.ShapeDtypeStruct(shape, parts[0].dtype),
        in_specs=[pl.BlockSpec(memory_space=pltpu.HBM)] + [vmem] * (len(parts) - 1),
        out_specs=vmem,
        scratch_shapes=[pltpu.SemaphoreType.DMA(())],
        compiler_params=pltpu.CompilerParams(vmem_limit_bytes=8 << 20),
        name="join",
    )(*parts)


def sums_kernel(half, count, lse_ref, top_ref, *refs):
    ps = refs[:count]
    rows = refs[count : 2 * count]
    out_ref = refs[2 * count]
    n, width = rows[0].shape

    def weights(k):
        lanes = slice(k * n, (k + 1) * n)
        f = jnp.exp2(top_ref[half : half + 1, lanes] - lse_ref[:, lanes])
        w = (ps[k][half] * f).astype(jnp.bfloat16)
        wide = w.astype(jnp.float32)
        return w, sum(wide[:, c : c + 128] for c in range(0, n, 128))

    w, mass = weights(0)
    for k in range(count):
        now = w
        if k + 1 < count:
            w, more = weights(k + 1)
            mass = mass + more
        add = jnp.dot(now, rows[k][...], preferred_element_type=jnp.float32)
        if k == 0:
            out_ref[:, :width] = add
        else:
            out_ref[:, :width] += add
    out_ref[:, width:] = mass


def sums_call(half, lse, tops, ps, rows):
    count = len(rows)
    width = rows[0].shape[1]
    vmem = pl.BlockSpec(memory_space=pltpu.VMEM)
    return pl.pallas_call(
        functools.partial(sums_kernel, half, count),
        out_shape=jax.ShapeDtypeStruct((512, width + 128), jnp.float32),
        in_specs=[vmem] * (2 + 2 * count),
        compiler_params=pltpu.CompilerParams(vmem_limit_bytes=12 << 20),
        cost_estimate=pl.CostEstimate(
            flops=2 * 512 * 512 * count * width, bytes_accessed=18 << 20, transcendentals=8192
        ),
        name="sums",
    )(lse, tops, *ps, *rows)


def final_kernel(skip, count, at_ref, lse_ref, top_ref, ours_ref, theirs_ref, mine_ref, pack_ref, other_ref, *refs):
    ps = refs[:count]
    rows = refs[count : 2 * count]
    out_ref, row_ref, buf, sems = refs[2 * count :]
    n, width = rows[0].shape
    mass = ours_ref[:, width:] + theirs_ref[:, width:]
    ws = []
    for k in range(count):
        lanes = slice((skip + k) * n, (skip + k + 1) * n)
        f = jnp.exp2(top_ref[0:1, lanes] - lse_ref[:, lanes])
        w = (ps[k][0] * f).astype(jnp.bfloat16)
        wide = w.astype(jnp.float32)
        mass = mass + sum(wide[:, c : c + 128] for c in range(0, n, 128))
        ws.append(w)
    inverse = 1.0 / (jnp.sum(mass, axis=1, keepdims=True) + prior_mass)
    base = (at_ref[0] * 16 + at_ref[1]) * UNIT
    logical = (lax.broadcasted_iota(jnp.int32, (UNIT, 128), 0) + base).astype(jnp.float32)
    routed = []
    copies = []
    for block in range(4):
        found = jnp.zeros((UNIT, 128), jnp.float32)
        for line in range(block * 8, block * 8 + 8):
            for ref in (pack_ref, other_ref):
                hit = ref[32 + line : 33 + line, :] == logical
                found = found + jnp.where(hit, ref[line : line + 1, :], 0.0)
        routed.append(found)
        columns = slice(block * width // 4, (block + 1) * width // 4)
        total = ours_ref[:, columns] + theirs_ref[:, columns]
        total = total + prior_mass * mine_ref[:, columns].astype(jnp.float32)
        for k in range(count):
            total = total + jnp.dot(ws[k], rows[k][:, columns], preferred_element_type=jnp.float32)
        buf[:, columns] = total * inverse
        copy = pltpu.make_async_copy(buf.at[:, columns], out_ref.at[:, columns], sems.at[block])
        copy.start()
        copies.append(copy)
    found = (routed[0] + routed[1]) + (routed[2] + routed[3])
    row_ref[...] = jnp.sum(found.T, axis=0, keepdims=True) * math.log(2.0)
    for copy in copies:
        copy.wait()


def share_kernel(at_ref, cents_ref, out_ref, sem):
    size = out_ref.shape[0]
    first = pl.multiple_of(at_ref[0] * size, size)
    part = size // 8
    copies = [
        pltpu.make_async_copy(
            cents_ref.at[pl.ds(first + k * part, part)], out_ref.at[pl.ds(k * part, part)], sem.at[k]
        )
        for k in range(8)
    ]
    for copy in copies:
        copy.start()
    for copy in copies:
        copy.wait()


def shards(embeddings, destination, centroids):
    samp, cent = lax.axis_index("samp"), lax.axis_index("cent")
    core = lax.bitwise_and(cent, 1)
    x = lax.shift_right_logical(samp, 2) * 2 + lax.shift_right_logical(cent, 3)
    y, z = lax.bitwise_and(lax.shift_right_logical(cent, 1), 3), lax.bitwise_and(samp, 3)
    side = lax.bitwise_and(x, 1)
    second = lax.bitwise_and(jnp.where(core == 0, y, z) + 2 * side, 3)
    step = jnp.where(side == core, 1, 3)
    spot = jnp.stack([x, second, jnp.where(core == 0, z, y), step, side]).astype(jnp.int32)
    share = centroids.shape[0] // 8
    width = embeddings.shape[1]
    smem = pl.BlockSpec(memory_space=pltpu.SMEM)
    vmem = pl.BlockSpec(memory_space=pltpu.VMEM)
    small = pltpu.CompilerParams(vmem_limit_bytes=8 << 20)
    ids = jnp.tile(destination.astype(jnp.float32), 2).reshape(1, 128)
    at_word = jnp.stack([samp, cent]).astype(jnp.int32)
    line = join((0, 2, 1, 3), embeddings, *[fetch(embeddings, 0, step) for step in (2, 1, 3)])
    spot, ids, at_word, line = lax.optimization_barrier((spot, ids, at_word, line))
    back, across, near = [fetch(line, 1, step) for step in (3, 2, 1)]
    first, second = pl.pallas_call(
        halves_kernel,
        out_shape=[jax.ShapeDtypeStruct((512, width), embeddings.dtype)] * 2,
        in_specs=[smem] + [vmem] * 4,
        out_specs=[vmem] * 2,
        compiler_params=small,
        name="halves",
    )(spot, line, across, near, back)
    far_first = fetch(first, 2, 2)
    after_first, before_first = fetch(first, 2, 1), fetch(first, 2, 3)
    after_second, before_second = fetch(second, 2, 1), fetch(second, 2, 3)
    at_word, first, second = lax.optimization_barrier((at_word, first, second))
    mine = pl.pallas_call(
        share_kernel,
        out_shape=jax.ShapeDtypeStruct((share, width), centroids.dtype),
        in_specs=[smem, pl.BlockSpec(memory_space=pltpu.HBM)],
        out_specs=vmem,
        scratch_shapes=[pltpu.SemaphoreType.DMA((8,))],
        compiler_params=small,
        name="share",
    )(at_word, centroids)
    other = swap_cores(mine)
    score = functools.partial(scores_call, mine, other)
    far_second = swap_sides(far_first)
    chunks = [first, second, after_first, after_second, far_first, far_second, before_first, before_second]
    swapped = (5,)
    early_ps, early_stat = score([far_first, first, second])
    calls, last = {}, early_stat
    for k in (3, 6, 5, 7, 2):
        chunks[k], _ = lax.optimization_barrier((chunks[k], last))
        calls[k] = score([chunks[k]])
        last = calls[k][1]
    ps = early_ps[1:] + [calls[2][0][0], calls[3][0][0], early_ps[0]] + [calls[k][0][0] for k in (5, 6, 7)]
    stats = [early_stat] + [calls[k][1] for k in (2, 3, 5, 6, 7)]
    order = ((0, 1), (0, 2), (1, 0), (2, 0), (0, 0), (3, 0), (4, 0), (5, 0))

    local, tops = pl.pallas_call(
        functools.partial(first_kernel, swapped, order),
        out_shape=(
            jax.ShapeDtypeStruct((16, 8, 640), jnp.float32),
            jax.ShapeDtypeStruct((2, 4096), jnp.float32),
        ),
        in_specs=[smem] + [vmem] * 7,
        compiler_params=small,
        name="first",
    )(spot, ids, *stats)
    planes = [[place(i % 4, i // 4, z, 0) for i in range(16)] for z in range(4)]
    planes += [[place(i % 4, y, i // 4, 1) for i in range(16)] for y in range(4)]
    shared = lax.all_to_all(local, BOTH, split_axis=0, concat_axis=0, tiled=True, axis_index_groups=planes)
    plane = pl.pallas_call(
        plane_kernel,
        out_shape=jax.ShapeDtypeStruct((8, 640), jnp.float32),
        in_specs=[vmem],
        out_specs=vmem,
        compiler_params=small,
        name="plane",
    )(shared)
    pack, lse = pl.pallas_call(
        functools.partial(merge_kernel, swapped),
        out_shape=(
            jax.ShapeDtypeStruct((64, 128), jnp.float32),
            jax.ShapeDtypeStruct((1, 4096), jnp.float32),
        ),
        in_specs=[smem] + [vmem] * 4,
        compiler_params=small,
        name="merge",
    )(spot, plane, *[fetch(plane, 2, offset) for offset in (3, 2, 1)])
    theirs = sums_call(1, lse, tops, ps, chunks)
    received = swap_cores(theirs)
    partner = swap_cores(pack)
    ours = sums_call(0, lse, tops, ps[:7], chunks[:7])
    new_centers, row_lse = pl.pallas_call(
        functools.partial(final_kernel, 7, 1),
        out_shape=(
            jax.ShapeDtypeStruct((share, width), jnp.float32),
            jax.ShapeDtypeStruct((1, UNIT), jnp.float32),
        ),
        in_specs=[smem] + [vmem] * 9,
        out_specs=(pl.BlockSpec(memory_space=pl.ANY), vmem),
        scratch_shapes=[pltpu.VMEM((share, width), jnp.float32), pltpu.SemaphoreType.DMA((4,))],
        compiler_params=pltpu.CompilerParams(vmem_limit_bytes=12 << 20),
        name="final",
    )(at_word, lse, tops, ours, received, mine, pack, partner, *ps[7:], *chunks[7:])
    return new_centers, row_lse.reshape(UNIT)


def solution(mesh):
    in_specs = (P(BOTH, None), P(BOTH), P("cent", None))
    out_specs = (P(("cent", "samp"), None), P(BOTH))
    return jax.shard_map(shards, mesh=mesh, in_specs=in_specs, out_specs=out_specs, check_vma=False)
```
